32 devices in a mesh: ctx: 16 (over z, x, core), head: 2 (over y).
Axes of the slice: x: 2, y: 2, z: 4, core: 2. Of those that a mesh axis runs over, the one named last changes fastest.
Arguments:
- queries: bfloat16 [6144, 2048], P('ctx', 'head')
- keys: bfloat16 [6144, 512], P('ctx', 'head')
- values: bfloat16 [6144, 512], P('ctx', 'head'), may hold values from -6 to 6
- block_start: int32 [48], P('ctx'), may hold values from 0 to 6016, as said below
- out_weight: bfloat16 [2048, 4096], P('head'), may hold values from -0.125 to 0.125
Outputs:
- attended: bfloat16 [6144, 4096], P('ctx', 'head')
The draws below stay inside these ranges and needn't reach their ends.
Inputs may be any that keep to these rules, and one draw needn't show every extreme that they name: block_start never falls; every document is a whole number of blocks and at most 3072 tokens long, and one document is exactly 3072 tokens long; the first and the last block each begin a document.
All inputs are finite; a program needn't handle non-finite values.
Results may differ from the reference program's by a relative error of at most 0.012.
Values may be sent and summed in bfloat16 or wider, within the bound.
No kernel may reach another device: no remote copies, remote signals or barrier semaphores. Data moves between devices by JAX's collectives and lax.ppermute only.
A program may use at most 64 MiB of HBM per device.

```python
import jax
import jax.numpy as jnp
from jax import lax

D = 4096
QUERY_HEADS = 16
KEY_VALUE_HEADS = 4
HEAD_SIZE = 128
BLOCK = 128
SPAN = 8
SHARD_TOKENS = 384
CONTEXT_TOKENS = 6144
MAXDOC = 3072
N_CTX = 16
N_HEAD = 2


def shared_pair(key):
    key_sample = jnp.clip(jax.random.normal(jax.random.fold_in(key, 12), (CONTEXT_TOKENS, KEY_VALUE_HEADS, HEAD_SIZE), jnp.float32), -4.0, 4.0)
    query_sample = jnp.clip(jax.random.normal(jax.random.fold_in(key, 11), (CONTEXT_TOKENS, QUERY_HEADS, HEAD_SIZE), jnp.float32), -4.0, 4.0)
    return (query_sample.reshape(CONTEXT_TOKENS, QUERY_HEADS * HEAD_SIZE), key_sample.reshape(CONTEXT_TOKENS, KEY_VALUE_HEADS * HEAD_SIZE))


def draw_queries(key, part):
    return shared_pair(key)[0].astype(jnp.bfloat16)


def draw_keys(key, part):
    return shared_pair(key)[1].astype(jnp.bfloat16)


def draw_block_start(key, part):
    blocks = CONTEXT_TOKENS // BLOCK
    longest = MAXDOC // BLOCK
    lens = jax.random.randint(jax.random.fold_in(key, 21), (blocks,), 1, longest + 1)
    lens = jnp.where(jnp.arange(blocks) == 0, longest, lens).astype(jnp.int32)
    ends = jnp.cumsum(lens)
    begins = ends - lens
    slots = jnp.where(begins < blocks, begins, blocks)
    marks = jnp.zeros((blocks,), jnp.int32).at[slots].set(1, mode='drop')
    marks = marks.at[blocks - 1].set(1)
    firsts = lax.cummax(jnp.arange(blocks, dtype=jnp.int32) * marks, axis=0)
    return (firsts * BLOCK).astype(jnp.int32)


def levels(key, shape, shards, low, high):
    def one(dim, parts):
        heights = jax.random.uniform(jax.random.fold_in(jax.random.fold_in(key, 6), dim), (parts,), jnp.float32, low / len(shards), high / len(shards))
        return jnp.repeat(jnp.exp(heights), shape[dim] // parts).reshape((-1,) + (1,) * (len(shape) - dim - 1))

    factor_of = one(*shards[0])
    for cut in shards[1:]:
        factor_of = factor_of * one(*cut)
    return factor_of


def bell_draw(rng, shape, width, most, cuts=(), held_as=jnp.bfloat16):
    factor_of = levels(rng, shape, cuts, -0.22, 0.18) if cuts else 1.0
    entries = jax.random.normal(rng, shape, jnp.float32) * width * factor_of
    return jnp.minimum(jnp.maximum(entries, -most), most).astype(held_as)


def setup_inputs(seed: int = 0) -> dict:
    streams_of = jax.random.split(jax.random.key(seed), 6)
    return {
        "queries": draw_queries(jax.random.fold_in(streams_of[5], 71), 0),
        "keys": draw_keys(jax.random.fold_in(streams_of[5], 71), 0),
        "values": bell_draw(streams_of[2], (CONTEXT_TOKENS, KEY_VALUE_HEADS * HEAD_SIZE), 1.0, 6.0, ((0, 16), (1, 2))),
        "block_start": draw_block_start(jax.random.fold_in(streams_of[5], 71), 0),
        "out_weight": bell_draw(streams_of[4], (QUERY_HEADS * HEAD_SIZE, D), (QUERY_HEADS * HEAD_SIZE) ** -0.5, 0.125, ((0, 2),)),
    }


def reference(queries, keys, values, block_start, out_weight):
    query_group = QUERY_HEADS // KEY_VALUE_HEADS
    padding = SPAN * SHARD_TOKENS
    window_width = padding + SHARD_TOKENS
    scale = HEAD_SIZE ** -0.5
    padded_keys = jnp.concatenate([jnp.zeros((padding, KEY_VALUE_HEADS * HEAD_SIZE), jnp.bfloat16), keys], axis=0)
    padded_values = jnp.concatenate([jnp.zeros((padding, KEY_VALUE_HEADS * HEAD_SIZE), jnp.bfloat16), values], axis=0)
    starts = jnp.repeat(block_start, BLOCK)

    def shard(index):
        first_token = index * SHARD_TOKENS
        query_rows = lax.dynamic_slice_in_dim(queries, first_token, SHARD_TOKENS, 0).astype(jnp.float32).reshape(SHARD_TOKENS, KEY_VALUE_HEADS, query_group, HEAD_SIZE)
        key_window = lax.dynamic_slice_in_dim(padded_keys, first_token, window_width, 0).astype(jnp.float32).reshape(window_width, KEY_VALUE_HEADS, HEAD_SIZE)
        value_window = lax.dynamic_slice_in_dim(padded_values, first_token, window_width, 0).astype(jnp.float32).reshape(window_width, KEY_VALUE_HEADS, HEAD_SIZE)
        scores = jnp.einsum("pgcd,jgd->gcpj", query_rows, key_window) * scale
        q_pos = first_token + jnp.arange(SHARD_TOKENS, dtype=jnp.int32)
        k_pos = first_token - padding + jnp.arange(window_width, dtype=jnp.int32)
        st = lax.dynamic_slice_in_dim(starts, first_token, SHARD_TOKENS, 0)
        valid = (k_pos[None, :] >= st[:, None]) & (k_pos[None, :] <= q_pos[:, None])
        masked = jnp.where(valid, scores, -1e30)
        top = jnp.max(masked, axis=-1, keepdims=True)
        expw = jnp.where(valid, jnp.exp(masked - top), 0.0)
        total = jnp.sum(expw, axis=-1)
        weights = lax.optimization_barrier(expw.astype(jnp.bfloat16)).astype(jnp.float32)
        numer = jnp.einsum("gcpj,jgd->gcpd", weights, value_window)
        out = (numer / total[..., None]).astype(jnp.bfloat16)
        return jnp.transpose(out, (2, 0, 1, 3)).reshape(SHARD_TOKENS, QUERY_HEADS * HEAD_SIZE)

    heads_out = lax.map(shard, jnp.arange(N_CTX, dtype=jnp.int32)).reshape(CONTEXT_TOKENS, QUERY_HEADS * HEAD_SIZE)
    half = QUERY_HEADS * HEAD_SIZE // N_HEAD
    summed = jnp.zeros((CONTEXT_TOKENS, D), jnp.float32)
    for part in range(N_HEAD):
        partial_value = jnp.dot(heads_out[:, part * half:(part + 1) * half], out_weight[part * half:(part + 1) * half], preferred_element_type=jnp.float32)
        summed = summed + lax.optimization_barrier(partial_value.astype(jnp.bfloat16)).astype(jnp.float32)
    return summed.astype(jnp.bfloat16)
```

```python
import functools

import jax
import jax.numpy as jnp
from jax import lax
from jax.experimental import pallas as pl
from jax.experimental.pallas import tpu as pltpu
from jax.sharding import PartitionSpec as P

HEAD_SIZE = 128
BLOCK = 128
LOG2E = 1.4426950408889634
MASKED = -1e30


def shift(x, distance):
    n = lax.axis_size("ctx")
    return lax.ppermute(x, "ctx", [(i, i + distance) for i in range(n - distance)])


def swap(x, mask):
    return lax.ppermute(x, "ctx", [(i, i ^ mask) for i in range(lax.axis_size("ctx"))])


def split_scaled(q, factor):
    exact = q.astype(jnp.float32) * factor
    high = exact.astype(jnp.bfloat16)
    low = (exact - high.astype(jnp.float32)).astype(jnp.bfloat16)
    return jnp.concatenate([high, low], axis=1)


def attention_kernel(first, last, distances, n_head, starts_ref, recv_starts_ref, *refs):
    refs = list(refs)
    me = lax.axis_index("ctx")
    pair, core, col = me // 2, me % 2, (me // 2) % 2
    if first:
        queries_ref, q_recv_ref, own_ref = refs[:3]
        refs = refs[3:]
    else:
        q2_ref, top_in, acc_in = refs[:3]
        refs = refs[3:]
    pieces = refs[: len(distances)]
    refs = refs[len(distances) :]
    if first:
        q2_ref, top_ref, acc_ref = refs
    elif last:
        out_own, out_other, top_ref, acc_ref = refs
    else:
        top_ref, acc_ref = refs
    tok = starts_ref.shape[0] * BLOCK
    half = tok // BLOCK
    blocks = 2 * half
    rows = n_head * BLOCK

    def start_of(b):
        mine = b // half == core
        return jnp.where(mine, starts_ref[b % half], recv_starts_ref[b % half])

    def rows_of(ref, j, lane0):
        t = slice(j * BLOCK, (j + 1) * BLOCK)
        return jnp.concatenate(
            [ref[t, pl.ds(lane0 + h * HEAD_SIZE, HEAD_SIZE)] for h in range(n_head)], axis=0
        )

    def key_pair(piece_ref, width):
        k = piece_ref[:width, :HEAD_SIZE]
        return jnp.concatenate([k, k], axis=1)

    def value_ones(piece_ref, width):
        v = piece_ref[:width, HEAD_SIZE:]
        return jnp.concatenate([v, jnp.ones_like(v)], axis=1)

    def dot_t(a, b):
        return lax.dot_general(a, b, (((1,), (1,)), ((), ())), preferred_element_type=jnp.float32)

    if first:
        factor = HEAD_SIZE**-0.5 * LOG2E
        for j in range(half):
            mine = rows_of(queries_ref, j, pl.multiple_of(core * rows, rows))
            q2_ref[core * half + j] = split_scaled(mine, factor)
            other = rows_of(q_recv_ref, j, 0)
            q2_ref[(1 - core) * half + j] = split_scaled(other, factor)
        for b in range(blocks):
            width = (b + 1) * BLOCK
            s = dot_t(q2_ref[b], key_pair(own_ref, width))
            since = start_of(b) - pair * 2 * tok
            t_id = lax.broadcasted_iota(jnp.int32, (rows, BLOCK), 0) % BLOCK
            c_id = lax.broadcasted_iota(jnp.int32, (rows, BLOCK), 1)
            diag = jnp.where(c_id <= t_id, s[:, b * BLOCK :], MASKED)
            if b:
                k_id = lax.broadcasted_iota(jnp.int32, (rows, b * BLOCK), 1)
                s = jnp.concatenate([jnp.where(k_id >= since, s[:, : b * BLOCK], MASKED), diag], 1)
            else:
                s = diag
            top = jnp.max(s, axis=1, keepdims=True)
            p = jnp.exp2(s - top).astype(jnp.bfloat16)
            top_ref[b] = jnp.broadcast_to(top, (rows, HEAD_SIZE))
            acc_ref[b] = jnp.dot(p, value_ones(own_ref, width), preferred_element_type=jnp.float32)
    else:
        top_ref[...] = top_in[...]
        acc_ref[...] = acc_in[...]

    def update(b, piece_ref, since):
        s = dot_t(q2_ref[b], key_pair(piece_ref, 2 * tok))
        if since is not None:
            k_id = lax.broadcasted_iota(jnp.int32, s.shape, 1)
            s = jnp.where(k_id >= since, s, MASKED)
        old = top_ref[b][:, :1]
        top = jnp.maximum(old, jnp.max(s, axis=1, keepdims=True))
        p = jnp.exp2(s - top).astype(jnp.bfloat16)
        top_ref[b] = jnp.broadcast_to(top, (rows, HEAD_SIZE))
        acc_ref[b] = acc_ref[b] * jnp.exp2(old - top) + jnp.dot(
            p, value_ones(piece_ref, 2 * tok), preferred_element_type=jnp.float32
        )

    for (if_left, if_right), piece_ref in zip(distances, pieces, strict=True):
        base = (pair - jnp.where(col == 0, if_left, if_right)) * 2 * tok
        whole = start_of(blocks - 1) <= base

        @pl.when(whole)
        def _(piece_ref=piece_ref):
            @pl.loop(0, blocks)
            def _(b):
                update(b, piece_ref, None)

        @pl.when(jnp.logical_not(whole))
        def _(piece_ref=piece_ref, base=base):
            @pl.loop(0, blocks)
            def _(b):
                since = start_of(b) - base

                @pl.when(since < 2 * tok)
                def _():
                    update(b, piece_ref, since)

    if last:
        for j in range(half):
            for out, shard in ((out_own, core), (out_other, 1 - core)):
                acc = acc_ref[shard * half + j]
                o = (acc[:, :HEAD_SIZE] / acc[:, HEAD_SIZE:]).astype(jnp.bfloat16)
                for h in range(n_head):
                    out[j * BLOCK : (j + 1) * BLOCK, h * HEAD_SIZE : (h + 1) * HEAD_SIZE] = o[
                        h * BLOCK : (h + 1) * BLOCK
                    ]


def attention_call(first, last, distances, n_head, starts, recv_starts, operands):
    tok = starts.shape[0] * BLOCK
    blocks, rows = 2 * starts.shape[0], n_head * BLOCK
    state = [
        jax.ShapeDtypeStruct((blocks, rows, HEAD_SIZE), jnp.float32),
        jax.ShapeDtypeStruct((blocks, rows, 2 * HEAD_SIZE), jnp.float32),
    ]
    scratch = []
    if first:
        outs = [jax.ShapeDtypeStruct((blocks, rows, 2 * HEAD_SIZE), jnp.bfloat16)] + state
    elif last:
        outs = [jax.ShapeDtypeStruct((tok, rows), jnp.bfloat16)] * 2
        scratch = [pltpu.VMEM(s.shape, s.dtype) for s in state]
    else:
        outs = state
    n_pieces = len(distances) + 0.5 * first
    vmem, smem = pl.BlockSpec(memory_space=pltpu.VMEM), pl.BlockSpec(memory_space=pltpu.SMEM)
    return pl.pallas_call(
        functools.partial(attention_kernel, first, last, distances, n_head),
        out_shape=outs,
        in_specs=[smem, smem] + [vmem] * len(operands),
        out_specs=[vmem] * len(outs),
        scratch_shapes=scratch,
        compiler_params=pltpu.CompilerParams(vmem_limit_bytes=40 * 2**20),
        cost_estimate=pl.CostEstimate(
            flops=int(n_pieces * blocks * rows * 2 * tok * HEAD_SIZE * 8),
            bytes_accessed=8 * 2**20,
            transcendentals=int(n_pieces * blocks * rows * 2 * tok),
        ),
    )(starts, recv_starts, *operands)


def per_device(queries, keys, values, block_start, out_weight):
    tok = queries.shape[0]
    group = queries.shape[1] // 2
    n_head = group // HEAD_SIZE
    me = lax.axis_index("ctx")
    core, col = me % 2, (me // 2) % 2
    head = lax.axis_index("head")

    def part(x, index, size):
        return lax.dynamic_slice_in_dim(x, index * size, size, 1)

    mine = jnp.concatenate([part(keys, core, HEAD_SIZE), part(values, core, HEAD_SIZE)], 1)
    theirs = jnp.concatenate([part(keys, 1 - core, HEAD_SIZE), part(values, 1 - core, HEAD_SIZE)], 1)
    recv = swap(theirs, 1)
    own = jnp.where(core == 0, jnp.concatenate([mine, recv]), jnp.concatenate([recv, mine]))
    one_behind = shift(own, 4)
    q_recv = swap(part(queries, 1 - core, group), 1)
    recv_starts = swap(block_start, 1)
    two_behind = shift(one_behind, 4)
    across = swap(one_behind, 2)
    q2, top, acc = attention_call(
        True, False, ((2, 2),), n_head, block_start, recv_starts, (queries, q_recv, own, one_behind)
    )
    third = swap(jnp.where(col == 1, two_behind, own), 2)
    top, acc = attention_call(
        False, False, ((1, 3), (4, 4)), n_head, block_start, recv_starts,
        (q2, top, acc, across, two_behind),
    )
    o_own, o_other = attention_call(
        False, True, ((3, 1),), n_head, block_start, recv_starts, (q2, top, acc, third)
    )
    o_recv = swap(o_other, 1)
    heads_out = jnp.where(
        core == 0, jnp.concatenate([o_own, o_recv], 1), jnp.concatenate([o_recv, o_own], 1)
    )
    cols = out_weight.shape[1] // 2
    away = jnp.dot(heads_out, part(out_weight, 1 - head, cols), preferred_element_type=jnp.float32)
    away = lax.ppermute(away.astype(jnp.bfloat16), "head", [(0, 1), (1, 0)])
    here = jnp.dot(heads_out, part(out_weight, head, cols), preferred_element_type=jnp.float32)
    here = here.astype(jnp.bfloat16).astype(jnp.float32)
    return (here + away.astype(jnp.float32)).astype(jnp.bfloat16)


def solution(mesh):
    in_specs = (P("ctx", "head"), P("ctx", "head"), P("ctx", "head"), P("ctx"), P("head", None))
    out_specs = P("ctx", "head")
    return jax.shard_map(
        per_device, mesh=mesh, in_specs=in_specs, out_specs=out_specs, check_vma=False
    )
```

```python
import functools

import jax
import jax.numpy as jnp
from jax import lax
from jax.experimental import pallas as pl
from jax.experimental.pallas import tpu as pltpu
from jax.sharding import PartitionSpec as P

HEAD_SIZE = 128
BLOCK = 128
LOG2E = 1.4426950408889634
MASKED = -1e30
TILE = 256


def shift(x, distance):
    n = lax.axis_size("ctx")
    return lax.ppermute(x, "ctx", [(i, i + distance) for i in range(n - distance)])


def swap(x, mask):
    return lax.ppermute(x, "ctx", [(i, i ^ mask) for i in range(lax.axis_size("ctx"))])


def attention_kernel(first, last, distances, n_head, starts_ref, recv_starts_ref, *refs):
    refs = list(refs)
    me = lax.axis_index("ctx")
    pair, core, col = me // 2, me % 2, (me // 2) % 2
    if first:
        queries_ref, q_recv_ref, own_ref = refs[:3]
        refs = refs[3:]
    else:
        q_ref, top_in, acc_in = refs[:3]
        refs = refs[3:]
    pieces = refs[: len(distances)]
    refs = refs[len(distances) :]
    if first:
        q_ref, top_ref, acc_ref = refs
    elif last:
        out_own, out_other, top_ref, acc_ref = refs
    else:
        top_ref, acc_ref = refs
    tok = starts_ref.shape[0] * BLOCK
    half = tok // BLOCK
    blocks = 2 * half
    rows = n_head * BLOCK

    def start_of(b):
        mine = b // half == core
        return jnp.where(mine, starts_ref[b % half], recv_starts_ref[b % half])

    def rows_of(ref, j, lane0):
        t = slice(j * BLOCK, (j + 1) * BLOCK)
        return jnp.concatenate(
            [ref[t, pl.ds(lane0 + h * HEAD_SIZE, HEAD_SIZE)] for h in range(n_head)], axis=0
        )

    def value_ones(piece_ref, width):
        v = piece_ref[:width, HEAD_SIZE:]
        return jnp.concatenate([v, jnp.ones_like(v)], axis=1)

    def dot_t(a, b):
        return lax.dot_general(a, b, (((1,), (1,)), ((), ())), preferred_element_type=jnp.float32)

    factor = HEAD_SIZE**-0.5 * LOG2E
    tiles = [(b, slice(r, r + TILE)) for b in range(blocks) for r in range(0, rows, TILE)]

    def keep(s, since):
        k_id = lax.broadcasted_iota(jnp.int32, (1, s.shape[1]), 1)
        return jnp.where(k_id >= since, s, MASKED)

    if first:
        for j in range(half):
            mine = rows_of(queries_ref, j, pl.multiple_of(core * rows, rows))
            q_ref[core * half + j] = mine
            q_ref[(1 - core) * half + j] = rows_of(q_recv_ref, j, 0)
        t_id = lax.broadcasted_iota(jnp.int32, (TILE, BLOCK), 0) % BLOCK
        causal = lax.broadcasted_iota(jnp.int32, (TILE, BLOCK), 1) <= t_id
        for b, r in tiles:
            width = (b + 1) * BLOCK
            s = dot_t(q_ref[b, r], own_ref[:width, :HEAD_SIZE])
            since = start_of(b) - pair * 2 * tok
            diag = jnp.where(causal, s[:, b * BLOCK :], MASKED)
            s = jnp.concatenate([keep(s[:, : b * BLOCK], since), diag], 1) if b else diag
            top = jnp.max(s, axis=1, keepdims=True)
            p = jnp.exp2(s * factor - top * factor).astype(jnp.bfloat16)
            top_ref[b, r] = jnp.broadcast_to(top, (TILE, HEAD_SIZE))
            acc_ref[b, r] = jnp.dot(p, value_ones(own_ref, width), preferred_element_type=jnp.float32)
    else:
        top_ref[...] = top_in[...]
        acc_ref[...] = acc_in[...]

    def update(piece_ref, base):
        for b, r in tiles:
            s = dot_t(q_ref[b, r], piece_ref[:, :HEAD_SIZE])
            if base is not None:
                s = keep(s, start_of(b) - base)
            old = top_ref[b, r][:, :1]
            top = jnp.maximum(old, jnp.max(s, axis=1, keepdims=True))
            p = jnp.exp2(s * factor - top * factor).astype(jnp.bfloat16)
            top_ref[b, r] = jnp.broadcast_to(top, (TILE, HEAD_SIZE))
            acc_ref[b, r] = acc_ref[b, r] * jnp.exp2((old - top) * factor) + jnp.dot(
                p, value_ones(piece_ref, 2 * tok), preferred_element_type=jnp.float32
            )

    for (if_left, if_right), piece_ref in zip(distances, pieces, strict=True):
        base = (pair - jnp.where(col == 0, if_left, if_right)) * 2 * tok
        whole = start_of(blocks - 1) <= base
        some = start_of(0) < base + 2 * tok

        @pl.when(whole)
        def _(piece_ref=piece_ref):
            update(piece_ref, None)

        @pl.when(jnp.logical_and(some, jnp.logical_not(whole)))
        def _(piece_ref=piece_ref, base=base):
            update(piece_ref, base)

    if last:
        for j in range(half):
            for out, shard in ((out_own, core), (out_other, 1 - core)):
                acc = acc_ref[shard * half + j]
                o = (acc[:, :HEAD_SIZE] / acc[:, HEAD_SIZE:]).astype(jnp.bfloat16)
                for h in range(n_head):
                    out[j * BLOCK : (j + 1) * BLOCK, h * HEAD_SIZE : (h + 1) * HEAD_SIZE] = o[
                        h * BLOCK : (h + 1) * BLOCK
                    ]


def attention_call(first, last, distances, n_head, starts, recv_starts, operands):
    tok = starts.shape[0] * BLOCK
    blocks, rows = 2 * starts.shape[0], n_head * BLOCK
    state = [
        jax.ShapeDtypeStruct((blocks, rows, HEAD_SIZE), jnp.float32),
        jax.ShapeDtypeStruct((blocks, rows, 2 * HEAD_SIZE), jnp.float32),
    ]
    scratch = []
    if first:
        outs = [jax.ShapeDtypeStruct((blocks, rows, HEAD_SIZE), jnp.bfloat16)] + state
    elif last:
        outs = [jax.ShapeDtypeStruct((tok, rows), jnp.bfloat16)] * 2
        scratch = [pltpu.VMEM(s.shape, s.dtype) for s in state]
    else:
        outs = state
    n_pieces = len(distances) + 0.5 * first
    vmem, smem = pl.BlockSpec(memory_space=pltpu.VMEM), pl.BlockSpec(memory_space=pltpu.SMEM)
    return pl.pallas_call(
        functools.partial(attention_kernel, first, last, distances, n_head),
        out_shape=outs,
        in_specs=[smem, smem] + [vmem] * len(operands),
        out_specs=[vmem] * len(outs),
        scratch_shapes=scratch,
        compiler_params=pltpu.CompilerParams(vmem_limit_bytes=40 * 2**20),
        cost_estimate=pl.CostEstimate(
            flops=int(n_pieces * blocks * rows * 2 * tok * HEAD_SIZE * 8),
            bytes_accessed=8 * 2**20,
            transcendentals=int(n_pieces * blocks * rows * 2 * tok),
        ),
    )(starts, recv_starts, *operands)


def per_device(queries, keys, values, block_start, out_weight):
    tok = queries.shape[0]
    group = queries.shape[1] // 2
    n_head = group // HEAD_SIZE
    me = lax.axis_index("ctx")
    core, col = me % 2, (me // 2) % 2
    head = lax.axis_index("head")

    def part(x, index, size):
        return lax.dynamic_slice_in_dim(x, index * size, size, 1)

    mine = jnp.concatenate([part(keys, core, HEAD_SIZE), part(values, core, HEAD_SIZE)], 1)
    theirs = jnp.concatenate([part(keys, 1 - core, HEAD_SIZE), part(values, 1 - core, HEAD_SIZE)], 1)
    recv = swap(theirs, 1)
    own = jnp.where(core == 0, jnp.concatenate([mine, recv]), jnp.concatenate([recv, mine]))
    one_behind = shift(own, 4)
    q_recv = swap(part(queries, 1 - core, group), 1)
    recv_starts = swap(block_start, 1)
    two_behind = shift(one_behind, 4)
    across = swap(one_behind, 2)
    q, top, acc = attention_call(
        True, False, ((2, 2),), n_head, block_start, recv_starts, (queries, q_recv, own, one_behind)
    )
    third = swap(jnp.where(col == 1, two_behind, own), 2)
    top, acc = attention_call(
        False, False, ((1, 3), (4, 4)), n_head, block_start, recv_starts,
        (q, top, acc, across, two_behind),
    )
    o_own, o_other = attention_call(
        False, True, ((3, 1),), n_head, block_start, recv_starts, (q, top, acc, third)
    )
    o_recv = swap(o_other, 1)
    heads_out = jnp.where(
        core == 0, jnp.concatenate([o_own, o_recv], 1), jnp.concatenate([o_recv, o_own], 1)
    )
    cols = out_weight.shape[1] // 2
    away = jnp.dot(heads_out, part(out_weight, 1 - head, cols), preferred_element_type=jnp.float32)
    away = lax.ppermute(away.astype(jnp.bfloat16), "head", [(0, 1), (1, 0)])
    here = jnp.dot(heads_out, part(out_weight, head, cols), preferred_element_type=jnp.float32)
    here = here.astype(jnp.bfloat16).astype(jnp.float32)
    return (here + away.astype(jnp.float32)).astype(jnp.bfloat16)


def solution(mesh):
    in_specs = (P("ctx", "head"), P("ctx", "head"), P("ctx", "head"), P("ctx"), P("head", None))
    out_specs = P("ctx", "head")
    return jax.shard_map(
        per_device, mesh=mesh, in_specs=in_specs, out_specs=out_specs, check_vma=False
    )
```

```python
import functools

import jax
import jax.numpy as jnp
from jax import lax
from jax.experimental import pallas as pl
from jax.experimental.pallas import tpu as pltpu
from jax.sharding import PartitionSpec as P

HEAD_SIZE = 128
BLOCK = 128
LOG2E = 1.4426950408889634
MASKED = -1e30
TILE = 256


def shift(x, distance):
    n = lax.axis_size("ctx")
    return lax.ppermute(x, "ctx", [(i, i + distance) for i in range(n - distance)])


def swap(x, mask):
    return lax.ppermute(x, "ctx", [(i, i ^ mask) for i in range(lax.axis_size("ctx"))])


def attention_kernel(first, last, distances, n_head, starts_ref, recv_starts_ref, *refs):
    refs = list(refs)
    me = lax.axis_index("ctx")
    pair, core, col = me // 2, me % 2, (me // 2) % 2
    if first:
        queries_ref, q_recv_ref, own_ref = refs[:3]
        refs = refs[3:]
    else:
        q_ref, top_in, acc_in = refs[:3]
        refs = refs[3:]
    pieces = refs[: len(distances)]
    refs = refs[len(distances) :]
    if first:
        q_ref, top_ref, acc_ref, held_ref = refs
    elif last:
        out_own, out_other, held_ref, top_ref, acc_ref = refs
    else:
        top_ref, acc_ref, held_ref = refs
    tok = starts_ref.shape[0] * BLOCK
    half = tok // BLOCK
    blocks = 2 * half
    rows = n_head * BLOCK

    def start_of(b):
        mine = b // half == core
        return jnp.where(mine, starts_ref[b % half], recv_starts_ref[b % half])

    def rows_of(ref, j, lane0):
        t = slice(j * BLOCK, (j + 1) * BLOCK)
        return jnp.concatenate(
            [ref[t, pl.ds(lane0 + h * HEAD_SIZE, HEAD_SIZE)] for h in range(n_head)], axis=0
        )

    def value_ones(piece_ref, width):
        v = piece_ref[:width, HEAD_SIZE:]
        return jnp.concatenate([v, jnp.ones_like(v)], axis=1)

    def dot_t(a, b):
        return lax.dot_general(a, b, (((1,), (1,)), ((), ())), preferred_element_type=jnp.float32)

    factor = HEAD_SIZE**-0.5 * LOG2E
    tiles = [(b, slice(r, r + TILE)) for b in range(blocks) for r in range(0, rows, TILE)]

    def keep(s, since):
        k_id = lax.broadcasted_iota(jnp.int32, (1, s.shape[1]), 1)
        return jnp.where(k_id >= since, s, MASKED)

    if first:
        for j in range(half):
            mine = rows_of(queries_ref, j, pl.multiple_of(core * rows, rows))
            q_ref[core * half + j] = mine
            q_ref[(1 - core) * half + j] = rows_of(q_recv_ref, j, 0)
        t_id = lax.broadcasted_iota(jnp.int32, (TILE, BLOCK), 0) % BLOCK
        causal = lax.broadcasted_iota(jnp.int32, (TILE, BLOCK), 1) <= t_id
        for b, r in tiles:
            width = (b + 1) * BLOCK
            s = dot_t(q_ref[b, r], own_ref[:width, :HEAD_SIZE])
            since = start_of(b) - pair * 2 * tok
            diag = jnp.where(causal, s[:, b * BLOCK :], MASKED)
            s = jnp.concatenate([keep(s[:, : b * BLOCK], since), diag], 1) if b else diag
            top = jnp.max(s, axis=1, keepdims=True)
            p = jnp.exp2(s * factor - top * factor).astype(jnp.bfloat16)
            top_ref[b, r] = jnp.broadcast_to(top, (TILE, HEAD_SIZE))
            acc_ref[b, r] = jnp.dot(p, value_ones(own_ref, width), preferred_element_type=jnp.float32)
    else:
        top_ref[...] = top_in[...]
        acc_ref[...] = acc_in[...]

    for i, piece_ref in enumerate(pieces):
        held_ref[i] = piece_ref[...]

    @pl.loop(0, 2 * len(pieces))
    def _(step):
        i, first_block = step // 2, step % 2 * half
        behind = sum(
            jnp.where(i == n, jnp.where(col == 0, *d), 0) for n, d in enumerate(distances)
        )
        base = (pair - behind) * 2 * tok

        @pl.when(start_of(first_block) < base + 2 * tok)
        def _():
            for b, r in tiles[: len(tiles) // 2]:
                b = first_block + b
                s = keep(dot_t(q_ref[b, r], held_ref[i, :, :HEAD_SIZE]), start_of(b) - base)
                old = top_ref[b, r][:, :1]
                top = jnp.maximum(old, jnp.max(s, axis=1, keepdims=True))
                p = jnp.exp2(s * factor - top * factor).astype(jnp.bfloat16)
                top_ref[b, r] = jnp.broadcast_to(top, (TILE, HEAD_SIZE))
                acc_ref[b, r] = acc_ref[b, r] * jnp.exp2((old - top) * factor) + jnp.dot(
                    p, value_ones(held_ref.at[i], 2 * tok), preferred_element_type=jnp.float32
                )

    if last:
        for j in range(half):
            for out, shard in ((out_own, core), (out_other, 1 - core)):
                acc = acc_ref[shard * half + j]
                o = (acc[:, :HEAD_SIZE] / acc[:, HEAD_SIZE:]).astype(jnp.bfloat16)
                for h in range(n_head):
                    out[j * BLOCK : (j + 1) * BLOCK, h * HEAD_SIZE : (h + 1) * HEAD_SIZE] = o[
                        h * BLOCK : (h + 1) * BLOCK
                    ]


def attention_call(first, last, distances, n_head, starts, recv_starts, operands):
    tok = starts.shape[0] * BLOCK
    blocks, rows = 2 * starts.shape[0], n_head * BLOCK
    state = [
        jax.ShapeDtypeStruct((blocks, rows, HEAD_SIZE), jnp.float32),
        jax.ShapeDtypeStruct((blocks, rows, 2 * HEAD_SIZE), jnp.float32),
    ]
    scratch = [pltpu.VMEM((len(distances), 2 * tok, 2 * HEAD_SIZE), jnp.bfloat16)]
    if first:
        outs = [jax.ShapeDtypeStruct((blocks, rows, HEAD_SIZE), jnp.bfloat16)] + state
    elif last:
        outs = [jax.ShapeDtypeStruct((tok, rows), jnp.bfloat16)] * 2
        scratch += [pltpu.VMEM(s.shape, s.dtype) for s in state]
    else:
        outs = state
    n_pieces = len(distances) + 0.5 * first
    vmem, smem = pl.BlockSpec(memory_space=pltpu.VMEM), pl.BlockSpec(memory_space=pltpu.SMEM)
    return pl.pallas_call(
        functools.partial(attention_kernel, first, last, distances, n_head),
        out_shape=outs,
        in_specs=[smem, smem] + [vmem] * len(operands),
        out_specs=[vmem] * len(outs),
        scratch_shapes=scratch,
        compiler_params=pltpu.CompilerParams(vmem_limit_bytes=40 * 2**20),
        cost_estimate=pl.CostEstimate(
            flops=int(n_pieces * blocks * rows * 2 * tok * HEAD_SIZE * 8),
            bytes_accessed=8 * 2**20,
            transcendentals=int(n_pieces * blocks * rows * 2 * tok),
        ),
    )(starts, recv_starts, *operands)


def per_device(queries, keys, values, block_start, out_weight):
    tok = queries.shape[0]
    group = queries.shape[1] // 2
    n_head = group // HEAD_SIZE
    me = lax.axis_index("ctx")
    core, col = me % 2, (me // 2) % 2
    head = lax.axis_index("head")

    def part(x, index, size):
        return lax.dynamic_slice_in_dim(x, index * size, size, 1)

    mine = jnp.concatenate([part(keys, core, HEAD_SIZE), part(values, core, HEAD_SIZE)], 1)
    theirs = jnp.concatenate([part(keys, 1 - core, HEAD_SIZE), part(values, 1 - core, HEAD_SIZE)], 1)
    recv = swap(theirs, 1)
    own = jnp.where(core == 0, jnp.concatenate([mine, recv]), jnp.concatenate([recv, mine]))
    one_behind = shift(own, 4)
    q_recv = swap(part(queries, 1 - core, group), 1)
    recv_starts = swap(block_start, 1)
    two_behind = shift(one_behind, 4)
    across = swap(one_behind, 2)
    q, top, acc = attention_call(
        True, False, ((2, 2),), n_head, block_start, recv_starts, (queries, q_recv, own, one_behind)
    )
    third = swap(jnp.where(col == 1, two_behind, own), 2)
    top, acc = attention_call(
        False, False, ((1, 3), (4, 4)), n_head, block_start, recv_starts,
        (q, top, acc, across, two_behind),
    )
    o_own, o_other = attention_call(
        False, True, ((3, 1),), n_head, block_start, recv_starts, (q, top, acc, third)
    )
    o_recv = swap(o_other, 1)
    heads_out = jnp.where(
        core == 0, jnp.concatenate([o_own, o_recv], 1), jnp.concatenate([o_recv, o_own], 1)
    )
    cols = out_weight.shape[1] // 2
    away = jnp.dot(heads_out, part(out_weight, 1 - head, cols), preferred_element_type=jnp.float32)
    away = lax.ppermute(away.astype(jnp.bfloat16), "head", [(0, 1), (1, 0)])
    here = jnp.dot(heads_out, part(out_weight, head, cols), preferred_element_type=jnp.float32)
    here = here.astype(jnp.bfloat16).astype(jnp.float32)
    return (here + away.astype(jnp.float32)).astype(jnp.bfloat16)


def solution(mesh):
    in_specs = (P("ctx", "head"), P("ctx", "head"), P("ctx", "head"), P("ctx"), P("head", None))
    out_specs = P("ctx", "head")
    return jax.shard_map(
        per_device, mesh=mesh, in_specs=in_specs, out_specs=out_specs, check_vma=False
    )
```

```python
import functools

import jax
import jax.numpy as jnp
from jax import lax
from jax.experimental import pallas as pl
from jax.experimental.pallas import tpu as pltpu
from jax.sharding import PartitionSpec as P

HEAD_SIZE = 128
BLOCK = 128
LOG2E = 1.4426950408889634
MASKED = -1e30
W_CHUNKS = 2
TILE = 256


def shift(x, distance):
    n = lax.axis_size("ctx")
    return lax.ppermute(x, "ctx", [(i, i + distance) for i in range(n - distance)])


def swap(x, mask):
    return lax.ppermute(x, "ctx", [(i, i ^ mask) for i in range(lax.axis_size("ctx"))])


def cross(x, mask):
    n = lax.axis_size("ctx")
    route = [(2 * i + h, 2 * (i ^ mask) + 1 - h) for i in range(n) for h in range(2)]
    return lax.ppermute(x, ("ctx", "head"), route)


def project_kernel(*refs):
    given_ref, heads_ref, *chunk_refs, out_ref = refs
    chunk = chunk_refs[0].shape[0]

    @pl.loop(0, out_ref.shape[1] // 512)
    def _(n):
        cols = pl.ds(pl.multiple_of(n * 512, 512), 512)
        total = given_ref[:, cols]
        for m, ref in enumerate(chunk_refs):
            total += jnp.dot(
                heads_ref[:, m * chunk : (m + 1) * chunk],
                ref[:, cols],
                preferred_element_type=jnp.float32,
            )
        out_ref[:, cols] = total.astype(out_ref.dtype)


def project(given, heads, chunks, dtype):
    vmem = pl.BlockSpec(memory_space=pltpu.VMEM)
    return pl.pallas_call(
        project_kernel,
        out_shape=jax.ShapeDtypeStruct(given.shape, dtype),
        in_specs=[vmem] * (2 + len(chunks)),
        out_specs=vmem,
        compiler_params=pltpu.CompilerParams(vmem_limit_bytes=40 * 2**20),
        cost_estimate=pl.CostEstimate(
            flops=2 * heads.shape[0] * heads.shape[1] * given.shape[1],
            bytes_accessed=8 * 2**20,
            transcendentals=0,
        ),
    )(given, heads, *chunks)


def attention_kernel(first, last, distances, n_head, starts_ref, recv_starts_ref, *refs):
    refs = list(refs)
    me = lax.axis_index("ctx")
    pair, core, col = me // 2, me % 2, (me // 2) % 2
    if first:
        queries_ref, q_recv_ref, own_ref = refs[:3]
        refs = refs[3:]
    else:
        q_ref, top_in, acc_in = refs[:3]
        refs = refs[3:]
    pieces = refs[: len(distances)]
    refs = refs[len(distances) :]
    if first:
        q_ref, top_ref, acc_ref, held_ref = refs
    elif last:
        out_ref, acc_ref = refs
    else:
        top_ref, acc_ref, held_ref = refs
    tok = starts_ref.shape[0] * BLOCK
    half = tok // BLOCK
    blocks = 2 * half
    rows = n_head * BLOCK

    def start_of(b):
        mine = b // half == core
        return jnp.where(mine, starts_ref[b % half], recv_starts_ref[b % half])

    def rows_of(ref, j, lane0):
        t = slice(j * BLOCK, (j + 1) * BLOCK)
        return jnp.concatenate(
            [ref[t, pl.ds(lane0 + h * HEAD_SIZE, HEAD_SIZE)] for h in range(n_head)], axis=0
        )

    def value_ones(piece_ref, width):
        v = piece_ref[:width, HEAD_SIZE:]
        return jnp.concatenate([v, jnp.ones_like(v)], axis=1)

    def dot_t(a, b):
        return lax.dot_general(a, b, (((1,), (1,)), ((), ())), preferred_element_type=jnp.float32)

    factor = HEAD_SIZE**-0.5 * LOG2E
    tiles = [(b, slice(r, r + TILE)) for b in range(blocks) for r in range(0, rows, TILE)]

    def keep(s, since):
        k_id = lax.broadcasted_iota(jnp.int32, (1, s.shape[1]), 1)
        return jnp.where(k_id >= since, s, MASKED)

    def update(piece_ref, base, b, r, top_from, acc_from, to):
        s = keep(dot_t(q_ref[b, r], piece_ref[:, :HEAD_SIZE]), start_of(b) - base)
        old = top_from[b, r][:, :1]
        top = jnp.maximum(old, jnp.max(s, axis=1, keepdims=True))
        p = jnp.exp2(s * factor - top * factor).astype(jnp.bfloat16)
        if not last:
            top_ref[to, r] = jnp.broadcast_to(top, (TILE, HEAD_SIZE))
        acc_ref[to, r] = acc_from[b, r] * jnp.exp2((old - top) * factor) + jnp.dot(
            p, value_ones(piece_ref, 2 * tok), preferred_element_type=jnp.float32
        )

    def attend_last(first_block):
        base = (pair - jnp.where(col == 0, *distances[0])) * 2 * tok
        needed = start_of(first_block) < base + 2 * tok

        @pl.when(needed)
        def _():
            for b, r in tiles[: len(tiles) // 2]:
                update(pieces[0], base, first_block + b, r, top_in, acc_in, b)

        @pl.when(jnp.logical_not(needed))
        def _():
            acc_ref[...] = acc_in[pl.ds(first_block, half)]

        for j in range(half):
            o = (acc_ref[j, :, :HEAD_SIZE] / acc_ref[j, :, HEAD_SIZE:]).astype(jnp.bfloat16)
            for h in range(n_head):
                out_ref[j * BLOCK : (j + 1) * BLOCK, h * HEAD_SIZE : (h + 1) * HEAD_SIZE] = o[
                    h * BLOCK : (h + 1) * BLOCK
                ]

    if first:
        for j in range(half):
            mine = rows_of(queries_ref, j, pl.multiple_of(core * rows, rows))
            q_ref[core * half + j] = mine
            q_ref[(1 - core) * half + j] = rows_of(q_recv_ref, j, 0)
        t_id = lax.broadcasted_iota(jnp.int32, (TILE, BLOCK), 0) % BLOCK
        causal = lax.broadcasted_iota(jnp.int32, (TILE, BLOCK), 1) <= t_id
        for b, r in tiles:
            width = (b + 1) * BLOCK
            s = dot_t(q_ref[b, r], own_ref[:width, :HEAD_SIZE])
            since = start_of(b) - pair * 2 * tok
            diag = jnp.where(causal, s[:, b * BLOCK :], MASKED)
            s = jnp.concatenate([keep(s[:, : b * BLOCK], since), diag], 1) if b else diag
            top = jnp.max(s, axis=1, keepdims=True)
            p = jnp.exp2(s * factor - top * factor).astype(jnp.bfloat16)
            top_ref[b, r] = jnp.broadcast_to(top, (TILE, HEAD_SIZE))
            acc_ref[b, r] = jnp.dot(p, value_ones(own_ref, width), preferred_element_type=jnp.float32)
    elif last:
        shard = core if last == "own" else 1 - core
        attend_last(shard * half)
        return
    else:
        top_ref[...] = top_in[...]
        acc_ref[...] = acc_in[...]

    for i, piece_ref in enumerate(pieces):
        held_ref[i] = piece_ref[...]

    @pl.loop(0, 2 * len(pieces))
    def _(step):
        i, first_block = step // 2, step % 2 * half
        behind = sum(
            jnp.where(i == n, jnp.where(col == 0, *d), 0) for n, d in enumerate(distances)
        )
        base = (pair - behind) * 2 * tok

        @pl.when(start_of(first_block) < base + 2 * tok)
        def _():
            for b, r in tiles[: len(tiles) // 2]:
                b = first_block + b
                update(held_ref.at[i], base, b, r, top_ref, acc_ref, b)


def attention_call(first, last, distances, n_head, starts, recv_starts, operands):
    tok = starts.shape[0] * BLOCK
    blocks, rows = 2 * starts.shape[0], n_head * BLOCK
    state = [
        jax.ShapeDtypeStruct((blocks, rows, HEAD_SIZE), jnp.float32),
        jax.ShapeDtypeStruct((blocks, rows, 2 * HEAD_SIZE), jnp.float32),
    ]
    scratch = [pltpu.VMEM((len(distances), 2 * tok, 2 * HEAD_SIZE), jnp.bfloat16)]
    if first:
        outs = [jax.ShapeDtypeStruct((blocks, rows, HEAD_SIZE), jnp.bfloat16)] + state
    elif last:
        outs = [jax.ShapeDtypeStruct((tok, rows), jnp.bfloat16)]
        scratch = [pltpu.VMEM((blocks // 2, rows, 2 * HEAD_SIZE), jnp.float32)]
    else:
        outs = state
    n_pieces = (len(distances) + 0.5 * first) / (2 if last else 1)
    vmem, smem = pl.BlockSpec(memory_space=pltpu.VMEM), pl.BlockSpec(memory_space=pltpu.SMEM)
    return pl.pallas_call(
        functools.partial(attention_kernel, first, last, distances, n_head),
        out_shape=outs,
        in_specs=[smem, smem] + [vmem] * len(operands),
        out_specs=[vmem] * len(outs),
        scratch_shapes=scratch,
        compiler_params=pltpu.CompilerParams(vmem_limit_bytes=40 * 2**20),
        cost_estimate=pl.CostEstimate(
            flops=int(n_pieces * blocks * rows * 2 * tok * HEAD_SIZE * 8),
            bytes_accessed=8 * 2**20,
            transcendentals=int(n_pieces * blocks * rows * 2 * tok),
        ),
    )(starts, recv_starts, *operands)


def per_device(queries, keys, values, block_start, out_weight):
    tok = queries.shape[0]
    group = queries.shape[1] // 2
    n_head = group // HEAD_SIZE
    me = lax.axis_index("ctx")
    core, col = me % 2, (me // 2) % 2
    head = lax.axis_index("head")

    def part(x, index, size):
        return lax.dynamic_slice_in_dim(x, index * size, size, 1)

    def rows_at(index, size=group):
        return lax.dynamic_slice_in_dim(out_weight, index * size, size, 0)

    cols = out_weight.shape[1] // 2
    chunk = group // W_CHUNKS
    mine = jnp.concatenate([part(keys, core, HEAD_SIZE), part(values, core, HEAD_SIZE)], 1)
    theirs = jnp.concatenate([part(keys, 1 - core, HEAD_SIZE), part(values, 1 - core, HEAD_SIZE)], 1)
    recv = swap(theirs, 1)
    own = jnp.where(core == 0, jnp.concatenate([mine, recv]), jnp.concatenate([recv, mine]))
    one_behind = shift(own, 4)
    q_recv = swap(part(queries, 1 - core, group), 1)
    recv_starts = swap(block_start, 1)
    sent = part(rows_at(core), 1 - head, cols)
    over = [
        cross(sent[n * chunk : (n + 1) * chunk], 0) for n in range(W_CHUNKS)
    ]
    weights = [over, [swap(w, 1) for w in over]]
    two_behind = shift(one_behind, 4)
    across = swap(one_behind, 2)
    q, top, acc = attention_call(
        True, False, ((2, 2),), n_head, block_start, recv_starts, (queries, q_recv, own, one_behind)
    )
    third = swap(jnp.where(col == 1, two_behind, own), 2)
    top, acc = attention_call(
        False, False, ((1, 3), (4, 4)), n_head, block_start, recv_starts,
        (q, top, acc, across, two_behind),
    )
    last = [
        attention_call(
            False, which, ((3, 1),), n_head, block_start, recv_starts, (q, top, acc, third)
        )[0]
        for which in ("own", "other")
    ]
    o_across = [cross(last[0], 0), cross(last[1], 1)]
    o_swapped = swap(last[1], 1)
    here = sum(
        jnp.dot(o, part(rows_at(c), head, cols), preferred_element_type=jnp.float32)
        for o, c in ((last[0], core), (o_swapped, 1 - core))
    )
    here = project(here, o_across[0], weights[0], jnp.float32)
    return project(here, o_across[1], weights[1], jnp.bfloat16)


def solution(mesh):
    in_specs = (P("ctx", "head"), P("ctx", "head"), P("ctx", "head"), P("ctx"), P("head", None))
    out_specs = P("ctx", "head")
    return jax.shard_map(
        per_device, mesh=mesh, in_specs=in_specs, out_specs=out_specs, check_vma=False
    )
```

```python
import functools

import jax
import jax.numpy as jnp
from jax import lax
from jax.experimental import pallas as pl
from jax.experimental.pallas import tpu as pltpu
from jax.sharding import PartitionSpec as P

HEAD_SIZE = 128
BLOCK = 128
LOG2E = 1.4426950408889634
MASKED = -1e30
TILE = 256


def shift(x, distance):
    n = lax.axis_size("ctx")
    return lax.ppermute(x, "ctx", [(i, i + distance) for i in range(n - distance)])


def swap(x, mask):
    return lax.ppermute(x, "ctx", [(i, i ^ mask) for i in range(lax.axis_size("ctx"))])


def cross(x, mask):
    n = lax.axis_size("ctx")
    route = [(2 * i + h, 2 * (i ^ mask) + 1 - h) for i in range(n) for h in range(2)]
    return lax.ppermute(x, ("ctx", "head"), route)


def project_kernel(given_ref, heads_a, rows_a, heads_b, rows_b, out_ref):
    width = out_ref.shape[1]
    cols = pl.ds(pl.multiple_of(pl.program_id(0) * width, width), width)
    total = given_ref[:, cols].astype(jnp.float32)
    for heads, rows in ((heads_a, rows_a), (heads_b, rows_b)):
        total += jnp.dot(heads[...], rows[:, cols], preferred_element_type=jnp.float32)
    out_ref[...] = total.astype(out_ref.dtype)


def project(given, *terms):
    tok, cols = given.shape
    vmem = pl.BlockSpec(memory_space=pltpu.VMEM)
    return pl.pallas_call(
        project_kernel,
        grid=(cols // 512,),
        out_shape=jax.ShapeDtypeStruct(given.shape, jnp.bfloat16),
        in_specs=[vmem] * 5,
        out_specs=pl.BlockSpec((tok, 512), lambda n: (0, n)),
        compiler_params=pltpu.CompilerParams(vmem_limit_bytes=16 * 2**20),
        cost_estimate=pl.CostEstimate(
            flops=4 * tok * terms[0].shape[1] * cols, bytes_accessed=8 * 2**20, transcendentals=0
        ),
    )(given, *terms)


def attention_kernel(first, last, distances, n_head, n_after, starts_ref, recv_starts_ref, *refs):
    refs = list(refs)
    me = lax.axis_index("ctx")
    pair, core, col = me // 2, me % 2, (me // 2) % 2
    if first:
        queries_ref, q_recv_ref, own_ref = refs[:3]
        refs = refs[3:]
    else:
        q_ref, top_in, acc_in = refs[:3]
        refs = refs[3:]
    pieces = refs[: len(distances)]
    refs = refs[len(distances) + n_after :]
    if first:
        q_ref, top_ref, acc_ref, held_ref = refs
    elif last:
        out_ref, acc_ref = refs[0], refs[-1]
    else:
        top_ref, acc_ref, held_ref = refs
    tok = starts_ref.shape[0] * BLOCK
    half = tok // BLOCK
    blocks = 2 * half
    rows = n_head * BLOCK

    def start_of(b):
        mine = b // half == core
        return jnp.where(mine, starts_ref[b % half], recv_starts_ref[b % half])

    def rows_of(ref, j, lane0):
        t = slice(j * BLOCK, (j + 1) * BLOCK)
        return jnp.concatenate(
            [ref[t, pl.ds(lane0 + h * HEAD_SIZE, HEAD_SIZE)] for h in range(n_head)], axis=0
        )

    def value_ones(piece_ref, width):
        v = piece_ref[:width, HEAD_SIZE:]
        return jnp.concatenate([v, jnp.ones_like(v)], axis=1)

    def dot_t(a, b):
        return lax.dot_general(a, b, (((1,), (1,)), ((), ())), preferred_element_type=jnp.float32)

    factor = HEAD_SIZE**-0.5 * LOG2E
    tiles = [(b, slice(r, r + TILE)) for b in range(blocks) for r in range(0, rows, TILE)]

    def keep(s, since):
        k_id = lax.broadcasted_iota(jnp.int32, (1, s.shape[1]), 1)
        return jnp.where(k_id >= since, s, MASKED)

    def update(piece_ref, base, b, r, top_from, acc_from, to):
        s = keep(dot_t(q_ref[b, r], piece_ref[:, :HEAD_SIZE]), start_of(b) - base)
        old = top_from[b, r][:, :1]
        top = jnp.maximum(old, jnp.max(s, axis=1, keepdims=True))
        p = jnp.exp2(s * factor - top * factor).astype(jnp.bfloat16)
        if not last:
            top_ref[to, r] = jnp.broadcast_to(top, (TILE, HEAD_SIZE))
        acc_ref[to, r] = acc_from[b, r] * jnp.exp2((old - top) * factor) + jnp.dot(
            p, value_ones(piece_ref, 2 * tok), preferred_element_type=jnp.float32
        )

    def attend_last(first_block):
        base = (pair - jnp.where(col == 0, *distances[0])) * 2 * tok
        needed = start_of(first_block) < base + 2 * tok

        @pl.when(needed)
        def _():
            for b, r in tiles[: len(tiles) // 2]:
                update(pieces[0], base, first_block + b, r, top_in, acc_in, b)

        @pl.when(jnp.logical_not(needed))
        def _():
            acc_ref[...] = acc_in[pl.ds(first_block, half)]

        for j in range(half):
            o = (acc_ref[j, :, :HEAD_SIZE] / acc_ref[j, :, HEAD_SIZE:]).astype(jnp.bfloat16)
            for h in range(n_head):
                out_ref[j * BLOCK : (j + 1) * BLOCK, h * HEAD_SIZE : (h + 1) * HEAD_SIZE] = o[
                    h * BLOCK : (h + 1) * BLOCK
                ]

    if first:
        for j in range(half):
            mine = rows_of(queries_ref, j, pl.multiple_of(core * rows, rows))
            q_ref[core * half + j] = mine
            q_ref[(1 - core) * half + j] = rows_of(q_recv_ref, j, 0)
        t_id = lax.broadcasted_iota(jnp.int32, (TILE, BLOCK), 0) % BLOCK
        causal = lax.broadcasted_iota(jnp.int32, (TILE, BLOCK), 1) <= t_id
        for b, r in tiles:
            width = (b + 1) * BLOCK
            s = dot_t(q_ref[b, r], own_ref[:width, :HEAD_SIZE])
            since = start_of(b) - pair * 2 * tok
            diag = jnp.where(causal, s[:, b * BLOCK :], MASKED)
            s = jnp.concatenate([keep(s[:, : b * BLOCK], since), diag], 1) if b else diag
            top = jnp.max(s, axis=1, keepdims=True)
            p = jnp.exp2(s * factor - top * factor).astype(jnp.bfloat16)
            top_ref[b, r] = jnp.broadcast_to(top, (TILE, HEAD_SIZE))
            acc_ref[b, r] = jnp.dot(p, value_ones(own_ref, width), preferred_element_type=jnp.float32)
    elif last:
        shard = core if last == "own" else 1 - core
        attend_last(shard * half)
        return
    else:
        top_ref[...] = top_in[...]
        acc_ref[...] = acc_in[...]

    for i, piece_ref in enumerate(pieces):
        held_ref[i] = piece_ref[...]

    @pl.loop(0, 2 * len(pieces))
    def _(step):
        i, first_block = step // 2, step % 2 * half
        behind = sum(
            jnp.where(i == n, jnp.where(col == 0, *d), 0) for n, d in enumerate(distances)
        )
        base = (pair - behind) * 2 * tok

        @pl.when(start_of(first_block) < base + 2 * tok)
        def _():
            for b, r in tiles[: len(tiles) // 2]:
                b = first_block + b
                update(held_ref.at[i], base, b, r, top_ref, acc_ref, b)


def attention_call(first, last, distances, n_head, starts, recv_starts, operands, held=(), after=()):
    tok = starts.shape[0] * BLOCK
    blocks, rows = 2 * starts.shape[0], n_head * BLOCK
    state = [
        jax.ShapeDtypeStruct((blocks, rows, HEAD_SIZE), jnp.float32),
        jax.ShapeDtypeStruct((blocks, rows, 2 * HEAD_SIZE), jnp.float32),
    ]
    scratch = [pltpu.VMEM((len(distances), 2 * tok, 2 * HEAD_SIZE), jnp.bfloat16)]
    if first:
        outs = [jax.ShapeDtypeStruct((blocks, rows, HEAD_SIZE), jnp.bfloat16)] + state
    elif last:
        outs = [jax.ShapeDtypeStruct((tok, rows), jnp.bfloat16)]
        scratch = [pltpu.VMEM((blocks // 2, rows, 2 * HEAD_SIZE), jnp.float32)]
    else:
        outs = state
    n_pieces = (len(distances) + 0.5 * first) / (2 if last else 1)
    vmem, smem = pl.BlockSpec(memory_space=pltpu.VMEM), pl.BlockSpec(memory_space=pltpu.SMEM)
    return pl.pallas_call(
        functools.partial(attention_kernel, first, last, distances, n_head, len(held + after)),
        out_shape=outs + [jax.ShapeDtypeStruct(x.shape, x.dtype) for x in held],
        in_specs=[smem, smem] + [vmem] * len(operands) + [pl.BlockSpec(memory_space=pl.ANY)] * len(held + after),
        out_specs=[vmem] * len(outs) + [pl.BlockSpec(memory_space=pl.ANY)] * len(held),
        scratch_shapes=scratch,
        input_output_aliases={2 + len(operands) + n: len(outs) + n for n in range(len(held))},
        compiler_params=pltpu.CompilerParams(vmem_limit_bytes=24 * 2**20),
        cost_estimate=pl.CostEstimate(
            flops=int(n_pieces * blocks * rows * 2 * tok * HEAD_SIZE * 8),
            bytes_accessed=8 * 2**20,
            transcendentals=int(n_pieces * blocks * rows * 2 * tok),
        ),
    )(starts, recv_starts, *operands, *held, *after)


def per_device(queries, keys, values, block_start, out_weight):
    tok = queries.shape[0]
    group = queries.shape[1] // 2
    n_head = group // HEAD_SIZE
    me = lax.axis_index("ctx")
    core, col = me % 2, (me // 2) % 2
    head = lax.axis_index("head")

    def part(x, index, size):
        return lax.dynamic_slice_in_dim(x, index * size, size, 1)

    def rows_at(index):
        return lax.dynamic_slice_in_dim(out_weight, index * group, group, 0)

    cols = out_weight.shape[1] // 2
    mine = jnp.concatenate([part(keys, core, HEAD_SIZE), part(values, core, HEAD_SIZE)], 1)
    theirs = jnp.concatenate([part(keys, 1 - core, HEAD_SIZE), part(values, 1 - core, HEAD_SIZE)], 1)
    recv = swap(theirs, 1)
    own = jnp.where(core == 0, jnp.concatenate([mine, recv]), jnp.concatenate([recv, mine]))
    one_behind = shift(own, 4)
    q_recv = swap(part(queries, 1 - core, group), 1)
    recv_starts = swap(block_start, 1)
    rows_own = cross(part(rows_at(core), 1 - head, cols), 0)
    two_behind = shift(one_behind, 4)
    across = swap(one_behind, 2)
    q, top, acc = attention_call(
        True, False, ((2, 2),), n_head, block_start, recv_starts, (queries, q_recv, own, one_behind)
    )
    third = swap(jnp.where(col == 1, two_behind, own), 2)
    top, acc = attention_call(
        False, False, ((1, 3), (4, 4)), n_head, block_start, recv_starts,
        (q, top, acc, across, two_behind),
    )
    args = (((3, 1),), n_head, block_start, recv_starts, (q, top, acc, third))
    (o_other,) = attention_call(False, "other", *args)
    across_other = cross(o_other, 1)
    swapped_other = swap(o_other, 1)
    o_own, rows_own = attention_call(False, "own", *args, (rows_own,), (o_other,))
    across_own = cross(o_own, 0)
    rows_other = swap(rows_own, 1)
    here = jnp.dot(o_own, part(rows_at(core), head, cols), preferred_element_type=jnp.float32)
    here += jnp.dot(
        swapped_other, part(rows_at(1 - core), head, cols), preferred_element_type=jnp.float32
    )
    return project(here.astype(jnp.bfloat16), across_own, rows_own, across_other, rows_other)


def solution(mesh):
    in_specs = (P("ctx", "head"), P("ctx", "head"), P("ctx", "head"), P("ctx"), P("head", None))
    out_specs = P("ctx", "head")
    return jax.shard_map(
        per_device, mesh=mesh, in_specs=in_specs, out_specs=out_specs, check_vma=False
    )
```

```python
import functools

import jax
import jax.numpy as jnp
from jax import lax
from jax.experimental import pallas as pl
from jax.experimental.pallas import tpu as pltpu
from jax.sharding import PartitionSpec as P

HEAD_SIZE = 128
BLOCK = 128
LOG2E = 1.4426950408889634
MASKED = -1e30
TILE = 256


def shift(x, distance):
    n = lax.axis_size("ctx")
    return lax.ppermute(x, "ctx", [(i, i + distance) for i in range(n - distance)])


def swap(x, mask):
    return lax.ppermute(x, "ctx", [(i, i ^ mask) for i in range(lax.axis_size("ctx"))])


def cross(x, mask):
    n = lax.axis_size("ctx")
    route = [(2 * i + h, 2 * (i ^ mask) + 1 - h) for i in range(n) for h in range(2)]
    return lax.ppermute(x, ("ctx", "head"), route)


def slice_kernel(weight_ref, _, *refs):
    outs, sems = refs[:2], refs[2]
    core, part = lax.axis_index("ctx") % 2, lax.axis_index("ctx") // 4 % 2
    rows, cols = outs[0].shape
    copies = []
    for n, out in enumerate(outs):
        col = ((1 - lax.axis_index("head")) * 4 + part * 2 + n) * cols
        source = weight_ref.at[pl.ds(core * rows, rows), pl.ds(pl.multiple_of(col, cols), cols)]
        copies.append(pltpu.make_async_copy(source, out, sems.at[n]))
    for copy in copies:
        copy.start()
    for copy in copies:
        copy.wait()


def slice_weight(weight, after):
    anywhere = pl.BlockSpec(memory_space=pl.ANY)
    hbm = pl.BlockSpec(memory_space=pltpu.HBM)
    out = jax.ShapeDtypeStruct((weight.shape[0] // 2, weight.shape[1] // 8), weight.dtype)
    return pl.pallas_call(
        slice_kernel,
        out_shape=[out] * 2,
        in_specs=[hbm, anywhere],
        out_specs=[hbm] * 2,
        scratch_shapes=[pltpu.SemaphoreType.DMA((2,))],
    )(weight, after)


def project_kernel(given_ref, heads_ref, *refs):
    tiles, out_ref, built, sems = refs[:8], refs[8], refs[9], refs[10]
    me = lax.axis_index("ctx")
    core, part = me % 2, me // 4 % 2
    group, width = tiles[0].shape
    copies = []
    for n in range(4):
        first = (part if n < 2 else 1 - part) * 2 + n % 2
        cols = pl.ds(pl.multiple_of(first * width, width), width)
        total = given_ref[:, cols].astype(jnp.float32)
        for index, tile in ((core, tiles[n]), (1 - core, tiles[4 + n])):
            heads = heads_ref[:, pl.ds(pl.multiple_of(index * group, group), group)]
            total += jnp.dot(heads, tile[...], preferred_element_type=jnp.float32)
        built[n] = total.astype(out_ref.dtype)
        copies.append(pltpu.make_async_copy(built.at[n], out_ref.at[:, cols], sems.at[n]))
        copies[-1].start()
    for copy in copies:
        copy.wait()


def project(given, heads, tiles):
    tok, cols = given.shape
    vmem = pl.BlockSpec(memory_space=pltpu.VMEM)
    return pl.pallas_call(
        project_kernel,
        out_shape=jax.ShapeDtypeStruct(given.shape, jnp.bfloat16),
        in_specs=[vmem] * 10,
        out_specs=pl.BlockSpec(memory_space=pltpu.HBM),
        scratch_shapes=[pltpu.VMEM((4, tok, cols // 4), jnp.bfloat16), pltpu.SemaphoreType.DMA((4,))],
        compiler_params=pltpu.CompilerParams(vmem_limit_bytes=16 * 2**20),
        cost_estimate=pl.CostEstimate(
            flops=2 * tok * heads.shape[1] * cols, bytes_accessed=4 * 2**20, transcendentals=0
        ),
    )(given, heads, *tiles)


def attention_kernel(stage, distances, n_head, n_after, starts_ref, recv_starts_ref, *refs):
    refs = list(refs)
    me = lax.axis_index("ctx")
    pair, core, col = me // 2, me % 2, (me // 2) % 2
    if stage == "first":
        queries_ref, q_recv_ref = refs[:2]
        refs = refs[2:]
    else:
        q_ref, top_in, acc_in = refs[:3]
        refs = refs[3:]
    n_pieces = len(distances)
    halves = refs[: 2 * n_pieces]
    refs = refs[2 * n_pieces + n_after :]
    if stage == "first":
        q_ref, top_ref, acc_ref, held_ref = refs
    elif stage == "next":
        top_ref, acc_ref, held_ref = refs
    else:
        if stage == "own":
            swapped_ref, *refs = refs
        out_ref, acc_ref, held_ref = refs
    tok = starts_ref.shape[0] * BLOCK
    half = tok // BLOCK
    blocks = 2 * half
    rows = n_head * BLOCK
    factor = HEAD_SIZE**-0.5 * LOG2E
    tiles = [(b, slice(r, r + TILE)) for b in range(blocks) for r in range(0, rows, TILE)]

    for n, ref in enumerate(halves):
        shard = core if n % 2 == 0 else 1 - core
        held_ref[n // 2, pl.ds(pl.multiple_of(shard * tok, tok), tok)] = ref[...]

    def start_of(b):
        mine = b // half == core
        return jnp.where(mine, starts_ref[b % half], recv_starts_ref[b % half])

    def rows_of(ref, j, lane0):
        t = slice(j * BLOCK, (j + 1) * BLOCK)
        return jnp.concatenate(
            [ref[t, pl.ds(lane0 + h * HEAD_SIZE, HEAD_SIZE)] for h in range(n_head)], axis=0
        )

    def scores(b, r, i, width):
        k = held_ref[i, :width, :HEAD_SIZE]
        return lax.dot_general(
            q_ref[b, r], k, (((1,), (1,)), ((), ())), preferred_element_type=jnp.float32
        )

    def weigh(p, i, width):
        v = held_ref[i, :width, HEAD_SIZE:]
        v = jnp.concatenate([v, jnp.ones_like(v)], axis=1)
        return jnp.dot(p.astype(jnp.bfloat16), v, preferred_element_type=jnp.float32)

    def keep(s, since):
        k_id = lax.broadcasted_iota(jnp.int32, (1, s.shape[1]), 1)
        return jnp.where(k_id >= since, s, MASKED)

    def update(i, base, b, r, top_from, acc_from, to):
        s = keep(scores(b, r, i, 2 * tok), start_of(b) - base)
        old = top_from[b, r][:, :1]
        top = jnp.maximum(old, jnp.max(s, axis=1, keepdims=True))
        p = jnp.exp2(s * factor - top * factor)
        if stage == "next":
            top_ref[to, r] = jnp.broadcast_to(top, (TILE, HEAD_SIZE))
        acc_ref[to, r] = acc_from[b, r] * jnp.exp2((old - top) * factor) + weigh(p, i, 2 * tok)

    def attend_own():
        for j in range(half):
            mine = rows_of(queries_ref, j, pl.multiple_of(core * rows, rows))
            q_ref[core * half + j] = mine
            q_ref[(1 - core) * half + j] = rows_of(q_recv_ref, j, 0)
        t_id = lax.broadcasted_iota(jnp.int32, (TILE, BLOCK), 0) % BLOCK
        causal = lax.broadcasted_iota(jnp.int32, (TILE, BLOCK), 1) <= t_id
        for b, r in tiles:
            width = (b + 1) * BLOCK
            s = scores(b, r, 0, width)
            since = start_of(b) - pair * 2 * tok
            diag = jnp.where(causal, s[:, b * BLOCK :], MASKED)
            s = jnp.concatenate([keep(s[:, : b * BLOCK], since), diag], 1) if b else diag
            top = jnp.max(s, axis=1, keepdims=True)
            p = jnp.exp2(s * factor - top * factor)
            top_ref[b, r] = jnp.broadcast_to(top, (TILE, HEAD_SIZE))
            acc_ref[b, r] = weigh(p, 0, width)

    def attend_next():
        top_ref[...] = top_in[...]
        acc_ref[...] = acc_in[...]

        @pl.loop(0, 2 * n_pieces)
        def _(step):
            i, first_block = step // 2, step % 2 * half
            behind = sum(
                jnp.where(i == n, jnp.where(col == 0, *d), 0) for n, d in enumerate(distances)
            )
            base = (pair - behind) * 2 * tok

            @pl.when(start_of(first_block) < base + 2 * tok)
            def _():
                for b, r in tiles[: len(tiles) // 2]:
                    b = first_block + b
                    update(i, base, b, r, top_ref, acc_ref, b)

    def attend_last(shard):
        first_block = shard * half
        base = (pair - jnp.where(col == 0, *distances[0])) * 2 * tok
        needed = start_of(first_block) < base + 2 * tok

        @pl.when(needed)
        def _():
            for b, r in tiles[: len(tiles) // 2]:
                update(0, base, first_block + b, r, top_in, acc_in, b)

        @pl.when(jnp.logical_not(needed))
        def _():
            acc_ref[...] = acc_in[pl.ds(first_block, half)]

        for j in range(half):
            o = (acc_ref[j, :, :HEAD_SIZE] / acc_ref[j, :, HEAD_SIZE:]).astype(jnp.bfloat16)
            for h in range(n_head):
                first = core * rows + h * HEAD_SIZE if stage == "own" else h * HEAD_SIZE
                lanes = pl.ds(pl.multiple_of(first, HEAD_SIZE), HEAD_SIZE)
                out_ref[j * BLOCK : (j + 1) * BLOCK, lanes] = o[h * BLOCK : (h + 1) * BLOCK]
        if stage == "own":
            out_ref[:, pl.ds(pl.multiple_of((1 - core) * rows, rows), rows)] = swapped_ref[...]

    if stage == "first":
        attend_own()
    elif stage == "next":
        attend_next()
    else:
        attend_last(core if stage == "own" else 1 - core)


def attention_call(stage, distances, starts, recv_starts, operands, after=()):
    tok, half = starts.shape[0] * BLOCK, starts.shape[0]
    rows = operands[1].shape[1]
    blocks, n_head, n_pieces = 2 * half, rows // BLOCK, len(distances)
    state = [
        jax.ShapeDtypeStruct((blocks, rows, HEAD_SIZE), jnp.float32),
        jax.ShapeDtypeStruct((blocks, rows, 2 * HEAD_SIZE), jnp.float32),
    ]
    scratch = [pltpu.VMEM((n_pieces, 2 * tok, 2 * HEAD_SIZE), jnp.bfloat16)]
    share = n_pieces
    if stage == "first":
        outs, share = [jax.ShapeDtypeStruct((blocks, rows, HEAD_SIZE), jnp.bfloat16)] + state, 0.6
    elif stage == "next":
        outs = state
    else:
        width = rows * (2 if stage == "own" else 1)
        outs, share = [jax.ShapeDtypeStruct((tok, width), jnp.bfloat16)], 0.5
        scratch = [pltpu.VMEM((half, rows, 2 * HEAD_SIZE), jnp.float32)] + scratch
    vmem, smem = pl.BlockSpec(memory_space=pltpu.VMEM), pl.BlockSpec(memory_space=pltpu.SMEM)
    return pl.pallas_call(
        functools.partial(attention_kernel, stage, distances, n_head, len(after)),
        out_shape=outs,
        in_specs=[smem, smem]
        + [vmem] * len(operands)
        + [pl.BlockSpec(memory_space=pl.ANY)] * len(after),
        out_specs=[vmem] * len(outs),
        scratch_shapes=scratch,
        compiler_params=pltpu.CompilerParams(vmem_limit_bytes=24 * 2**20),
        cost_estimate=pl.CostEstimate(
            flops=int(share * blocks * rows * 2 * tok * HEAD_SIZE * 8),
            bytes_accessed=8 * 2**20,
            transcendentals=int(share * blocks * rows * 2 * tok),
        ),
    )(starts, recv_starts, *operands, *after)


def per_device(queries, keys, values, block_start, out_weight):
    group = queries.shape[1] // 2
    me = lax.axis_index("ctx")
    core, col = me % 2, (me // 2) % 2
    head = lax.axis_index("head")

    def part(x, index, size):
        return lax.dynamic_slice_in_dim(x, index * size, size, 1)

    cols = out_weight.shape[1] // 2
    mine = jnp.concatenate([part(keys, core, HEAD_SIZE), part(values, core, HEAD_SIZE)], 1)
    theirs = jnp.concatenate([part(keys, 1 - core, HEAD_SIZE), part(values, 1 - core, HEAD_SIZE)], 1)
    own = (mine, swap(theirs, 1))
    q_recv = swap(part(queries, 1 - core, group), 1)
    recv_starts = swap(block_start, 1)
    one_behind = [shift(x, 4) for x in own]
    two_behind = [shift(x, 4) for x in one_behind]
    across = [swap(x, 2) for x in one_behind]
    third = [swap(jnp.where(col == 1, x, y), 2) for x, y in zip(two_behind, own, strict=True)]

    tiles = [cross(x, 0) for x in slice_weight(out_weight, one_behind[0])]
    tiles += [swap(x, 4) for x in tiles]

    starts = (block_start, recv_starts)
    q, *state = attention_call("first", ((0, 0),), *starts, (queries, q_recv, *own))
    state = attention_call("next", ((2, 2),), *starts, (q, *state, *one_behind))
    state = attention_call("next", ((1, 3), (4, 4)), *starts, (q, *state, *across, *two_behind))
    (o_other,) = attention_call("other", ((3, 1),), *starts, (q, *state, *third))
    (heads,) = attention_call("own", ((3, 1),), *starts, (q, *state, *third, swap(o_other, 1)))
    across = cross(heads, 0)
    here = jnp.dot(heads, part(out_weight, head, cols), preferred_element_type=jnp.float32)
    tiles += [swap(x, 1) for x in tiles]
    return project(here.astype(jnp.bfloat16), across, tiles)


def solution(mesh):
    in_specs = (P("ctx", "head"), P("ctx", "head"), P("ctx", "head"), P("ctx"), P("head", None))
    out_specs = P("ctx", "head")
    return jax.shard_map(
        per_device, mesh=mesh, in_specs=in_specs, out_specs=out_specs, check_vma=False
    )
```

```python
import functools

import jax
import jax.numpy as jnp
from jax import lax
from jax.experimental import pallas as pl
from jax.experimental.pallas import tpu as pltpu
from jax.sharding import PartitionSpec as P

HEAD_SIZE = 128
BLOCK = 128
LOG2E = 1.4426950408889634
MASKED = -1e30
TILE = 256


def shift(x, distance):
    n = lax.axis_size("ctx")
    return lax.ppermute(x, "ctx", [(i, i + distance) for i in range(n - distance)])


def swap(x, mask):
    return lax.ppermute(x, "ctx", [(i, i ^ mask) for i in range(lax.axis_size("ctx"))])


def cross(x, mask):
    n = lax.axis_size("ctx")
    route = [(2 * i + h, 2 * (i ^ mask) + 1 - h) for i in range(n) for h in range(2)]
    return lax.ppermute(x, ("ctx", "head"), route)


def slice_kernel(weight_ref, _, *refs):
    outs, sems = refs[:2], refs[2]
    core, part = lax.axis_index("ctx") % 2, lax.axis_index("ctx") // 4 % 2
    rows, cols = outs[0].shape
    copies = []
    for n, out in enumerate(outs):
        col = ((1 - lax.axis_index("head")) * 4 + part * 2 + n) * cols
        source = weight_ref.at[pl.ds(core * rows, rows), pl.ds(pl.multiple_of(col, cols), cols)]
        copies.append(pltpu.make_async_copy(source, out, sems.at[n]))
    for copy in copies:
        copy.start()
    for copy in copies:
        copy.wait()


def slice_weight(weight, after):
    anywhere = pl.BlockSpec(memory_space=pl.ANY)
    out = jax.ShapeDtypeStruct((weight.shape[0] // 2, weight.shape[1] // 8), weight.dtype)
    return pl.pallas_call(
        slice_kernel,
        out_shape=[out] * 2,
        in_specs=[pl.BlockSpec(memory_space=pltpu.HBM), anywhere],
        out_specs=[pl.BlockSpec(memory_space=pltpu.VMEM)] * 2,
        scratch_shapes=[pltpu.SemaphoreType.DMA((2,))],
        compiler_params=pltpu.CompilerParams(vmem_limit_bytes=57 * 2**20),
    )(weight, after)


def project_kernel(given_ref, heads_ref, *refs):
    tiles, out_ref, built, sems = refs[:8], refs[8], refs[9], refs[10]
    me = lax.axis_index("ctx")
    core, part = me % 2, me // 4 % 2
    group, width = tiles[0].shape
    copies = []
    for n in range(4):
        first = (part if n < 2 else 1 - part) * 2 + n % 2
        cols = pl.ds(pl.multiple_of(first * width, width), width)
        total = given_ref[:, cols].astype(jnp.float32)
        for index, tile in ((core, tiles[n]), (1 - core, tiles[4 + n])):
            heads = heads_ref[:, pl.ds(pl.multiple_of(index * group, group), group)]
            total += jnp.dot(heads, tile[...], preferred_element_type=jnp.float32)
        built[n] = total.astype(out_ref.dtype)
        copies.append(pltpu.make_async_copy(built.at[n], out_ref.at[:, cols], sems.at[n]))
        copies[-1].start()
    for copy in copies:
        copy.wait()


def project(given, heads, tiles):
    tok, cols = given.shape
    vmem = pl.BlockSpec(memory_space=pltpu.VMEM)
    return pl.pallas_call(
        project_kernel,
        out_shape=jax.ShapeDtypeStruct(given.shape, jnp.bfloat16),
        in_specs=[vmem] * 10,
        out_specs=pl.BlockSpec(memory_space=pltpu.HBM),
        scratch_shapes=[pltpu.VMEM((4, tok, cols // 4), jnp.bfloat16), pltpu.SemaphoreType.DMA((4,))],
        compiler_params=pltpu.CompilerParams(vmem_limit_bytes=16 * 2**20),
        cost_estimate=pl.CostEstimate(
            flops=2 * tok * heads.shape[1] * cols, bytes_accessed=4 * 2**20, transcendentals=0
        ),
    )(given, heads, *tiles)


def attention_kernel(stage, distances, n_head, n_after, starts_ref, recv_starts_ref, *refs):
    refs = list(refs)
    me = lax.axis_index("ctx")
    pair, core, col = me // 2, me % 2, (me // 2) % 2
    if stage == "first":
        queries_ref, q_recv_ref = refs[:2]
        refs = refs[2:]
    else:
        q_ref, top_in, acc_in = refs[:3]
        refs = refs[3:]
    n_pieces = len(distances)
    halves = refs[: 2 * n_pieces]
    refs = refs[2 * n_pieces + n_after :]
    if stage == "first":
        q_ref, top_ref, acc_ref, held_ref = refs
    elif stage == "next":
        top_ref, acc_ref, held_ref = refs
    else:
        if stage == "own":
            swapped_ref, *refs = refs
        out_ref, acc_ref, held_ref = refs
    tok = starts_ref.shape[0] * BLOCK
    half = tok // BLOCK
    blocks = 2 * half
    rows = n_head * BLOCK
    factor = HEAD_SIZE**-0.5 * LOG2E
    tiles = [(b, slice(r, r + TILE)) for b in range(blocks) for r in range(0, rows, TILE)]

    for n, ref in enumerate(halves):
        shard = core if n % 2 == 0 else 1 - core
        held_ref[n // 2, pl.ds(pl.multiple_of(shard * tok, tok), tok)] = ref[...]

    def start_of(b):
        mine = b // half == core
        return jnp.where(mine, starts_ref[b % half], recv_starts_ref[b % half])

    def rows_of(ref, j, lane0):
        t = slice(j * BLOCK, (j + 1) * BLOCK)
        return jnp.concatenate(
            [ref[t, pl.ds(lane0 + h * HEAD_SIZE, HEAD_SIZE)] for h in range(n_head)], axis=0
        )

    def scores(b, r, i, width):
        k = held_ref[i, :width, :HEAD_SIZE]
        return lax.dot_general(
            q_ref[b, r], k, (((1,), (1,)), ((), ())), preferred_element_type=jnp.float32
        )

    def weigh(p, i, width):
        v = held_ref[i, :width, HEAD_SIZE:]
        v = jnp.concatenate([v, jnp.ones_like(v)], axis=1)
        return jnp.dot(p.astype(jnp.bfloat16), v, preferred_element_type=jnp.float32)

    def keep(s, since):
        k_id = lax.broadcasted_iota(jnp.int32, (1, s.shape[1]), 1)
        return jnp.where(k_id >= since, s, MASKED)

    def update(i, base, b, r, top_from, acc_from, to):
        s = keep(scores(b, r, i, 2 * tok), start_of(b) - base)
        old = top_from[b, r][:, :1]
        top = jnp.maximum(old, jnp.max(s, axis=1, keepdims=True))
        p = jnp.exp2(s * factor - top * factor)
        if stage == "next":
            top_ref[to, r] = jnp.broadcast_to(top, (TILE, HEAD_SIZE))
        acc_ref[to, r] = acc_from[b, r] * jnp.exp2((old - top) * factor) + weigh(p, i, 2 * tok)

    def attend_own():
        for j in range(half):
            mine = rows_of(queries_ref, j, pl.multiple_of(core * rows, rows))
            q_ref[core * half + j] = mine
            q_ref[(1 - core) * half + j] = rows_of(q_recv_ref, j, 0)
        t_id = lax.broadcasted_iota(jnp.int32, (TILE, BLOCK), 0) % BLOCK
        causal = lax.broadcasted_iota(jnp.int32, (TILE, BLOCK), 1) <= t_id
        for b, r in tiles:
            width = (b + 1) * BLOCK
            s = scores(b, r, 0, width)
            since = start_of(b) - pair * 2 * tok
            diag = jnp.where(causal, s[:, b * BLOCK :], MASKED)
            s = jnp.concatenate([keep(s[:, : b * BLOCK], since), diag], 1) if b else diag
            top = jnp.max(s, axis=1, keepdims=True)
            p = jnp.exp2(s * factor - top * factor)
            top_ref[b, r] = jnp.broadcast_to(top, (TILE, HEAD_SIZE))
            acc_ref[b, r] = weigh(p, 0, width)

    def attend_next():
        top_ref[...] = top_in[...]
        acc_ref[...] = acc_in[...]

        @pl.loop(0, 2 * n_pieces)
        def _(step):
            i, first_block = step // 2, step % 2 * half
            behind = sum(
                jnp.where(i == n, jnp.where(col == 0, *d), 0) for n, d in enumerate(distances)
            )
            base = (pair - behind) * 2 * tok

            @pl.when(start_of(first_block) < base + 2 * tok)
            def _():
                for b, r in tiles[: len(tiles) // 2]:
                    b = first_block + b
                    update(i, base, b, r, top_ref, acc_ref, b)

    def attend_last(shard):
        first_block = shard * half
        base = (pair - jnp.where(col == 0, *distances[0])) * 2 * tok
        needed = start_of(first_block) < base + 2 * tok

        @pl.when(needed)
        def _():
            for b, r in tiles[: len(tiles) // 2]:
                update(0, base, first_block + b, r, top_in, acc_in, b)

        @pl.when(jnp.logical_not(needed))
        def _():
            acc_ref[...] = acc_in[pl.ds(first_block, half)]

        for j in range(half):
            o = (acc_ref[j, :, :HEAD_SIZE] / acc_ref[j, :, HEAD_SIZE:]).astype(jnp.bfloat16)
            for h in range(n_head):
                first = core * rows + h * HEAD_SIZE if stage == "own" else h * HEAD_SIZE
                lanes = pl.ds(pl.multiple_of(first, HEAD_SIZE), HEAD_SIZE)
                out_ref[j * BLOCK : (j + 1) * BLOCK, lanes] = o[h * BLOCK : (h + 1) * BLOCK]
        if stage == "own":
            out_ref[:, pl.ds(pl.multiple_of((1 - core) * rows, rows), rows)] = swapped_ref[...]

    if stage == "first":
        attend_own()
    elif stage == "next":
        attend_next()
    else:
        attend_last(core if stage == "own" else 1 - core)


def attention_call(stage, distances, starts, recv_starts, operands, after=()):
    tok, half = starts.shape[0] * BLOCK, starts.shape[0]
    rows = operands[1].shape[1]
    blocks, n_head, n_pieces = 2 * half, rows // BLOCK, len(distances)
    state = [
        jax.ShapeDtypeStruct((blocks, rows, HEAD_SIZE), jnp.float32),
        jax.ShapeDtypeStruct((blocks, rows, 2 * HEAD_SIZE), jnp.float32),
    ]
    scratch = [pltpu.VMEM((n_pieces, 2 * tok, 2 * HEAD_SIZE), jnp.bfloat16)]
    share = n_pieces
    if stage == "first":
        outs, share = [jax.ShapeDtypeStruct((blocks, rows, HEAD_SIZE), jnp.bfloat16)] + state, 0.6
    elif stage == "next":
        outs = state
    else:
        width = rows * (2 if stage == "own" else 1)
        outs, share = [jax.ShapeDtypeStruct((tok, width), jnp.bfloat16)], 0.5
        scratch = [pltpu.VMEM((half, rows, 2 * HEAD_SIZE), jnp.float32)] + scratch
    vmem, smem = pl.BlockSpec(memory_space=pltpu.VMEM), pl.BlockSpec(memory_space=pltpu.SMEM)
    return pl.pallas_call(
        functools.partial(attention_kernel, stage, distances, n_head, len(after)),
        out_shape=outs,
        in_specs=[smem, smem]
        + [vmem] * len(operands)
        + [pl.BlockSpec(memory_space=pl.ANY)] * len(after),
        out_specs=[vmem] * len(outs),
        scratch_shapes=scratch,
        compiler_params=pltpu.CompilerParams(vmem_limit_bytes=24 * 2**20),
        cost_estimate=pl.CostEstimate(
            flops=int(share * blocks * rows * 2 * tok * HEAD_SIZE * 8),
            bytes_accessed=8 * 2**20,
            transcendentals=int(share * blocks * rows * 2 * tok),
        ),
    )(starts, recv_starts, *operands, *after)


def per_device(queries, keys, values, block_start, out_weight):
    group = queries.shape[1] // 2
    me = lax.axis_index("ctx")
    core, col = me % 2, (me // 2) % 2
    head = lax.axis_index("head")

    def part(x, index, size):
        return lax.dynamic_slice_in_dim(x, index * size, size, 1)

    cols = out_weight.shape[1] // 2
    mine = jnp.concatenate([part(keys, core, HEAD_SIZE), part(values, core, HEAD_SIZE)], 1)
    theirs = jnp.concatenate([part(keys, 1 - core, HEAD_SIZE), part(values, 1 - core, HEAD_SIZE)], 1)
    own = (mine, swap(theirs, 1))
    q_recv = swap(part(queries, 1 - core, group), 1)
    recv_starts = swap(block_start, 1)
    one_behind = [shift(x, 4) for x in own]
    two_behind = [shift(x, 4) for x in one_behind]
    across = [swap(x, 2) for x in one_behind]
    third = [swap(jnp.where(col == 1, x, y), 2) for x, y in zip(two_behind, own, strict=True)]

    tiles = [cross(x, 0) for x in slice_weight(out_weight, one_behind[0])]
    tiles += [swap(x, 4) for x in tiles]

    starts = (block_start, recv_starts)
    q, *state = attention_call("first", ((0, 0),), *starts, (queries, q_recv, *own))
    state = attention_call("next", ((2, 2),), *starts, (q, *state, *one_behind))
    state = attention_call("next", ((1, 3), (4, 4)), *starts, (q, *state, *across, *two_behind))
    (o_other,) = attention_call("other", ((3, 1),), *starts, (q, *state, *third))
    (heads,) = attention_call("own", ((3, 1),), *starts, (q, *state, *third, swap(o_other, 1)))
    across = cross(heads, 0)
    here = jnp.dot(heads, part(out_weight, head, cols), preferred_element_type=jnp.float32)
    tiles += [swap(x, 1) for x in tiles]
    return project(here.astype(jnp.bfloat16), across, tiles)


def solution(mesh):
    in_specs = (P("ctx", "head"), P("ctx", "head"), P("ctx", "head"), P("ctx"), P("head", None))
    out_specs = P("ctx", "head")
    return jax.shard_map(
        per_device, mesh=mesh, in_specs=in_specs, out_specs=out_specs, check_vma=False
    )
```

```python
import functools

import jax
import jax.numpy as jnp
from jax import lax
from jax.experimental import pallas as pl
from jax.experimental.pallas import tpu as pltpu
from jax.sharding import PartitionSpec as P

HEAD_SIZE = 128
BLOCK = 128
LOG2E = 1.4426950408889634
MASKED = -1e30
TILE = 256


def rotate(x, distance):
    n = lax.axis_size("ctx")
    return lax.ppermute(x, "ctx", [(i, (i + distance) % n) for i in range(n)])


def swap(x, mask):
    return lax.ppermute(x, "ctx", [(i, i ^ mask) for i in range(lax.axis_size("ctx"))])


def cross(x, mask):
    n = lax.axis_size("ctx")
    route = [(2 * i + h, 2 * (i ^ mask) + 1 - h) for i in range(n) for h in range(2)]
    return lax.ppermute(x, ("ctx", "head"), route)


def slice_weight(weight_ref, common_ref, single_ref):
    core, part = lax.axis_index("ctx") % 2, lax.axis_index("ctx") // 4 % 2
    rows, width = single_ref.shape
    for out, tile in ((single_ref, 2 + part), (common_ref, 0)):
        col = pl.multiple_of(((1 - lax.axis_index("head")) * 4 + tile) * width, width)
        out[...] = weight_ref[pl.ds(pl.multiple_of(core * rows, rows), rows), pl.ds(col, out.shape[1])]


def join_kernel(first_ref, second_ref, _, out_ref):
    tok = first_ref.shape[0]
    out_ref[:tok] = first_ref[...]
    out_ref[tok:] = second_ref[...]


def join(first, second, after):
    vmem = pl.BlockSpec(memory_space=pltpu.VMEM)
    return pl.pallas_call(
        join_kernel,
        out_shape=jax.ShapeDtypeStruct((2 * first.shape[0], first.shape[1]), first.dtype),
        in_specs=[vmem, vmem, pl.BlockSpec(memory_space=pl.ANY)],
        out_specs=vmem,
        compiler_params=pltpu.CompilerParams(vmem_limit_bytes=4 * 2**20),
    )(first, second, after)


def project_kernel(given_ref, heads_ref, *refs):
    parts, out_ref, built, sems = refs[:6], refs[6], refs[7], refs[8]
    me = lax.axis_index("ctx")
    core, part = me % 2, me // 4 % 2
    group, width = parts[1].shape
    copies = []
    for n, first in enumerate((0, 1, 2 + part, 3 - part)):
        cols = pl.ds(pl.multiple_of(first * width, width), width)
        total = given_ref[:, cols].astype(jnp.float32)
        for index, (common, *single) in ((core, parts[:3]), (1 - core, parts[3:])):
            heads = heads_ref[:, pl.ds(pl.multiple_of(index * group, group), group)]
            tile = common[:, n * width : (n + 1) * width] if n < 2 else single[n - 2][...]
            total += jnp.dot(heads, tile, preferred_element_type=jnp.float32)
        built[n] = total.astype(out_ref.dtype)
        copies.append(pltpu.make_async_copy(built.at[n], out_ref.at[:, cols], sems.at[n]))
        copies[-1].start()
    for copy in copies:
        copy.wait()


def project(given, heads, tiles):
    tok, cols = given.shape
    vmem = pl.BlockSpec(memory_space=pltpu.VMEM)
    return pl.pallas_call(
        project_kernel,
        out_shape=jax.ShapeDtypeStruct(given.shape, jnp.bfloat16),
        in_specs=[vmem] * 8,
        out_specs=pl.BlockSpec(memory_space=pltpu.HBM),
        scratch_shapes=[pltpu.VMEM((4, tok, cols // 4), jnp.bfloat16), pltpu.SemaphoreType.DMA((4,))],
        compiler_params=pltpu.CompilerParams(vmem_limit_bytes=16 * 2**20),
        cost_estimate=pl.CostEstimate(
            flops=2 * tok * heads.shape[1] * cols, bytes_accessed=4 * 2**20, transcendentals=0
        ),
    )(given, heads, *tiles)


def attention_kernel(stage, distances, n_head, starts_ref, recv_starts_ref, *refs):
    refs = list(refs)
    me = lax.axis_index("ctx")
    pair, core, col = me // 2, me % 2, (me // 2) % 2
    if stage == "first":
        weight_ref, queries_ref, q_recv_ref = refs[:3]
        refs = refs[3:]
    else:
        q_ref, top_in, acc_in = refs[:3]
        refs = refs[3:]
    n_pieces = len(distances)
    pieces = refs[:n_pieces]
    refs = refs[n_pieces:]
    if stage == "first":
        q_ref, top_ref, acc_ref, common_ref, single_ref, held_ref = refs
    elif stage == "next":
        top_ref, acc_ref, held_ref = refs
    else:
        if stage == "own":
            swapped_ref, *refs = refs
        out_ref, acc_ref, held_ref = refs
    tok = starts_ref.shape[0] * BLOCK
    half = tok // BLOCK
    blocks = 2 * half
    rows = n_head * BLOCK
    factor = HEAD_SIZE**-0.5 * LOG2E
    tiles = [(b, slice(r, r + TILE)) for b in range(blocks) for r in range(0, rows, TILE)]

    for n, ref in enumerate(pieces):
        held_ref[n, pl.ds(pl.multiple_of(core * tok, tok), tok)] = ref[:tok]
        held_ref[n, pl.ds(pl.multiple_of((1 - core) * tok, tok), tok)] = ref[tok:]

    def start_of(b):
        mine = b // half == core
        return jnp.where(mine, starts_ref[b % half], recv_starts_ref[b % half])

    def rows_of(ref, j, lane0):
        t = slice(j * BLOCK, (j + 1) * BLOCK)
        return jnp.concatenate(
            [ref[t, pl.ds(lane0 + h * HEAD_SIZE, HEAD_SIZE)] for h in range(n_head)], axis=0
        )

    def scores(b, r, i, width):
        k = held_ref[i, :width, :HEAD_SIZE]
        return lax.dot_general(
            q_ref[b, r], k, (((1,), (1,)), ((), ())), preferred_element_type=jnp.float32
        )

    def weigh(p, i, width):
        v = held_ref[i, :width, HEAD_SIZE:]
        v = jnp.concatenate([v, jnp.ones_like(v)], axis=1)
        return jnp.dot(p.astype(jnp.bfloat16), v, preferred_element_type=jnp.float32)

    def keep(s, since):
        k_id = lax.broadcasted_iota(jnp.int32, (1, s.shape[1]), 1)
        return jnp.where(k_id >= since, s, MASKED)

    def update(i, base, b, r, top_from, acc_from, to):
        s = keep(scores(b, r, i, 2 * tok), start_of(b) - base)
        old = top_from[b, r][:, :1]
        top = jnp.maximum(old, jnp.max(s, axis=1, keepdims=True))
        p = jnp.exp2(s * factor - top * factor)
        if stage == "next":
            top_ref[to, r] = jnp.broadcast_to(top, (TILE, HEAD_SIZE))
        acc_ref[to, r] = acc_from[b, r] * jnp.exp2((old - top) * factor) + weigh(p, i, 2 * tok)

    def attend_own():
        for j in range(half):
            mine = rows_of(queries_ref, j, pl.multiple_of(core * rows, rows))
            q_ref[core * half + j] = mine
            q_ref[(1 - core) * half + j] = rows_of(q_recv_ref, j, 0)
        t_id = lax.broadcasted_iota(jnp.int32, (TILE, BLOCK), 0) % BLOCK
        causal = lax.broadcasted_iota(jnp.int32, (TILE, BLOCK), 1) <= t_id
        for b, r in tiles:
            width = (b + 1) * BLOCK
            s = scores(b, r, 0, width)
            since = start_of(b) - pair * 2 * tok
            diag = jnp.where(causal, s[:, b * BLOCK :], MASKED)
            s = jnp.concatenate([keep(s[:, : b * BLOCK], since), diag], 1) if b else diag
            top = jnp.max(s, axis=1, keepdims=True)
            p = jnp.exp2(s * factor - top * factor)
            top_ref[b, r] = jnp.broadcast_to(top, (TILE, HEAD_SIZE))
            acc_ref[b, r] = weigh(p, 0, width)

    def attend_next():
        top_ref[...] = top_in[...]
        acc_ref[...] = acc_in[...]

        @pl.loop(0, 2 * n_pieces)
        def _(step):
            i, first_block = step // 2, step % 2 * half
            behind = sum(
                jnp.where(i == n, jnp.where(col == 0, *d), 0) for n, d in enumerate(distances)
            )
            base = (pair - behind) * 2 * tok

            @pl.when(start_of(first_block) < base + 2 * tok)
            def _():
                for b, r in tiles[: len(tiles) // 2]:
                    b = first_block + b
                    update(i, base, b, r, top_ref, acc_ref, b)

    def attend_last(shard):
        first_block = shard * half
        base = (pair - jnp.where(col == 0, *distances[0])) * 2 * tok
        needed = start_of(first_block) < base + 2 * tok

        @pl.when(needed)
        def _():
            for b, r in tiles[: len(tiles) // 2]:
                update(0, base, first_block + b, r, top_in, acc_in, b)

        @pl.when(jnp.logical_not(needed))
        def _():
            acc_ref[...] = acc_in[pl.ds(first_block, half)]

        for j in range(half):
            o = (acc_ref[j, :, :HEAD_SIZE] / acc_ref[j, :, HEAD_SIZE:]).astype(jnp.bfloat16)
            for h in range(n_head):
                first = core * rows + h * HEAD_SIZE if stage == "own" else h * HEAD_SIZE
                lanes = pl.ds(pl.multiple_of(first, HEAD_SIZE), HEAD_SIZE)
                out_ref[j * BLOCK : (j + 1) * BLOCK, lanes] = o[h * BLOCK : (h + 1) * BLOCK]
        if stage == "own":
            out_ref[:, pl.ds(pl.multiple_of((1 - core) * rows, rows), rows)] = swapped_ref[...]

    if stage == "first":
        slice_weight(weight_ref, common_ref, single_ref)
        attend_own()
    elif stage == "next":
        attend_next()
    else:
        attend_last(core if stage == "own" else 1 - core)


def attention_call(stage, distances, starts, recv_starts, operands):
    tok, half = starts.shape[0] * BLOCK, starts.shape[0]
    rows = operands[2].shape[1] if stage == "first" else operands[1].shape[1]
    blocks, n_head, n_pieces = 2 * half, rows // BLOCK, len(distances)
    state = [
        jax.ShapeDtypeStruct((blocks, rows, HEAD_SIZE), jnp.float32),
        jax.ShapeDtypeStruct((blocks, rows, 2 * HEAD_SIZE), jnp.float32),
    ]
    scratch = [pltpu.VMEM((n_pieces, 2 * tok, 2 * HEAD_SIZE), jnp.bfloat16)]
    share = n_pieces
    if stage == "first":
        outs, share = [jax.ShapeDtypeStruct((blocks, rows, HEAD_SIZE), jnp.bfloat16)] + state, 0.6
        weight = operands[0]
        deep, wide = weight.shape[0] // 2, weight.shape[1] // 8
        outs += [jax.ShapeDtypeStruct((deep, n * wide), weight.dtype) for n in (2, 1)]
    elif stage == "next":
        outs = state
    else:
        width = rows * (2 if stage == "own" else 1)
        outs, share = [jax.ShapeDtypeStruct((tok, width), jnp.bfloat16)], 0.5
        scratch = [pltpu.VMEM((half, rows, 2 * HEAD_SIZE), jnp.float32)] + scratch
    vmem, smem = pl.BlockSpec(memory_space=pltpu.VMEM), pl.BlockSpec(memory_space=pltpu.SMEM)
    return pl.pallas_call(
        functools.partial(attention_kernel, stage, distances, n_head),
        out_shape=outs,
        in_specs=[smem, smem] + [vmem] * len(operands),
        out_specs=[vmem] * len(outs),
        scratch_shapes=scratch,
        compiler_params=pltpu.CompilerParams(vmem_limit_bytes=24 * 2**20),
        cost_estimate=pl.CostEstimate(
            flops=int(share * blocks * rows * 2 * tok * HEAD_SIZE * 8),
            bytes_accessed=8 * 2**20,
            transcendentals=int(share * blocks * rows * 2 * tok),
        ),
    )(starts, recv_starts, *operands)


def per_device(queries, keys, values, block_start, out_weight):
    group = queries.shape[1] // 2
    me = lax.axis_index("ctx")
    core, col = me % 2, (me // 2) % 2
    head = lax.axis_index("head")

    def part(x, index, size):
        return lax.dynamic_slice_in_dim(x, index * size, size, 1)

    cols = out_weight.shape[1] // 2
    mine = jnp.concatenate([part(keys, core, HEAD_SIZE), part(values, core, HEAD_SIZE)], 1)
    theirs = jnp.concatenate([part(keys, 1 - core, HEAD_SIZE), part(values, 1 - core, HEAD_SIZE)], 1)
    recv = swap(theirs, 1)
    one_behind = [rotate(mine, 4), rotate(recv, 4)]
    q_recv = swap(part(queries, 1 - core, group), 1)
    recv_starts = swap(block_start, 1)
    own = jnp.concatenate([mine, recv])
    starts = (block_start, recv_starts)
    q, *state, common, single = attention_call(
        "first", ((0, 0),), *starts, (out_weight, queries, q_recv, own)
    )
    single, common = cross(single, 0), cross(common, 0)
    weights = [common, single, swap(single, 4)]
    one_behind = join(*one_behind, q)
    two_behind = rotate(one_behind, 4)
    across = swap(one_behind, 2)
    third = swap(jnp.where(col == 1, two_behind, own), 2)
    state = attention_call("next", ((2, 2),), *starts, (q, *state, one_behind))
    state = attention_call("next", ((1, 3), (4, 4)), *starts, (q, *state, across, two_behind))
    (o_other,) = attention_call("other", ((3, 1),), *starts, (q, *state, third))
    (heads,) = attention_call("own", ((3, 1),), *starts, (q, *state, third, swap(o_other, 1)))
    heads_across = cross(heads, 0)
    here = jnp.dot(heads, part(out_weight, head, cols), preferred_element_type=jnp.float32)
    weights += [swap(x, 1) for x in weights]
    return project(here.astype(jnp.bfloat16), heads_across, weights)


def solution(mesh):
    in_specs = (P("ctx", "head"), P("ctx", "head"), P("ctx", "head"), P("ctx"), P("head", None))
    out_specs = P("ctx", "head")
    return jax.shard_map(
        per_device, mesh=mesh, in_specs=in_specs, out_specs=out_specs, check_vma=False
    )
```

```python
import functools

import jax
import jax.numpy as jnp
from jax import lax
from jax.experimental import pallas as pl
from jax.experimental.pallas import tpu as pltpu
from jax.sharding import PartitionSpec as P

HEAD_SIZE = 128
BLOCK = 128
LOG2E = 1.4426950408889634
MASKED = -1e30
TILE = 256


def rotate(x, distance):
    n = lax.axis_size("ctx")
    return lax.ppermute(x, "ctx", [(i, (i + distance) % n) for i in range(n)])


def swap(x, mask):
    return lax.ppermute(x, "ctx", [(i, i ^ mask) for i in range(lax.axis_size("ctx"))])


def cross(x, mask):
    n = lax.axis_size("ctx")
    route = [(2 * i + h, 2 * (i ^ mask) + 1 - h) for i in range(n) for h in range(2)]
    return lax.ppermute(x, ("ctx", "head"), route)


def project_kernel(given_ref, heads_ref, *refs):
    parts, out_ref, built, sems = refs[:4], refs[4], refs[5], refs[6]
    me = lax.axis_index("ctx")
    core, part = me % 2, me // 4 % 2
    group, width = parts[1].shape
    copies = []
    for n, first in enumerate((part, part + 1, part + 2, 3 - 3 * part)):
        cols = pl.ds(pl.multiple_of(first * width, width), width)
        total = given_ref[:, cols].astype(jnp.float32)
        for index, (fetched, single) in ((core, parts[:2]), (1 - core, parts[2:])):
            heads = heads_ref[:, pl.ds(pl.multiple_of(index * group, group), group)]
            tile = fetched[:, n * width : (n + 1) * width] if n < 3 else single[...]
            total += jnp.dot(heads, tile, preferred_element_type=jnp.float32)
        built[n] = total.astype(out_ref.dtype)
        copies.append(pltpu.make_async_copy(built.at[n], out_ref.at[:, cols], sems.at[n]))
        copies[-1].start()
    for copy in copies:
        copy.wait()


def project(given, heads, tiles):
    tok, cols = given.shape
    vmem = pl.BlockSpec(memory_space=pltpu.VMEM)
    return pl.pallas_call(
        project_kernel,
        out_shape=jax.ShapeDtypeStruct(given.shape, jnp.bfloat16),
        in_specs=[vmem] * 6,
        out_specs=pl.BlockSpec(memory_space=pltpu.HBM),
        scratch_shapes=[pltpu.VMEM((4, tok, cols // 4), jnp.bfloat16), pltpu.SemaphoreType.DMA((4,))],
        compiler_params=pltpu.CompilerParams(vmem_limit_bytes=16 * 2**20),
        cost_estimate=pl.CostEstimate(
            flops=2 * tok * heads.shape[1] * cols, bytes_accessed=4 * 2**20, transcendentals=0
        ),
    )(given, heads, *tiles)


def attention_kernel(stage, distances, n_head, starts_ref, recv_starts_ref, *refs):
    refs = list(refs)
    me = lax.axis_index("ctx")
    pair, core, col = me // 2, me % 2, (me // 2) % 2
    if stage == "first":
        queries_ref, q_recv_ref = refs[:2]
        refs = refs[2:]
    else:
        q_ref, top_in, acc_in = refs[:3]
        refs = refs[3:]
    n_pieces = len(distances)
    pieces = refs[:n_pieces]
    refs = refs[n_pieces:]
    if stage == "first":
        q_ref, top_ref, acc_ref, held_ref = refs
    elif stage == "next":
        top_ref, acc_ref, held_ref = refs
    else:
        if stage == "own":
            swapped_ref, *refs = refs
        out_ref, acc_ref, held_ref = refs
    tok = starts_ref.shape[0] * BLOCK
    half = tok // BLOCK
    blocks = 2 * half
    rows = n_head * BLOCK
    factor = HEAD_SIZE**-0.5 * LOG2E
    tiles = [(b, slice(r, r + TILE)) for b in range(blocks) for r in range(0, rows, TILE)]

    for n, ref in enumerate(pieces):
        held_ref[n, pl.ds(pl.multiple_of(core * tok, tok), tok)] = ref[:tok]
        held_ref[n, pl.ds(pl.multiple_of((1 - core) * tok, tok), tok)] = ref[tok:]

    def start_of(b):
        mine = b // half == core
        return jnp.where(mine, starts_ref[b % half], recv_starts_ref[b % half])

    def rows_of(ref, j, lane0):
        t = slice(j * BLOCK, (j + 1) * BLOCK)
        return jnp.concatenate(
            [ref[t, pl.ds(lane0 + h * HEAD_SIZE, HEAD_SIZE)] for h in range(n_head)], axis=0
        )

    def scores(b, r, i, width):
        k = held_ref[i, :width, :HEAD_SIZE]
        return lax.dot_general(
            q_ref[b, r], k, (((1,), (1,)), ((), ())), preferred_element_type=jnp.float32
        )

    def weigh(p, i, width):
        v = held_ref[i, :width, HEAD_SIZE:]
        v = jnp.concatenate([v, jnp.ones_like(v)], axis=1)
        return jnp.dot(p.astype(jnp.bfloat16), v, preferred_element_type=jnp.float32)

    def keep(s, since):
        k_id = lax.broadcasted_iota(jnp.int32, (1, s.shape[1]), 1)
        return jnp.where(k_id >= since, s, MASKED)

    def update(i, base, b, r, top_from, acc_from, to):
        s = keep(scores(b, r, i, 2 * tok), start_of(b) - base)
        old = top_from[b, r][:, :1]
        top = jnp.maximum(old, jnp.max(s, axis=1, keepdims=True))
        p = jnp.exp2(s * factor - top * factor)
        if stage == "next":
            top_ref[to, r] = jnp.broadcast_to(top, (TILE, HEAD_SIZE))
        acc_ref[to, r] = acc_from[b, r] * jnp.exp2((old - top) * factor) + weigh(p, i, 2 * tok)

    def attend_own():
        for j in range(half):
            mine = rows_of(queries_ref, j, pl.multiple_of(core * rows, rows))
            q_ref[core * half + j] = mine
            q_ref[(1 - core) * half + j] = rows_of(q_recv_ref, j, 0)
        t_id = lax.broadcasted_iota(jnp.int32, (TILE, BLOCK), 0) % BLOCK
        causal = lax.broadcasted_iota(jnp.int32, (TILE, BLOCK), 1) <= t_id
        for b, r in tiles:
            width = (b + 1) * BLOCK
            s = scores(b, r, 0, width)
            since = start_of(b) - pair * 2 * tok
            diag = jnp.where(causal, s[:, b * BLOCK :], MASKED)
            s = jnp.concatenate([keep(s[:, : b * BLOCK], since), diag], 1) if b else diag
            top = jnp.max(s, axis=1, keepdims=True)
            p = jnp.exp2(s * factor - top * factor)
            top_ref[b, r] = jnp.broadcast_to(top, (TILE, HEAD_SIZE))
            acc_ref[b, r] = weigh(p, 0, width)

    def attend_next():
        top_ref[...] = top_in[...]
        acc_ref[...] = acc_in[...]

        @pl.loop(0, 2 * n_pieces)
        def _(step):
            i, first_block = step // 2, step % 2 * half
            behind = sum(
                jnp.where(i == n, jnp.where(col == 0, *d), 0) for n, d in enumerate(distances)
            )
            base = (pair - behind) * 2 * tok

            @pl.when(start_of(first_block) < base + 2 * tok)
            def _():
                for b, r in tiles[: len(tiles) // 2]:
                    b = first_block + b
                    update(i, base, b, r, top_ref, acc_ref, b)

    def attend_last(shard):
        first_block = shard * half
        base = (pair - jnp.where(col == 0, *distances[0])) * 2 * tok
        needed = start_of(first_block) < base + 2 * tok

        @pl.when(needed)
        def _():
            for b, r in tiles[: len(tiles) // 2]:
                update(0, base, first_block + b, r, top_in, acc_in, b)

        @pl.when(jnp.logical_not(needed))
        def _():
            acc_ref[...] = acc_in[pl.ds(first_block, half)]

        for j in range(half):
            o = (acc_ref[j, :, :HEAD_SIZE] / acc_ref[j, :, HEAD_SIZE:]).astype(jnp.bfloat16)
            for h in range(n_head):
                first = core * rows + h * HEAD_SIZE if stage == "own" else h * HEAD_SIZE
                lanes = pl.ds(pl.multiple_of(first, HEAD_SIZE), HEAD_SIZE)
                out_ref[j * BLOCK : (j + 1) * BLOCK, lanes] = o[h * BLOCK : (h + 1) * BLOCK]
        if stage == "own":
            out_ref[:, pl.ds(pl.multiple_of((1 - core) * rows, rows), rows)] = swapped_ref[...]

    if stage == "first":
        attend_own()
    elif stage == "next":
        attend_next()
    else:
        attend_last(core if stage == "own" else 1 - core)


def attention_call(stage, distances, starts, recv_starts, operands):
    tok, half = starts.shape[0] * BLOCK, starts.shape[0]
    rows = operands[1].shape[1]
    blocks, n_head, n_pieces = 2 * half, rows // BLOCK, len(distances)
    state = [
        jax.ShapeDtypeStruct((blocks, rows, HEAD_SIZE), jnp.float32),
        jax.ShapeDtypeStruct((blocks, rows, 2 * HEAD_SIZE), jnp.float32),
    ]
    scratch = [pltpu.VMEM((n_pieces, 2 * tok, 2 * HEAD_SIZE), jnp.bfloat16)]
    share = n_pieces
    if stage == "first":
        outs, share = [jax.ShapeDtypeStruct((blocks, rows, HEAD_SIZE), jnp.bfloat16)] + state, 0.6
    elif stage == "next":
        outs = state
    else:
        width = rows * (2 if stage == "own" else 1)
        outs, share = [jax.ShapeDtypeStruct((tok, width), jnp.bfloat16)], 0.5
        scratch = [pltpu.VMEM((half, rows, 2 * HEAD_SIZE), jnp.float32)] + scratch
    vmem, smem = pl.BlockSpec(memory_space=pltpu.VMEM), pl.BlockSpec(memory_space=pltpu.SMEM)
    return pl.pallas_call(
        functools.partial(attention_kernel, stage, distances, n_head),
        out_shape=outs,
        in_specs=[smem, smem] + [vmem] * len(operands),
        out_specs=[vmem] * len(outs),
        scratch_shapes=scratch,
        compiler_params=pltpu.CompilerParams(vmem_limit_bytes=24 * 2**20),
        cost_estimate=pl.CostEstimate(
            flops=int(share * blocks * rows * 2 * tok * HEAD_SIZE * 8),
            bytes_accessed=8 * 2**20,
            transcendentals=int(share * blocks * rows * 2 * tok),
        ),
    )(starts, recv_starts, *operands)


def per_device(queries, keys, values, block_start, out_weight):
    group = queries.shape[1] // 2
    me = lax.axis_index("ctx")
    core, col = me % 2, (me // 2) % 2
    head = lax.axis_index("head")

    def part(x, index, size):
        return lax.dynamic_slice_in_dim(x, index * size, size, 1)

    cols = out_weight.shape[1] // 2
    mine = jnp.concatenate([part(keys, core, HEAD_SIZE), part(values, core, HEAD_SIZE)], 1)
    theirs = jnp.concatenate([part(keys, 1 - core, HEAD_SIZE), part(values, 1 - core, HEAD_SIZE)], 1)
    recv = swap(theirs, 1)
    one_behind = [rotate(mine, 4), rotate(recv, 4)]
    q_recv = swap(part(queries, 1 - core, group), 1)
    recv_starts = swap(block_start, 1)
    own = jnp.concatenate([mine, recv])
    starts = (block_start, recv_starts)
    tile = cols // 4
    part_id = me // 4 % 2
    q_recv, weight = lax.optimization_barrier((q_recv, out_weight))
    first_col = ((1 - head) * 4 + part_id) * tile
    sent = lax.dynamic_slice(weight, (core * group, first_col), (group, 3 * tile))
    q_recv, sent = lax.optimization_barrier((q_recv, sent))
    fetched = cross(sent, 0)
    q, *state = attention_call("first", ((0, 0),), *starts, (queries, q_recv, own))
    q, one_behind = lax.optimization_barrier((q, one_behind))
    one_behind = jnp.concatenate(one_behind)
    two_behind = rotate(one_behind, 4)
    across = swap(one_behind, 2)
    third = swap(jnp.where(col == 1, two_behind, own), 2)
    state = attention_call("next", ((2, 2),), *starts, (q, *state, one_behind))
    state = attention_call("next", ((1, 3), (4, 4)), *starts, (q, *state, across, two_behind))
    state, fetched = lax.optimization_barrier((state, fetched))
    weights = [fetched, swap(lax.dynamic_slice_in_dim(fetched, 2 * tile * part_id, tile, 1), 4)]
    (o_other,) = attention_call("other", ((3, 1),), *starts, (q, *state, third))
    (heads,) = attention_call("own", ((3, 1),), *starts, (q, *state, third, swap(o_other, 1)))
    heads_across = cross(heads, 0)
    other_weights = [swap(x, 1) for x in weights]
    here = jnp.dot(heads, part(out_weight, head, cols), preferred_element_type=jnp.float32)
    return project(here.astype(jnp.bfloat16), heads_across, (*weights, *other_weights))


def solution(mesh):
    in_specs = (P("ctx", "head"), P("ctx", "head"), P("ctx", "head"), P("ctx"), P("head", None))
    out_specs = P("ctx", "head")
    return jax.shard_map(
        per_device, mesh=mesh, in_specs=in_specs, out_specs=out_specs, check_vma=False
    )
```

```python
import functools

import jax
import jax.numpy as jnp
from jax import lax
from jax.experimental import pallas as pl
from jax.experimental.pallas import tpu as pltpu
from jax.sharding import PartitionSpec as P

HEAD_SIZE = 128
BLOCK = 128
LOG2E = 1.4426950408889634
MASKED = -1e30
TILE = 256


def rotate(x, distance):
    n = lax.axis_size("ctx")
    return lax.ppermute(x, "ctx", [(i, (i + distance) % n) for i in range(n)])


def swap(x, mask):
    return lax.ppermute(x, "ctx", [(i, i ^ mask) for i in range(lax.axis_size("ctx"))])


def cross(x, mask):
    n = lax.axis_size("ctx")
    route = [(2 * i + h, 2 * (i ^ mask) + 1 - h) for i in range(n) for h in range(2)]
    return lax.ppermute(x, ("ctx", "head"), route)


def join_kernel(first_ref, second_ref, out_ref):
    tok = first_ref.shape[0]
    out_ref[:tok] = first_ref[...]
    out_ref[tok:] = second_ref[...]


def join(first, second):
    vmem = pl.BlockSpec(memory_space=pltpu.VMEM)
    return pl.pallas_call(
        join_kernel,
        out_shape=jax.ShapeDtypeStruct((2 * first.shape[0], first.shape[1]), first.dtype),
        in_specs=[vmem, vmem],
        out_specs=vmem,
        compiler_params=pltpu.CompilerParams(vmem_limit_bytes=4 * 2**20),
    )(first, second)


def project_kernel(given_ref, heads_ref, *refs):
    parts, out_ref, built, sems = refs[:4], refs[4], refs[5], refs[6]
    me = lax.axis_index("ctx")
    core, part = me % 2, me // 4 % 2
    group, width = parts[1].shape
    copies = []
    for n, first in enumerate((part, part + 1, part + 2, 3 - 3 * part)):
        cols = pl.ds(pl.multiple_of(first * width, width), width)
        total = given_ref[:, cols].astype(jnp.float32)
        for index, (fetched, single) in ((core, parts[:2]), (1 - core, parts[2:])):
            heads = heads_ref[:, pl.ds(pl.multiple_of(index * group, group), group)]
            tile = fetched[:, n * width : (n + 1) * width] if n < 3 else single[...]
            total += jnp.dot(heads, tile, preferred_element_type=jnp.float32)
        built[n] = total.astype(out_ref.dtype)
        copies.append(pltpu.make_async_copy(built.at[n], out_ref.at[:, cols], sems.at[n]))
        copies[-1].start()
    for copy in copies:
        copy.wait()


def project(given, heads, tiles):
    tok, cols = given.shape
    vmem = pl.BlockSpec(memory_space=pltpu.VMEM)
    return pl.pallas_call(
        project_kernel,
        out_shape=jax.ShapeDtypeStruct(given.shape, jnp.bfloat16),
        in_specs=[vmem] * 6,
        out_specs=pl.BlockSpec(memory_space=pltpu.HBM),
        scratch_shapes=[pltpu.VMEM((4, tok, cols // 4), jnp.bfloat16), pltpu.SemaphoreType.DMA((4,))],
        compiler_params=pltpu.CompilerParams(vmem_limit_bytes=16 * 2**20),
        cost_estimate=pl.CostEstimate(
            flops=2 * tok * heads.shape[1] * cols, bytes_accessed=4 * 2**20, transcendentals=0
        ),
    )(given, heads, *tiles)


def attention_kernel(stage, distances, n_head, starts_ref, recv_starts_ref, *refs):
    refs = list(refs)
    me = lax.axis_index("ctx")
    pair, core, col = me // 2, me % 2, (me // 2) % 2
    if stage == "first":
        queries_ref, q_recv_ref = refs[:2]
        refs = refs[2:]
    else:
        q_ref, stats_in, acc_in = refs[:3]
        refs = refs[3:]
    n_pieces = len(distances)
    pieces = refs[:n_pieces]
    refs = refs[n_pieces:]
    if stage == "first":
        q_ref, stats_ref, acc_ref, held_ref = refs
    elif stage == "next":
        stats_ref, acc_ref, held_ref = refs
    else:
        if stage == "own":
            swapped_ref, *refs = refs
        out_ref, stats_ref, acc_ref, held_ref = refs
    tok = starts_ref.shape[0] * BLOCK
    half = tok // BLOCK
    blocks = 2 * half
    rows = n_head * BLOCK
    factor = HEAD_SIZE**-0.5 * LOG2E
    tiles = [(b, slice(r, r + TILE)) for b in range(blocks) for r in range(0, rows, TILE)]

    for n, ref in enumerate(pieces):
        held_ref[n, pl.ds(pl.multiple_of(core * tok, tok), tok)] = ref[:tok]
        held_ref[n, pl.ds(pl.multiple_of((1 - core) * tok, tok), tok)] = ref[tok:]

    def start_of(b):
        mine = b // half == core
        return jnp.where(mine, starts_ref[b % half], recv_starts_ref[b % half])

    def rows_of(ref, j, lane0):
        t = slice(j * BLOCK, (j + 1) * BLOCK)
        return jnp.concatenate(
            [ref[t, pl.ds(lane0 + h * HEAD_SIZE, HEAD_SIZE)] for h in range(n_head)], axis=0
        )

    def scores(b, r, i, width):
        k = held_ref[i, :width, :HEAD_SIZE]
        return lax.dot_general(
            q_ref[b, r], k, (((1,), (1,)), ((), ())), preferred_element_type=jnp.float32
        )

    def weigh(p, i, width):
        v = held_ref[i, :width, HEAD_SIZE:]
        v = jnp.concatenate([v, jnp.ones_like(v)], axis=1)
        return jnp.dot(p.astype(jnp.bfloat16), v, preferred_element_type=jnp.float32)

    def keep(s, since):
        k_id = lax.broadcasted_iota(jnp.int32, (1, s.shape[1]), 1)
        return jnp.where(k_id >= since, s, MASKED)

    def both(top, total):
        lane = lax.broadcasted_iota(jnp.int32, total.shape, 1)
        return jnp.where(lane < HEAD_SIZE // 2, top, total)

    def update(i, base, b, r, stats_from, acc_from, to):
        s = keep(scores(b, r, i, 2 * tok), start_of(b) - base)
        stats = stats_from[b, r]
        old = stats[:, :1]
        top = jnp.maximum(old, jnp.max(s, axis=1, keepdims=True))
        p = jnp.exp2(s * factor - top * factor)
        decay = jnp.exp2((old - top) * factor)
        added = weigh(p, i, 2 * tok)
        stats_ref[to, r] = both(top, stats * decay + added[:, HEAD_SIZE:])
        acc_ref[to, r] = acc_from[b, r] * decay + added[:, :HEAD_SIZE]

    def attend_own():
        for j in range(half):
            mine = rows_of(queries_ref, j, pl.multiple_of(core * rows, rows))
            q_ref[core * half + j] = mine
            q_ref[(1 - core) * half + j] = rows_of(q_recv_ref, j, 0)
        t_id = lax.broadcasted_iota(jnp.int32, (TILE, BLOCK), 0) % BLOCK
        causal = lax.broadcasted_iota(jnp.int32, (TILE, BLOCK), 1) <= t_id
        for b, r in tiles:
            width = (b + 1) * BLOCK
            s = scores(b, r, 0, width)
            since = start_of(b) - pair * 2 * tok
            diag = jnp.where(causal, s[:, b * BLOCK :], MASKED)
            s = jnp.concatenate([keep(s[:, : b * BLOCK], since), diag], 1) if b else diag
            top = jnp.max(s, axis=1, keepdims=True)
            p = jnp.exp2(s * factor - top * factor)
            added = weigh(p, 0, width)
            stats_ref[b, r] = both(top, added[:, HEAD_SIZE:])
            acc_ref[b, r] = added[:, :HEAD_SIZE]

    def attend_next():
        stats_ref[...] = stats_in[...]
        acc_ref[...] = acc_in[...]

        @pl.loop(0, 2 * n_pieces)
        def _(step):
            i, first_block = step // 2, step % 2 * half
            behind = sum(
                jnp.where(i == n, jnp.where(col == 0, *d), 0) for n, d in enumerate(distances)
            )
            base = (pair - behind) * 2 * tok

            @pl.when(start_of(first_block) < base + 2 * tok)
            def _():
                for b, r in tiles[: len(tiles) // 2]:
                    b = first_block + b
                    update(i, base, b, r, stats_ref, acc_ref, b)

    def attend_last(shard):
        first_block = shard * half
        base = (pair - jnp.where(col == 0, *distances[0])) * 2 * tok
        needed = start_of(first_block) < base + 2 * tok

        @pl.when(needed)
        def _():
            for b, r in tiles[: len(tiles) // 2]:
                update(0, base, first_block + b, r, stats_in, acc_in, b)

        @pl.when(jnp.logical_not(needed))
        def _():
            stats_ref[...] = stats_in[pl.ds(first_block, half)]
            acc_ref[...] = acc_in[pl.ds(first_block, half)]

        for j in range(half):
            total = stats_ref[j, :, HEAD_SIZE // 2 : HEAD_SIZE // 2 + 1]
            o = (acc_ref[j] / total).astype(jnp.bfloat16)
            for h in range(n_head):
                first = core * rows + h * HEAD_SIZE if stage == "own" else h * HEAD_SIZE
                lanes = pl.ds(pl.multiple_of(first, HEAD_SIZE), HEAD_SIZE)
                out_ref[j * BLOCK : (j + 1) * BLOCK, lanes] = o[h * BLOCK : (h + 1) * BLOCK]
        if stage == "own":
            out_ref[:, pl.ds(pl.multiple_of((1 - core) * rows, rows), rows)] = swapped_ref[...]

    if stage == "first":
        attend_own()
    elif stage == "next":
        attend_next()
    else:
        attend_last(core if stage == "own" else 1 - core)


def attention_call(stage, distances, starts, recv_starts, operands):
    tok, half = starts.shape[0] * BLOCK, starts.shape[0]
    rows = operands[1].shape[1]
    blocks, n_head, n_pieces = 2 * half, rows // BLOCK, len(distances)
    state = [jax.ShapeDtypeStruct((blocks, rows, HEAD_SIZE), jnp.float32)] * 2
    scratch = [pltpu.VMEM((n_pieces, 2 * tok, 2 * HEAD_SIZE), jnp.bfloat16)]
    share = n_pieces
    if stage == "first":
        outs, share = [jax.ShapeDtypeStruct((blocks, rows, HEAD_SIZE), jnp.bfloat16)] + state, 0.6
    elif stage == "next":
        outs = state
    else:
        width = rows * (2 if stage == "own" else 1)
        outs, share = [jax.ShapeDtypeStruct((tok, width), jnp.bfloat16)], 0.5
        scratch = [pltpu.VMEM((half, rows, HEAD_SIZE), jnp.float32)] * 2 + scratch
    vmem, smem = pl.BlockSpec(memory_space=pltpu.VMEM), pl.BlockSpec(memory_space=pltpu.SMEM)
    return pl.pallas_call(
        functools.partial(attention_kernel, stage, distances, n_head),
        out_shape=outs,
        in_specs=[smem, smem] + [vmem] * len(operands),
        out_specs=[vmem] * len(outs),
        scratch_shapes=scratch,
        compiler_params=pltpu.CompilerParams(vmem_limit_bytes=24 * 2**20),
        cost_estimate=pl.CostEstimate(
            flops=int(share * blocks * rows * 2 * tok * HEAD_SIZE * 8),
            bytes_accessed=8 * 2**20,
            transcendentals=int(share * blocks * rows * 2 * tok),
        ),
    )(starts, recv_starts, *operands)


def per_device(queries, keys, values, block_start, out_weight):
    group = queries.shape[1] // 2
    me = lax.axis_index("ctx")
    core, col = me % 2, (me // 2) % 2
    head = lax.axis_index("head")

    def part(x, index, size):
        return lax.dynamic_slice_in_dim(x, index * size, size, 1)

    cols = out_weight.shape[1] // 2
    mine = jnp.concatenate([part(keys, core, HEAD_SIZE), part(values, core, HEAD_SIZE)], 1)
    theirs = jnp.concatenate([part(keys, 1 - core, HEAD_SIZE), part(values, 1 - core, HEAD_SIZE)], 1)
    recv = swap(theirs, 1)
    one_behind = [rotate(mine, 4), rotate(recv, 4)]
    q_recv = swap(part(queries, 1 - core, group), 1)
    recv_starts = swap(block_start, 1)
    own = jnp.concatenate([mine, recv])
    starts = (block_start, recv_starts)
    tile, quarter = cols // 4, me // 4 % 2
    q_recv, weight = lax.optimization_barrier((q_recv, out_weight))
    first_col = ((1 - head) * 4 + quarter) * tile
    sent = lax.dynamic_slice(weight, (core * group, first_col), (group, 3 * tile))
    q_recv, sent = lax.optimization_barrier((q_recv, sent))
    fetched = cross(sent, 0)
    q, *state = attention_call("first", ((0, 0),), *starts, (queries, q_recv, own))
    q, one_behind = lax.optimization_barrier((q, one_behind))
    one_behind = join(*one_behind)
    two_behind = rotate(one_behind, 4)
    across = swap(one_behind, 2)
    third = swap(jnp.where(col == 1, two_behind, own), 2)
    state = attention_call("next", ((2, 2),), *starts, (q, *state, one_behind))
    state = attention_call("next", ((1, 3), (4, 4)), *starts, (q, *state, across, two_behind))
    (o_other,) = attention_call("other", ((3, 1),), *starts, (q, *state, third))
    _, fetched = lax.optimization_barrier((o_other, fetched))
    weights = [fetched, swap(lax.dynamic_slice_in_dim(fetched, 2 * tile * quarter, tile, 1), 4)]
    (heads,) = attention_call("own", ((3, 1),), *starts, (q, *state, third, swap(o_other, 1)))
    heads_across = cross(heads, 0)
    here = jnp.dot(heads, part(out_weight, head, cols), preferred_element_type=jnp.float32)
    weights += [swap(x, 1) for x in weights]
    return project(here.astype(jnp.bfloat16), heads_across, weights)


def solution(mesh):
    in_specs = (P("ctx", "head"), P("ctx", "head"), P("ctx", "head"), P("ctx"), P("head", None))
    out_specs = P("ctx", "head")
    return jax.shard_map(
        per_device, mesh=mesh, in_specs=in_specs, out_specs=out_specs, check_vma=False
    )
```

```python
import functools

import jax
import jax.numpy as jnp
from jax import lax
from jax.experimental import pallas as pl
from jax.experimental.pallas import tpu as pltpu
from jax.sharding import PartitionSpec as P

HEAD_SIZE = 128
BLOCK = 128
LOG2E = 1.4426950408889634
MASKED = -1e30
TILE = 256


def rotate(x, distance):
    n = lax.axis_size("ctx")
    return lax.ppermute(x, "ctx", [(i, (i + distance) % n) for i in range(n)])


def swap(x, mask):
    return lax.ppermute(x, "ctx", [(i, i ^ mask) for i in range(lax.axis_size("ctx"))])


def cross(x, mask):
    n = lax.axis_size("ctx")
    route = [(2 * i + h, 2 * (i ^ mask) + 1 - h) for i in range(n) for h in range(2)]
    return lax.ppermute(x, ("ctx", "head"), route)


def small_call(kernel, shapes, operands):
    vmem = pl.BlockSpec(memory_space=pltpu.VMEM)
    return pl.pallas_call(
        kernel,
        out_shape=[jax.ShapeDtypeStruct(shape, operands[0].dtype) for shape in shapes],
        in_specs=[vmem] * len(operands),
        out_specs=[vmem] * len(shapes),
        compiler_params=pltpu.CompilerParams(vmem_limit_bytes=6 * 2**20),
        cost_estimate=pl.CostEstimate(flops=2**20, bytes_accessed=2**20, transcendentals=0),
    )(*operands)


def prepare_kernel(keys_ref, values_ref, queries_ref, mine_ref, theirs_ref, queries_out):
    core = lax.axis_index("ctx") % 2
    for out, index in ((mine_ref, core), (theirs_ref, 1 - core)):
        lanes = pl.ds(pl.multiple_of(index * HEAD_SIZE, HEAD_SIZE), HEAD_SIZE)
        out[:, :HEAD_SIZE] = keys_ref[:, lanes]
        out[:, HEAD_SIZE:] = values_ref[:, lanes]
    group = queries_out.shape[1]
    queries_out[...] = queries_ref[:, pl.ds(pl.multiple_of((1 - core) * group, group), group)]


def join_kernel(first_ref, second_ref, out_ref):
    tok = first_ref.shape[0]
    out_ref[:tok] = first_ref[...]
    out_ref[tok:] = second_ref[...]


def pick_kernel(even_ref, odd_ref, out_ref):
    odd = lax.axis_index("ctx") // 2 % 2 == 1

    @pl.when(odd)
    def _():
        out_ref[...] = odd_ref[...]

    @pl.when(jnp.logical_not(odd))
    def _():
        out_ref[...] = even_ref[...]


def project_kernel(given_ref, heads_ref, *refs):
    parts, out_ref, built, sems = refs[:4], refs[4], refs[5], refs[6]
    me = lax.axis_index("ctx")
    core, part = me % 2, me // 4 % 2
    group, width = parts[1].shape
    copies = []
    for n, first in enumerate((part, part + 1, part + 2, 3 - 3 * part)):
        cols = pl.ds(pl.multiple_of(first * width, width), width)
        total = given_ref[:, cols].astype(jnp.float32)
        for index, (fetched, single) in ((core, parts[:2]), (1 - core, parts[2:])):
            heads = heads_ref[:, pl.ds(pl.multiple_of(index * group, group), group)]
            tile = fetched[:, n * width : (n + 1) * width] if n < 3 else single[...]
            total += jnp.dot(heads, tile, preferred_element_type=jnp.float32)
        built[n] = total.astype(out_ref.dtype)
        copies.append(pltpu.make_async_copy(built.at[n], out_ref.at[:, cols], sems.at[n]))
        copies[-1].start()
    for copy in copies:
        copy.wait()


def project(given, heads, tiles):
    tok, cols = given.shape
    vmem = pl.BlockSpec(memory_space=pltpu.VMEM)
    return pl.pallas_call(
        project_kernel,
        out_shape=jax.ShapeDtypeStruct(given.shape, jnp.bfloat16),
        in_specs=[vmem] * 6,
        out_specs=pl.BlockSpec(memory_space=pltpu.HBM),
        scratch_shapes=[pltpu.VMEM((4, tok, cols // 4), jnp.bfloat16), pltpu.SemaphoreType.DMA((4,))],
        compiler_params=pltpu.CompilerParams(vmem_limit_bytes=16 * 2**20),
        cost_estimate=pl.CostEstimate(
            flops=2 * tok * heads.shape[1] * cols, bytes_accessed=4 * 2**20, transcendentals=0
        ),
    )(given, heads, *tiles)


def attention_kernel(stage, distances, n_head, starts_ref, recv_starts_ref, *refs):
    refs = list(refs)
    me = lax.axis_index("ctx")
    pair, core, col = me // 2, me % 2, (me // 2) % 2
    if stage == "first":
        queries_ref, q_recv_ref = refs[:2]
        refs = refs[2:]
    else:
        q_ref, stats_in, acc_in = refs[:3]
        refs = refs[3:]
    n_pieces = len(distances)
    pieces = refs[:n_pieces]
    refs = refs[n_pieces:]
    if stage == "first":
        q_ref, stats_ref, acc_ref, held_ref = refs
    elif stage == "next":
        stats_ref, acc_ref, held_ref = refs
    else:
        if stage == "own":
            swapped_ref, *refs = refs
        out_ref, stats_ref, acc_ref, held_ref = refs
    tok = starts_ref.shape[0] * BLOCK
    half = tok // BLOCK
    blocks = 2 * half
    rows = n_head * BLOCK
    factor = HEAD_SIZE**-0.5 * LOG2E
    tiles = [(b, slice(r, r + TILE)) for b in range(blocks) for r in range(0, rows, TILE)]

    for n, ref in enumerate(pieces):
        held_ref[n, pl.ds(pl.multiple_of(core * tok, tok), tok)] = ref[:tok]
        held_ref[n, pl.ds(pl.multiple_of((1 - core) * tok, tok), tok)] = ref[tok:]

    def start_of(b):
        mine = b // half == core
        return jnp.where(mine, starts_ref[b % half], recv_starts_ref[b % half])

    def rows_of(ref, j, lane0):
        t = slice(j * BLOCK, (j + 1) * BLOCK)
        return jnp.concatenate(
            [ref[t, pl.ds(lane0 + h * HEAD_SIZE, HEAD_SIZE)] for h in range(n_head)], axis=0
        )

    def scores(b, r, i, width):
        k = held_ref[i, :width, :HEAD_SIZE]
        return lax.dot_general(
            q_ref[b, r], k, (((1,), (1,)), ((), ())), preferred_element_type=jnp.float32
        )

    def weigh(p, i, width):
        v = held_ref[i, :width, HEAD_SIZE:]
        v = jnp.concatenate([v, jnp.ones_like(v)], axis=1)
        return jnp.dot(p.astype(jnp.bfloat16), v, preferred_element_type=jnp.float32)

    def keep(s, since):
        k_id = lax.broadcasted_iota(jnp.int32, (1, s.shape[1]), 1)
        return jnp.where(k_id >= since, s, MASKED)

    def both(top, total):
        lane = lax.broadcasted_iota(jnp.int32, total.shape, 1)
        return jnp.where(lane < HEAD_SIZE // 2, top, total)

    def update(i, base, b, r, stats_from, acc_from, to):
        s = keep(scores(b, r, i, 2 * tok), start_of(b) - base)
        stats = stats_from[b, r]
        old = stats[:, :1]
        top = jnp.maximum(old, jnp.max(s, axis=1, keepdims=True))
        p = jnp.exp2(s * factor - top * factor)
        decay = jnp.exp2((old - top) * factor)
        added = weigh(p, i, 2 * tok)
        stats_ref[to, r] = both(top, stats * decay + added[:, HEAD_SIZE:])
        acc_ref[to, r] = acc_from[b, r] * decay + added[:, :HEAD_SIZE]

    def attend_own():
        for j in range(half):
            mine = rows_of(queries_ref, j, pl.multiple_of(core * rows, rows))
            q_ref[core * half + j] = mine
            q_ref[(1 - core) * half + j] = rows_of(q_recv_ref, j, 0)
        t_id = lax.broadcasted_iota(jnp.int32, (TILE, BLOCK), 0) % BLOCK
        causal = lax.broadcasted_iota(jnp.int32, (TILE, BLOCK), 1) <= t_id
        for b, r in tiles:
            width = (b + 1) * BLOCK
            s = scores(b, r, 0, width)
            since = start_of(b) - pair * 2 * tok
            diag = jnp.where(causal, s[:, b * BLOCK :], MASKED)
            s = jnp.concatenate([keep(s[:, : b * BLOCK], since), diag], 1) if b else diag
            top = jnp.max(s, axis=1, keepdims=True)
            p = jnp.exp2(s * factor - top * factor)
            added = weigh(p, 0, width)
            stats_ref[b, r] = both(top, added[:, HEAD_SIZE:])
            acc_ref[b, r] = added[:, :HEAD_SIZE]

    def attend_next():
        stats_ref[...] = stats_in[...]
        acc_ref[...] = acc_in[...]

        @pl.loop(0, 2 * n_pieces)
        def _(step):
            i, first_block = step // 2, step % 2 * half
            behind = sum(
                jnp.where(i == n, jnp.where(col == 0, *d), 0) for n, d in enumerate(distances)
            )
            base = (pair - behind) * 2 * tok

            @pl.when(start_of(first_block) < base + 2 * tok)
            def _():
                for b, r in tiles[: len(tiles) // 2]:
                    b = first_block + b
                    update(i, base, b, r, stats_ref, acc_ref, b)

    def attend_last(shard):
        first_block = shard * half
        base = (pair - jnp.where(col == 0, *distances[0])) * 2 * tok
        needed = start_of(first_block) < base + 2 * tok

        @pl.when(needed)
        def _():
            for b, r in tiles[: len(tiles) // 2]:
                update(0, base, first_block + b, r, stats_in, acc_in, b)

        @pl.when(jnp.logical_not(needed))
        def _():
            stats_ref[...] = stats_in[pl.ds(first_block, half)]
            acc_ref[...] = acc_in[pl.ds(first_block, half)]

        for j in range(half):
            total = stats_ref[j, :, HEAD_SIZE // 2 : HEAD_SIZE // 2 + 1]
            o = (acc_ref[j] / total).astype(jnp.bfloat16)
            for h in range(n_head):
                first = core * rows + h * HEAD_SIZE if stage == "own" else h * HEAD_SIZE
                lanes = pl.ds(pl.multiple_of(first, HEAD_SIZE), HEAD_SIZE)
                out_ref[j * BLOCK : (j + 1) * BLOCK, lanes] = o[h * BLOCK : (h + 1) * BLOCK]
        if stage == "own":
            out_ref[:, pl.ds(pl.multiple_of((1 - core) * rows, rows), rows)] = swapped_ref[...]

    if stage == "first":
        attend_own()
    elif stage == "next":
        attend_next()
    else:
        attend_last(core if stage == "own" else 1 - core)


def attention_call(stage, distances, starts, recv_starts, operands):
    tok, half = starts.shape[0] * BLOCK, starts.shape[0]
    rows = operands[1].shape[1]
    blocks, n_head, n_pieces = 2 * half, rows // BLOCK, len(distances)
    state = [jax.ShapeDtypeStruct((blocks, rows, HEAD_SIZE), jnp.float32)] * 2
    scratch = [pltpu.VMEM((n_pieces, 2 * tok, 2 * HEAD_SIZE), jnp.bfloat16)]
    share = n_pieces
    if stage == "first":
        outs, share = [jax.ShapeDtypeStruct((blocks, rows, HEAD_SIZE), jnp.bfloat16)] + state, 0.6
    elif stage == "next":
        outs = state
    else:
        width = rows * (2 if stage == "own" else 1)
        outs, share = [jax.ShapeDtypeStruct((tok, width), jnp.bfloat16)], 0.5
        scratch = [pltpu.VMEM((half, rows, HEAD_SIZE), jnp.float32)] * 2 + scratch
    vmem, smem = pl.BlockSpec(memory_space=pltpu.VMEM), pl.BlockSpec(memory_space=pltpu.SMEM)
    return pl.pallas_call(
        functools.partial(attention_kernel, stage, distances, n_head),
        out_shape=outs,
        in_specs=[smem, smem] + [vmem] * len(operands),
        out_specs=[vmem] * len(outs),
        scratch_shapes=scratch,
        compiler_params=pltpu.CompilerParams(vmem_limit_bytes=24 * 2**20),
        cost_estimate=pl.CostEstimate(
            flops=int(share * blocks * rows * 2 * tok * HEAD_SIZE * 14),
            bytes_accessed=8 * 2**20,
            transcendentals=int(share * blocks * rows * 2 * tok),
        ),
    )(starts, recv_starts, *operands)


def per_device(queries, keys, values, block_start, out_weight):
    tok, group = queries.shape[0], queries.shape[1] // 2
    me, head = lax.axis_index("ctx"), lax.axis_index("head")
    cols = out_weight.shape[1] // 2
    tile, quarter = cols // 4, me // 4 % 2
    places = (me % 2 * group, ((1 - head) * 4 + quarter) * tile, 2 * quarter * tile, head * cols)
    keys, places = lax.optimization_barrier((keys, places))
    first_row, first_col, spare_col, here_col = places

    mine, theirs, q_send = small_call(
        prepare_kernel,
        [(tok, 2 * HEAD_SIZE)] * 2 + [(tok, group)],
        (keys, values, queries),
    )
    recv = swap(theirs, 1)
    one_behind = [rotate(mine, 4), rotate(recv, 4)]
    q_recv = swap(q_send, 1)
    recv_starts = swap(block_start, 1)
    (own,) = small_call(join_kernel, [(2 * tok, 2 * HEAD_SIZE)], (mine, recv))
    starts = (block_start, recv_starts)
    q_recv, weight = lax.optimization_barrier((q_recv, out_weight))
    sent = lax.dynamic_slice(weight, (first_row, first_col), (group, 3 * tile))
    q_recv, sent = lax.optimization_barrier((q_recv, sent))
    fetched = cross(sent, 0)
    q, *state = attention_call("first", ((0, 0),), *starts, (queries, q_recv, own))
    q, one_behind = lax.optimization_barrier((q, one_behind))
    (one_behind,) = small_call(join_kernel, [own.shape], one_behind)
    two_behind = rotate(one_behind, 4)
    across = swap(one_behind, 2)
    third = swap(small_call(pick_kernel, [own.shape], (own, two_behind))[0], 2)
    state = attention_call("next", ((2, 2),), *starts, (q, *state, one_behind))
    state = attention_call("next", ((1, 3), (4, 4)), *starts, (q, *state, across, two_behind))
    (o_other,) = attention_call("other", ((3, 1),), *starts, (q, *state, third))
    _, fetched = lax.optimization_barrier((o_other, fetched))
    weights = [fetched, swap(lax.dynamic_slice_in_dim(fetched, spare_col, tile, 1), 4)]
    (heads,) = attention_call("own", ((3, 1),), *starts, (q, *state, third, swap(o_other, 1)))
    heads_across = cross(heads, 0)
    rows_here = lax.dynamic_slice_in_dim(out_weight, here_col, cols, 1)
    here = jnp.dot(heads, rows_here, preferred_element_type=jnp.float32)
    weights += [swap(x, 1) for x in weights]
    return project(here.astype(jnp.bfloat16), heads_across, weights)


def solution(mesh):
    in_specs = (P("ctx", "head"), P("ctx", "head"), P("ctx", "head"), P("ctx"), P("head", None))
    out_specs = P("ctx", "head")
    return jax.shard_map(
        per_device, mesh=mesh, in_specs=in_specs, out_specs=out_specs, check_vma=False
    )
```

```python
import functools

import jax
import jax.numpy as jnp
from jax import lax
from jax.experimental import pallas as pl
from jax.experimental.pallas import tpu as pltpu
from jax.sharding import PartitionSpec as P

HEAD_SIZE = 128
BLOCK = 128
LOG2E = 1.4426950408889634
MASKED = -1e30
TILE = 256


def rotate(x, distance):
    n = lax.axis_size("ctx")
    return lax.ppermute(x, "ctx", [(i, (i + distance) % n) for i in range(n)])


def swap(x, mask):
    return lax.ppermute(x, "ctx", [(i, i ^ mask) for i in range(lax.axis_size("ctx"))])


def cross(x, mask):
    n = lax.axis_size("ctx")
    route = [(2 * i + h, 2 * (i ^ mask) + 1 - h) for i in range(n) for h in range(2)]
    return lax.ppermute(x, ("ctx", "head"), route)


def small_call(kernel, shapes, operands):
    vmem = pl.BlockSpec(memory_space=pltpu.VMEM)
    return pl.pallas_call(
        kernel,
        out_shape=[jax.ShapeDtypeStruct(shape, operands[0].dtype) for shape in shapes],
        in_specs=[vmem] * len(operands),
        out_specs=[vmem] * len(shapes),
        compiler_params=pltpu.CompilerParams(vmem_limit_bytes=6 * 2**20),
        cost_estimate=pl.CostEstimate(flops=2**20, bytes_accessed=2**20, transcendentals=0),
    )(*operands)


def join_kernel(first_ref, second_ref, out_ref):
    tok = first_ref.shape[0]
    out_ref[:tok] = first_ref[...]
    out_ref[tok:] = second_ref[...]


def pick_kernel(even_ref, odd_ref, out_ref):
    odd = lax.axis_index("ctx") // 2 % 2 == 1

    @pl.when(odd)
    def _():
        out_ref[...] = odd_ref[...]

    @pl.when(jnp.logical_not(odd))
    def _():
        out_ref[...] = even_ref[...]


def project_kernel(given_ref, heads_ref, *refs):
    parts, out_ref, built, sems = refs[:4], refs[4], refs[5], refs[6]
    me = lax.axis_index("ctx")
    core, part = me % 2, me // 4 % 2
    group, width = parts[1].shape
    copies = []
    for n, first in enumerate((part, part + 1, part + 2, 3 - 3 * part)):
        cols = pl.ds(pl.multiple_of(first * width, width), width)
        total = given_ref[:, cols].astype(jnp.float32)
        for index, (fetched, single) in ((core, parts[:2]), (1 - core, parts[2:])):
            heads = heads_ref[:, pl.ds(pl.multiple_of(index * group, group), group)]
            tile = fetched[:, n * width : (n + 1) * width] if n < 3 else single[...]
            total += jnp.dot(heads, tile, preferred_element_type=jnp.float32)
        built[n] = total.astype(out_ref.dtype)
        copies.append(pltpu.make_async_copy(built.at[n], out_ref.at[:, cols], sems.at[n]))
        copies[-1].start()
    for copy in copies:
        copy.wait()


def project(given, heads, tiles):
    tok, cols = given.shape
    vmem = pl.BlockSpec(memory_space=pltpu.VMEM)
    return pl.pallas_call(
        project_kernel,
        out_shape=jax.ShapeDtypeStruct(given.shape, jnp.bfloat16),
        in_specs=[vmem] * 6,
        out_specs=pl.BlockSpec(memory_space=pltpu.HBM),
        scratch_shapes=[pltpu.VMEM((4, tok, cols // 4), jnp.bfloat16), pltpu.SemaphoreType.DMA((4,))],
        compiler_params=pltpu.CompilerParams(vmem_limit_bytes=16 * 2**20),
        cost_estimate=pl.CostEstimate(
            flops=2 * tok * heads.shape[1] * cols, bytes_accessed=4 * 2**20, transcendentals=0
        ),
    )(given, heads, *tiles)


def attention_kernel(stage, distances, n_head, starts_ref, recv_starts_ref, *refs):
    refs = list(refs)
    me = lax.axis_index("ctx")
    pair, core, col = me // 2, me % 2, (me // 2) % 2
    if stage == "first":
        queries_ref, q_recv_ref = refs[:2]
        refs = refs[2:]
    else:
        q_ref, stats_in, acc_in = refs[:3]
        refs = refs[3:]
    n_pieces = len(distances)
    pieces = refs[:n_pieces]
    refs = refs[n_pieces:]
    if stage == "first":
        q_ref, stats_ref, acc_ref, held_ref = refs
    elif stage == "next":
        stats_ref, acc_ref, held_ref = refs
    else:
        if stage == "own":
            swapped_ref, *refs = refs
        out_ref, stats_ref, acc_ref, held_ref = refs
    tok = starts_ref.shape[0] * BLOCK
    half = tok // BLOCK
    blocks = 2 * half
    rows = n_head * BLOCK
    factor = HEAD_SIZE**-0.5 * LOG2E
    tiles = [(b, slice(r, r + TILE)) for b in range(blocks) for r in range(0, rows, TILE)]

    for n, ref in enumerate(pieces):
        held_ref[n, pl.ds(pl.multiple_of(core * tok, tok), tok)] = ref[:tok]
        held_ref[n, pl.ds(pl.multiple_of((1 - core) * tok, tok), tok)] = ref[tok:]

    def start_of(b):
        mine = b // half == core
        return jnp.where(mine, starts_ref[b % half], recv_starts_ref[b % half])

    def rows_of(ref, j, lane0):
        t = slice(j * BLOCK, (j + 1) * BLOCK)
        return jnp.concatenate(
            [ref[t, pl.ds(lane0 + h * HEAD_SIZE, HEAD_SIZE)] for h in range(n_head)], axis=0
        )

    def scores(b, r, i, width):
        k = held_ref[i, :width, :HEAD_SIZE]
        return lax.dot_general(
            q_ref[b, r], k, (((1,), (1,)), ((), ())), preferred_element_type=jnp.float32
        )

    def weigh(p, i, width):
        v = held_ref[i, :width, HEAD_SIZE:]
        v = jnp.concatenate([v, jnp.ones_like(v)], axis=1)
        return jnp.dot(p.astype(jnp.bfloat16), v, preferred_element_type=jnp.float32)

    def keep(s, since):
        k_id = lax.broadcasted_iota(jnp.int32, (1, s.shape[1]), 1)
        return jnp.where(k_id >= since, s, MASKED)

    def both(top, total):
        lane = lax.broadcasted_iota(jnp.int32, total.shape, 1)
        return jnp.where(lane < HEAD_SIZE // 2, top, total)

    def update(i, base, b, r, stats_from, acc_from, to):
        s = keep(scores(b, r, i, 2 * tok), start_of(b) - base)
        stats = stats_from[b, r]
        old = stats[:, :1]
        top = jnp.maximum(old, jnp.max(s, axis=1, keepdims=True))
        p = jnp.exp2(s * factor - top * factor)
        decay = jnp.exp2((old - top) * factor)
        added = weigh(p, i, 2 * tok)
        stats_ref[to, r] = both(top, stats * decay + added[:, HEAD_SIZE:])
        acc_ref[to, r] = acc_from[b, r] * decay + added[:, :HEAD_SIZE]

    def attend_own():
        for j in range(half):
            lanes = pl.multiple_of(core * rows, rows)
            q_ref[core * half + j] = rows_of(queries_ref, j, lanes)
            q_ref[(1 - core) * half + j] = rows_of(q_recv_ref, j, lanes)
        t_id = lax.broadcasted_iota(jnp.int32, (TILE, BLOCK), 0) % BLOCK
        causal = lax.broadcasted_iota(jnp.int32, (TILE, BLOCK), 1) <= t_id
        for b, r in tiles:
            width = (b + 1) * BLOCK
            s = scores(b, r, 0, width)
            since = start_of(b) - pair * 2 * tok
            diag = jnp.where(causal, s[:, b * BLOCK :], MASKED)
            s = jnp.concatenate([keep(s[:, : b * BLOCK], since), diag], 1) if b else diag
            top = jnp.max(s, axis=1, keepdims=True)
            p = jnp.exp2(s * factor - top * factor)
            added = weigh(p, 0, width)
            stats_ref[b, r] = both(top, added[:, HEAD_SIZE:])
            acc_ref[b, r] = added[:, :HEAD_SIZE]

    def attend_next():
        stats_ref[...] = stats_in[...]
        acc_ref[...] = acc_in[...]

        @pl.loop(0, 2 * n_pieces)
        def _(step):
            i, first_block = step // 2, step % 2 * half
            behind = sum(
                jnp.where(i == n, jnp.where(col == 0, *d), 0) for n, d in enumerate(distances)
            )
            base = (pair - behind) * 2 * tok

            @pl.when(start_of(first_block) < base + 2 * tok)
            def _():
                for b, r in tiles[: len(tiles) // 2]:
                    b = first_block + b
                    update(i, base, b, r, stats_ref, acc_ref, b)

    def attend_last(shard):
        first_block = shard * half
        base = (pair - jnp.where(col == 0, *distances[0])) * 2 * tok
        needed = start_of(first_block) < base + 2 * tok

        @pl.when(needed)
        def _():
            for b, r in tiles[: len(tiles) // 2]:
                update(0, base, first_block + b, r, stats_in, acc_in, b)

        @pl.when(jnp.logical_not(needed))
        def _():
            stats_ref[...] = stats_in[pl.ds(first_block, half)]
            acc_ref[...] = acc_in[pl.ds(first_block, half)]

        for j in range(half):
            total = stats_ref[j, :, HEAD_SIZE // 2 : HEAD_SIZE // 2 + 1]
            o = (acc_ref[j] / total).astype(jnp.bfloat16)
            for h in range(n_head):
                first = core * rows + h * HEAD_SIZE if stage == "own" else h * HEAD_SIZE
                lanes = pl.ds(pl.multiple_of(first, HEAD_SIZE), HEAD_SIZE)
                out_ref[j * BLOCK : (j + 1) * BLOCK, lanes] = o[h * BLOCK : (h + 1) * BLOCK]
        if stage == "own":
            out_ref[:, pl.ds(pl.multiple_of((1 - core) * rows, rows), rows)] = swapped_ref[...]

    if stage == "first":
        attend_own()
    elif stage == "next":
        attend_next()
    else:
        attend_last(core if stage == "own" else 1 - core)


def attention_call(stage, distances, starts, recv_starts, operands):
    tok, half = starts.shape[0] * BLOCK, starts.shape[0]
    rows = operands[1].shape[1] // (2 if stage == "first" else 1)
    blocks, n_head, n_pieces = 2 * half, rows // BLOCK, len(distances)
    state = [jax.ShapeDtypeStruct((blocks, rows, HEAD_SIZE), jnp.float32)] * 2
    scratch = [pltpu.VMEM((n_pieces, 2 * tok, 2 * HEAD_SIZE), jnp.bfloat16)]
    share = n_pieces
    if stage == "first":
        outs, share = [jax.ShapeDtypeStruct((blocks, rows, HEAD_SIZE), jnp.bfloat16)] + state, 0.6
    elif stage == "next":
        outs = state
    else:
        width = rows * (2 if stage == "own" else 1)
        outs, share = [jax.ShapeDtypeStruct((tok, width), jnp.bfloat16)], 0.5
        scratch = [pltpu.VMEM((half, rows, HEAD_SIZE), jnp.float32)] * 2 + scratch
    vmem, smem = pl.BlockSpec(memory_space=pltpu.VMEM), pl.BlockSpec(memory_space=pltpu.SMEM)
    return pl.pallas_call(
        functools.partial(attention_kernel, stage, distances, n_head),
        out_shape=outs,
        in_specs=[smem, smem] + [vmem] * len(operands),
        out_specs=[vmem] * len(outs),
        scratch_shapes=scratch,
        compiler_params=pltpu.CompilerParams(vmem_limit_bytes=24 * 2**20),
        cost_estimate=pl.CostEstimate(
            flops=int(share * blocks * rows * 2 * tok * HEAD_SIZE * 7),
            bytes_accessed=8 * 2**20,
            transcendentals=int(share * blocks * rows * 2 * tok),
        ),
    )(starts, recv_starts, *operands)


def per_device(queries, keys, values, block_start, out_weight):
    tok, group = queries.shape[0], queries.shape[1] // 2
    me, head = lax.axis_index("ctx"), lax.axis_index("head")
    cols = out_weight.shape[1] // 2
    tile, quarter = cols // 4, me // 4 % 2
    core = me % 2
    places = (core, 1 - core, core * group, ((1 - head) * 4 + quarter) * tile, 2 * quarter * tile)
    keys, (core, other, first_row, first_col, spare_col) = lax.optimization_barrier((keys, places))

    def part(x, index, size):
        return lax.dynamic_slice_in_dim(x, index * size, size, 1)

    mine = jnp.concatenate([part(keys, core, HEAD_SIZE), part(values, core, HEAD_SIZE)], 1)
    theirs = jnp.concatenate([part(keys, other, HEAD_SIZE), part(values, other, HEAD_SIZE)], 1)
    recv = swap(theirs, 1)
    one_behind = [rotate(mine, 4), rotate(recv, 4)]
    q_recv = swap(queries, 1)
    recv_starts = swap(block_start, 1)
    (own,) = small_call(join_kernel, [(2 * tok, 2 * HEAD_SIZE)], (mine, recv))
    starts = (block_start, recv_starts)
    q_recv, weight = lax.optimization_barrier((q_recv, out_weight))
    sent = lax.dynamic_slice(weight, (first_row, first_col), (group, 3 * tile))
    q_recv, sent = lax.optimization_barrier((q_recv, sent))
    fetched = cross(sent, 0)
    q, *state = attention_call("first", ((0, 0),), *starts, (queries, q_recv, own))
    q, one_behind = lax.optimization_barrier((q, one_behind))
    (one_behind,) = small_call(join_kernel, [own.shape], one_behind)
    two_behind = rotate(one_behind, 4)
    across = swap(one_behind, 2)
    third = swap(small_call(pick_kernel, [own.shape], (own, two_behind))[0], 2)
    state = attention_call("next", ((2, 2),), *starts, (q, *state, one_behind))
    state = attention_call("next", ((1, 3), (4, 4)), *starts, (q, *state, across, two_behind))
    (o_other,) = attention_call("other", ((3, 1),), *starts, (q, *state, third))
    (heads,) = attention_call("own", ((3, 1),), *starts, (q, *state, third, swap(o_other, 1)))
    _, fetched = lax.optimization_barrier((heads, fetched))
    weights = [fetched, swap(lax.dynamic_slice_in_dim(fetched, spare_col, tile, 1), 4)]
    heads_across = cross(heads, 0)
    here = jnp.dot(heads, part(out_weight, head, cols), preferred_element_type=jnp.float32)
    weights += [swap(x, 1) for x in weights]
    return project(here.astype(jnp.bfloat16), heads_across, weights)


def solution(mesh):
    in_specs = (P("ctx", "head"), P("ctx", "head"), P("ctx", "head"), P("ctx"), P("head", None))
    out_specs = P("ctx", "head")
    return jax.shard_map(
        per_device, mesh=mesh, in_specs=in_specs, out_specs=out_specs, check_vma=False
    )
```

```python
import functools

import jax
import jax.numpy as jnp
from jax import lax
from jax.experimental import pallas as pl
from jax.experimental.pallas import tpu as pltpu
from jax.sharding import PartitionSpec as P

HEAD_SIZE = 128
BLOCK = 128
LOG2E = 1.4426950408889634
MASKED = -1e30
TILE = 256


def rotate(x, distance):
    n = lax.axis_size("ctx")
    return lax.ppermute(x, "ctx", [(i, (i + distance) % n) for i in range(n)])


def swap(x, mask):
    return lax.ppermute(x, "ctx", [(i, i ^ mask) for i in range(lax.axis_size("ctx"))])


def cross(x, mask):
    n = lax.axis_size("ctx")
    route = [(2 * i + h, 2 * (i ^ mask) + 1 - h) for i in range(n) for h in range(2)]
    return lax.ppermute(x, ("ctx", "head"), route)


def small_call(kernel, shapes, operands):
    vmem = pl.BlockSpec(memory_space=pltpu.VMEM)
    return pl.pallas_call(
        kernel,
        out_shape=[jax.ShapeDtypeStruct(shape, operands[0].dtype) for shape in shapes],
        in_specs=[vmem] * len(operands),
        out_specs=[vmem] * len(shapes),
        compiler_params=pltpu.CompilerParams(vmem_limit_bytes=6 * 2**20),
        cost_estimate=pl.CostEstimate(flops=2**20, bytes_accessed=2**20, transcendentals=0),
    )(*operands)


def join_kernel(first_ref, second_ref, out_ref):
    tok = first_ref.shape[0]
    out_ref[:tok] = first_ref[...]
    out_ref[tok:] = second_ref[...]


def pick_kernel(even_ref, odd_ref, out_ref):
    odd = lax.axis_index("ctx") // 2 % 2 == 1

    @pl.when(odd)
    def _():
        out_ref[...] = odd_ref[...]

    @pl.when(jnp.logical_not(odd))
    def _():
        out_ref[...] = even_ref[...]


def project_kernel(given_ref, heads_ref, *refs):
    parts, out_ref, built, sems = refs[:5], refs[5], refs[6], refs[7]
    me = lax.axis_index("ctx")
    core, fetched = me % 2, me // 4 % 2
    group, width = parts[3].shape
    tiles = [x.at[:, n * width : (n + 1) * width] for x in parts[:3] for n in range(2)]
    tiles += parts[3:]
    copies = []
    for n in range(4):
        first = (fetched if n < 2 else 1 - fetched) * 2 + n % 2
        cols = pl.ds(pl.multiple_of(first * width, width), width)
        total = given_ref[:, cols].astype(jnp.float32)
        for index, tile in ((core, tiles[n]), (1 - core, tiles[4 + n])):
            heads = heads_ref[:, pl.ds(pl.multiple_of(index * group, group), group)]
            total += jnp.dot(heads, tile[...], preferred_element_type=jnp.float32)
        built[n] = total.astype(out_ref.dtype)
        copies.append(pltpu.make_async_copy(built.at[n], out_ref.at[:, cols], sems.at[n]))
        copies[-1].start()
    for copy in copies:
        copy.wait()


def project(given, heads, tiles):
    tok, cols = given.shape
    vmem = pl.BlockSpec(memory_space=pltpu.VMEM)
    return pl.pallas_call(
        project_kernel,
        out_shape=jax.ShapeDtypeStruct(given.shape, jnp.bfloat16),
        in_specs=[vmem] * 7,
        out_specs=pl.BlockSpec(memory_space=pltpu.HBM),
        scratch_shapes=[pltpu.VMEM((4, tok, cols // 4), jnp.bfloat16), pltpu.SemaphoreType.DMA((4,))],
        compiler_params=pltpu.CompilerParams(vmem_limit_bytes=16 * 2**20),
        cost_estimate=pl.CostEstimate(
            flops=2 * tok * heads.shape[1] * cols, bytes_accessed=4 * 2**20, transcendentals=0
        ),
    )(given, heads, *tiles)


def attention_kernel(stage, distances, n_head, starts_ref, recv_starts_ref, *refs):
    refs = list(refs)
    me = lax.axis_index("ctx")
    pair, core, col = me // 2, me % 2, (me // 2) % 2
    if stage == "first":
        queries_ref, q_recv_ref = refs[:2]
        refs = refs[2:]
    else:
        q_ref, stats_in, acc_in = refs[:3]
        refs = refs[3:]
    n_pieces = len(distances)
    pieces = refs[:n_pieces]
    refs = refs[n_pieces:]
    if stage == "first":
        q_ref, stats_ref, acc_ref, held_ref = refs
    elif stage == "next":
        stats_ref, acc_ref, held_ref = refs
    else:
        if stage == "own":
            swapped_ref, *refs = refs
        out_ref, stats_ref, acc_ref, held_ref = refs
    tok = starts_ref.shape[0] * BLOCK
    half = tok // BLOCK
    blocks = 2 * half
    rows = n_head * BLOCK
    factor = HEAD_SIZE**-0.5 * LOG2E
    tiles = [(b, slice(r, r + TILE)) for b in range(blocks) for r in range(0, rows, TILE)]

    for n, ref in enumerate(pieces):
        held_ref[n, pl.ds(pl.multiple_of(core * tok, tok), tok)] = ref[:tok]
        held_ref[n, pl.ds(pl.multiple_of((1 - core) * tok, tok), tok)] = ref[tok:]

    def start_of(b):
        mine = b // half == core
        return jnp.where(mine, starts_ref[b % half], recv_starts_ref[b % half])

    def rows_of(ref, j, lane0):
        t = slice(j * BLOCK, (j + 1) * BLOCK)
        return jnp.concatenate(
            [ref[t, pl.ds(lane0 + h * HEAD_SIZE, HEAD_SIZE)] for h in range(n_head)], axis=0
        )

    def scores(b, r, i, width):
        k = held_ref[i, :width, :HEAD_SIZE]
        return lax.dot_general(
            q_ref[b, r], k, (((1,), (1,)), ((), ())), preferred_element_type=jnp.float32
        )

    def weigh(p, i, width):
        v = held_ref[i, :width, HEAD_SIZE:]
        v = jnp.concatenate([v, jnp.ones_like(v)], axis=1)
        return jnp.dot(p.astype(jnp.bfloat16), v, preferred_element_type=jnp.float32)

    def keep(s, since):
        k_id = lax.broadcasted_iota(jnp.int32, (1, s.shape[1]), 1)
        return jnp.where(k_id >= since, s, MASKED)

    def both(top, total):
        lane = lax.broadcasted_iota(jnp.int32, total.shape, 1)
        return jnp.where(lane < HEAD_SIZE // 2, top, total)

    def update(i, base, b, r, stats_from, acc_from, to):
        s = keep(scores(b, r, i, 2 * tok), start_of(b) - base)
        stats = stats_from[b, r]
        old = stats[:, :1]
        top = jnp.maximum(old, jnp.max(s, axis=1, keepdims=True))
        p = jnp.exp2(s * factor - top * factor)
        decay = jnp.exp2((old - top) * factor)
        added = weigh(p, i, 2 * tok)
        stats_ref[to, r] = both(top, stats * decay + added[:, HEAD_SIZE:])
        acc_ref[to, r] = acc_from[b, r] * decay + added[:, :HEAD_SIZE]

    def attend_own():
        for j in range(half):
            lanes = pl.multiple_of(core * rows, rows)
            q_ref[core * half + j] = rows_of(queries_ref, j, lanes)
            q_ref[(1 - core) * half + j] = rows_of(q_recv_ref, j, lanes)
        t_id = lax.broadcasted_iota(jnp.int32, (TILE, BLOCK), 0) % BLOCK
        causal = lax.broadcasted_iota(jnp.int32, (TILE, BLOCK), 1) <= t_id
        for b, r in tiles:
            width = (b + 1) * BLOCK
            s = scores(b, r, 0, width)
            since = start_of(b) - pair * 2 * tok
            diag = jnp.where(causal, s[:, b * BLOCK :], MASKED)
            s = jnp.concatenate([keep(s[:, : b * BLOCK], since), diag], 1) if b else diag
            top = jnp.max(s, axis=1, keepdims=True)
            p = jnp.exp2(s * factor - top * factor)
            added = weigh(p, 0, width)
            stats_ref[b, r] = both(top, added[:, HEAD_SIZE:])
            acc_ref[b, r] = added[:, :HEAD_SIZE]

    def attend_next():
        stats_ref[...] = stats_in[...]
        acc_ref[...] = acc_in[...]

        @pl.loop(0, 2 * n_pieces)
        def _(step):
            i, first_block = step // 2, step % 2 * half
            behind = sum(
                jnp.where(i == n, jnp.where(col == 0, *d), 0) for n, d in enumerate(distances)
            )
            base = (pair - behind) * 2 * tok

            @pl.when(start_of(first_block) < base + 2 * tok)
            def _():
                for b, r in tiles[: len(tiles) // 2]:
                    b = first_block + b
                    update(i, base, b, r, stats_ref, acc_ref, b)

    def attend_last(shard):
        first_block = shard * half
        base = (pair - jnp.where(col == 0, *distances[0])) * 2 * tok
        needed = start_of(first_block) < base + 2 * tok

        @pl.when(needed)
        def _():
            for b, r in tiles[: len(tiles) // 2]:
                update(0, base, first_block + b, r, stats_in, acc_in, b)

        @pl.when(jnp.logical_not(needed))
        def _():
            stats_ref[...] = stats_in[pl.ds(first_block, half)]
            acc_ref[...] = acc_in[pl.ds(first_block, half)]

        for j in range(half):
            total = stats_ref[j, :, HEAD_SIZE // 2 : HEAD_SIZE // 2 + 1]
            o = (acc_ref[j] / total).astype(jnp.bfloat16)
            for h in range(n_head):
                first = core * rows + h * HEAD_SIZE if stage == "own" else h * HEAD_SIZE
                lanes = pl.ds(pl.multiple_of(first, HEAD_SIZE), HEAD_SIZE)
                out_ref[j * BLOCK : (j + 1) * BLOCK, lanes] = o[h * BLOCK : (h + 1) * BLOCK]
        if stage == "own":
            out_ref[:, pl.ds(pl.multiple_of((1 - core) * rows, rows), rows)] = swapped_ref[...]

    if stage == "first":
        attend_own()
    elif stage == "next":
        attend_next()
    else:
        attend_last(core if stage == "own" else 1 - core)


def attention_call(stage, distances, starts, recv_starts, operands):
    tok, half = starts.shape[0] * BLOCK, starts.shape[0]
    rows = operands[1].shape[1] // (2 if stage == "first" else 1)
    blocks, n_head, n_pieces = 2 * half, rows // BLOCK, len(distances)
    state = [jax.ShapeDtypeStruct((blocks, rows, HEAD_SIZE), jnp.float32)] * 2
    scratch = [pltpu.VMEM((n_pieces, 2 * tok, 2 * HEAD_SIZE), jnp.bfloat16)]
    share = n_pieces
    if stage == "first":
        outs, share = [jax.ShapeDtypeStruct((blocks, rows, HEAD_SIZE), jnp.bfloat16)] + state, 0.6
    elif stage == "next":
        outs = state
    else:
        width = rows * (2 if stage == "own" else 1)
        outs, share = [jax.ShapeDtypeStruct((tok, width), jnp.bfloat16)], 0.5
        scratch = [pltpu.VMEM((half, rows, HEAD_SIZE), jnp.float32)] * 2 + scratch
    vmem, smem = pl.BlockSpec(memory_space=pltpu.VMEM), pl.BlockSpec(memory_space=pltpu.SMEM)
    late = stage in ("own", "other")
    return pl.pallas_call(
        functools.partial(attention_kernel, stage, distances, n_head),
        out_shape=outs,
        in_specs=[smem, smem] + [vmem] * len(operands),
        out_specs=[vmem] * len(outs),
        scratch_shapes=scratch,
        compiler_params=pltpu.CompilerParams(vmem_limit_bytes=24 * 2**20),
        cost_estimate=pl.CostEstimate(
            flops=int(share * blocks * rows * 2 * tok * HEAD_SIZE * (25 if late else 10)),
            bytes_accessed=8 * 2**20,
            transcendentals=int(share * blocks * rows * 2 * tok),
        ),
    )(starts, recv_starts, *operands)


def per_device(queries, keys, values, block_start, out_weight):
    tok, group = queries.shape[0], queries.shape[1] // 2
    me, head = lax.axis_index("ctx"), lax.axis_index("head")
    cols = out_weight.shape[1] // 2
    core = me % 2
    places = (core, 1 - core, core * group, ((1 - head) * 2 + me // 4 % 2) * (cols // 2))
    keys, (core, other, first_row, first_col) = lax.optimization_barrier((keys, places))

    def part(x, index, size):
        return lax.dynamic_slice_in_dim(x, index * size, size, 1)

    mine = jnp.concatenate([part(keys, core, HEAD_SIZE), part(values, core, HEAD_SIZE)], 1)
    theirs = jnp.concatenate([part(keys, other, HEAD_SIZE), part(values, other, HEAD_SIZE)], 1)
    recv, recv_starts = lax.optimization_barrier((swap(theirs, 1), swap(block_start, 1)))
    one_behind = [rotate(mine, 4), rotate(recv, 4)]
    q_recv = swap(queries, 1)
    (own,) = small_call(join_kernel, [(2 * tok, 2 * HEAD_SIZE)], (mine, recv))
    starts = (block_start, recv_starts)
    q_recv, weight = lax.optimization_barrier((q_recv, out_weight))
    sent = lax.dynamic_slice(weight, (first_row, first_col), (group, cols // 2))
    q_recv, sent = lax.optimization_barrier((q_recv, sent))
    fetched = cross(sent, 0)
    q, *state = attention_call("first", ((0, 0),), *starts, (queries, q_recv, own))
    q, one_behind = lax.optimization_barrier((q, one_behind))
    (one_behind,) = small_call(join_kernel, [own.shape], one_behind)
    two_behind = rotate(one_behind, 4)
    across = swap(one_behind, 2)
    third = swap(small_call(pick_kernel, [own.shape], (own, two_behind))[0], 2)
    state = attention_call("next", ((2, 2),), *starts, (q, *state, one_behind))
    state = attention_call("next", ((1, 3), (4, 4)), *starts, (q, *state, across, two_behind))
    _, fetched = lax.optimization_barrier((third, fetched))
    passed = swap(fetched, 4)
    (o_other,) = attention_call("other", ((3, 1),), *starts, (q, *state, third))
    (heads,) = attention_call("own", ((3, 1),), *starts, (q, *state, third, swap(o_other, 1)))
    heads_across = cross(heads, 0)
    here = jnp.dot(heads, part(out_weight, head, cols), preferred_element_type=jnp.float32)
    here = here.astype(jnp.bfloat16)
    _, late = lax.optimization_barrier((here, passed))
    weights = [fetched, passed, swap(fetched, 1)]
    weights += [swap(part(late, n, cols // 4), 1) for n in range(2)]
    return project(here, heads_across, weights)


def solution(mesh):
    in_specs = (P("ctx", "head"), P("ctx", "head"), P("ctx", "head"), P("ctx"), P("head", None))
    out_specs = P("ctx", "head")
    return jax.shard_map(
        per_device, mesh=mesh, in_specs=in_specs, out_specs=out_specs, check_vma=False
    )
```

```python
import functools

import jax
import jax.numpy as jnp
from jax import lax
from jax.experimental import pallas as pl
from jax.experimental.pallas import tpu as pltpu
from jax.sharding import PartitionSpec as P

HEAD_SIZE = 128
BLOCK = 128
LOG2E = 1.4426950408889634
MASKED = -1e30
TILE = 256


def rotate(x, distance):
    n = lax.axis_size("ctx")
    return lax.ppermute(x, "ctx", [(i, (i + distance) % n) for i in range(n)])


def swap(x, mask):
    return lax.ppermute(x, "ctx", [(i, i ^ mask) for i in range(lax.axis_size("ctx"))])


def cross(x, mask):
    n = lax.axis_size("ctx")
    route = [(2 * i + h, 2 * (i ^ mask) + 1 - h) for i in range(n) for h in range(2)]
    return lax.ppermute(x, ("ctx", "head"), route)


def small_call(kernel, shapes, operands):
    vmem = pl.BlockSpec(memory_space=pltpu.VMEM)
    return pl.pallas_call(
        kernel,
        out_shape=[jax.ShapeDtypeStruct(shape, operands[0].dtype) for shape in shapes],
        in_specs=[vmem] * len(operands),
        out_specs=[vmem] * len(shapes),
        compiler_params=pltpu.CompilerParams(vmem_limit_bytes=6 * 2**20),
        cost_estimate=pl.CostEstimate(flops=2**20, bytes_accessed=2**20, transcendentals=0),
    )(*operands)


def join_kernel(first_ref, second_ref, out_ref):
    tok = first_ref.shape[0]
    out_ref[:tok] = first_ref[...]
    out_ref[tok:] = second_ref[...]


def pick_kernel(even_ref, odd_ref, out_ref):
    odd = lax.axis_index("ctx") // 2 % 2 == 1

    @pl.when(odd)
    def _():
        out_ref[...] = odd_ref[...]

    @pl.when(jnp.logical_not(odd))
    def _():
        out_ref[...] = even_ref[...]


def project_kernel(given_ref, heads_ref, *refs):
    parts, out_ref, built, sems = refs[:5], refs[5], refs[6], refs[7]
    me = lax.axis_index("ctx")
    core, fetched = me % 2, me // 4 % 2
    group, width = parts[3].shape
    tiles = [x.at[:, n * width : (n + 1) * width] for x in parts[:3] for n in range(2)]
    tiles += parts[3:]
    copies = []
    for n in range(4):
        first = (fetched if n < 2 else 1 - fetched) * 2 + n % 2
        cols = pl.ds(pl.multiple_of(first * width, width), width)
        total = given_ref[:, cols].astype(jnp.float32)
        for index, tile in ((core, tiles[n]), (1 - core, tiles[4 + n])):
            heads = heads_ref[:, pl.ds(pl.multiple_of(index * group, group), group)]
            total += jnp.dot(heads, tile[...], preferred_element_type=jnp.float32)
        built[n] = total.astype(out_ref.dtype)
        copies.append(pltpu.make_async_copy(built.at[n], out_ref.at[:, cols], sems.at[n]))
        copies[-1].start()
    for copy in copies:
        copy.wait()


def project(given, heads, tiles):
    tok, cols = given.shape
    vmem = pl.BlockSpec(memory_space=pltpu.VMEM)
    return pl.pallas_call(
        project_kernel,
        out_shape=jax.ShapeDtypeStruct(given.shape, jnp.bfloat16),
        in_specs=[vmem] * 7,
        out_specs=pl.BlockSpec(memory_space=pltpu.HBM),
        scratch_shapes=[pltpu.VMEM((4, tok, cols // 4), jnp.bfloat16), pltpu.SemaphoreType.DMA((4,))],
        compiler_params=pltpu.CompilerParams(vmem_limit_bytes=16 * 2**20),
        cost_estimate=pl.CostEstimate(
            flops=2 * tok * heads.shape[1] * cols, bytes_accessed=4 * 2**20, transcendentals=0
        ),
    )(given, heads, *tiles)


def attention_kernel(stage, distances, n_head, starts_ref, recv_starts_ref, *refs):
    refs = list(refs)
    me = lax.axis_index("ctx")
    pair, core, col = me // 2, me % 2, (me // 2) % 2
    if stage == "first":
        queries_ref, q_recv_ref = refs[:2]
        refs = refs[2:]
    else:
        q_ref, stats_in, acc_in = refs[:3]
        refs = refs[3:]
    n_pieces = len(distances)
    pieces = refs[:n_pieces]
    refs = refs[n_pieces:]
    if stage == "first":
        q_ref, stats_ref, acc_ref, held_ref = refs
    elif stage == "next":
        stats_ref, acc_ref, held_ref = refs
    else:
        if stage == "own":
            swapped_ref, *refs = refs
        out_ref, stats_ref, acc_ref, held_ref = refs
    tok = starts_ref.shape[0] * BLOCK
    half = tok // BLOCK
    blocks = 2 * half
    rows = n_head * BLOCK
    factor = HEAD_SIZE**-0.5 * LOG2E
    tiles = [(b, slice(r, r + TILE)) for b in range(blocks) for r in range(0, rows, TILE)]

    for n, ref in enumerate(pieces):
        held_ref[n, pl.ds(pl.multiple_of(core * tok, tok), tok)] = ref[:tok]
        held_ref[n, pl.ds(pl.multiple_of((1 - core) * tok, tok), tok)] = ref[tok:]

    def start_of(b):
        mine = b // half == core
        return jnp.where(mine, starts_ref[b % half], recv_starts_ref[b % half])

    def rows_of(ref, j, lane0):
        t = slice(j * BLOCK, (j + 1) * BLOCK)
        return jnp.concatenate(
            [ref[t, pl.ds(lane0 + h * HEAD_SIZE, HEAD_SIZE)] for h in range(n_head)], axis=0
        )

    def scores(b, r, i, width):
        k = held_ref[i, :width, :HEAD_SIZE]
        return lax.dot_general(
            q_ref[b, r], k, (((1,), (1,)), ((), ())), preferred_element_type=jnp.float32
        )

    def weigh(p, i, width):
        v = held_ref[i, :width, HEAD_SIZE:]
        v = jnp.concatenate([v, jnp.ones_like(v)], axis=1)
        return jnp.dot(p.astype(jnp.bfloat16), v, preferred_element_type=jnp.float32)

    def keep(s, since):
        k_id = lax.broadcasted_iota(jnp.int32, (1, s.shape[1]), 1)
        return jnp.where(k_id >= since, s, MASKED)

    def both(top, total):
        lane = lax.broadcasted_iota(jnp.int32, total.shape, 1)
        return jnp.where(lane < HEAD_SIZE // 2, top, total)

    def update(i, base, b, r, stats_from, acc_from, to):
        s = keep(scores(b, r, i, 2 * tok), start_of(b) - base)
        stats = stats_from[b, r]
        old = stats[:, :1]
        top = jnp.maximum(old, jnp.max(s, axis=1, keepdims=True))
        p = jnp.exp2(s * factor - top * factor)
        decay = jnp.exp2((old - top) * factor)
        added = weigh(p, i, 2 * tok)
        stats_ref[to, r] = both(top, stats * decay + added[:, HEAD_SIZE:])
        acc_ref[to, r] = acc_from[b, r] * decay + added[:, :HEAD_SIZE]

    def attend_own():
        for j in range(half):
            lanes = pl.multiple_of(core * rows, rows)
            q_ref[core * half + j] = rows_of(queries_ref, j, lanes)
            q_ref[(1 - core) * half + j] = rows_of(q_recv_ref, j, lanes)
        t_id = lax.broadcasted_iota(jnp.int32, (TILE, BLOCK), 0) % BLOCK
        causal = lax.broadcasted_iota(jnp.int32, (TILE, BLOCK), 1) <= t_id
        for b, r in tiles:
            width = (b + 1) * BLOCK
            s = scores(b, r, 0, width)
            since = start_of(b) - pair * 2 * tok
            diag = jnp.where(causal, s[:, b * BLOCK :], MASKED)
            s = jnp.concatenate([keep(s[:, : b * BLOCK], since), diag], 1) if b else diag
            top = jnp.max(s, axis=1, keepdims=True)
            p = jnp.exp2(s * factor - top * factor)
            added = weigh(p, 0, width)
            stats_ref[b, r] = both(top, added[:, HEAD_SIZE:])
            acc_ref[b, r] = added[:, :HEAD_SIZE]

    def attend_next():
        stats_ref[...] = stats_in[...]
        acc_ref[...] = acc_in[...]

        @pl.loop(0, 2 * n_pieces)
        def _(step):
            i, first_block = step // 2, step % 2 * half
            behind = sum(
                jnp.where(i == n, jnp.where(col == 0, *d), 0) for n, d in enumerate(distances)
            )
            base = (pair - behind) * 2 * tok

            @pl.when(start_of(first_block) < base + 2 * tok)
            def _():
                for b, r in tiles[: len(tiles) // 2]:
                    b = first_block + b
                    update(i, base, b, r, stats_ref, acc_ref, b)

    def attend_last(shard):
        first_block = shard * half
        base = (pair - jnp.where(col == 0, *distances[0])) * 2 * tok
        needed = start_of(first_block) < base + 2 * tok

        @pl.when(needed)
        def _():
            for b, r in tiles[: len(tiles) // 2]:
                update(0, base, first_block + b, r, stats_in, acc_in, b)

        @pl.when(jnp.logical_not(needed))
        def _():
            stats_ref[...] = stats_in[pl.ds(first_block, half)]
            acc_ref[...] = acc_in[pl.ds(first_block, half)]

        for j in range(half):
            total = stats_ref[j, :, HEAD_SIZE // 2 : HEAD_SIZE // 2 + 1]
            o = (acc_ref[j] / total).astype(jnp.bfloat16)
            for h in range(n_head):
                first = core * rows + h * HEAD_SIZE if stage == "own" else h * HEAD_SIZE
                lanes = pl.ds(pl.multiple_of(first, HEAD_SIZE), HEAD_SIZE)
                out_ref[j * BLOCK : (j + 1) * BLOCK, lanes] = o[h * BLOCK : (h + 1) * BLOCK]
        if stage == "own":
            out_ref[:, pl.ds(pl.multiple_of((1 - core) * rows, rows), rows)] = swapped_ref[...]

    if stage == "first":
        attend_own()
    elif stage == "next":
        attend_next()
    else:
        attend_last(core if stage == "own" else 1 - core)


def attention_call(stage, distances, cost, starts, recv_starts, operands):
    tok, half = starts.shape[0] * BLOCK, starts.shape[0]
    rows = operands[1].shape[1] // (2 if stage == "first" else 1)
    blocks, n_head, n_pieces = 2 * half, rows // BLOCK, len(distances)
    state = [jax.ShapeDtypeStruct((blocks, rows, HEAD_SIZE), jnp.float32)] * 2
    scratch = [pltpu.VMEM((n_pieces, 2 * tok, 2 * HEAD_SIZE), jnp.bfloat16)]
    share = n_pieces
    if stage == "first":
        outs, share = [jax.ShapeDtypeStruct((blocks, rows, HEAD_SIZE), jnp.bfloat16)] + state, 0.6
    elif stage == "next":
        outs = state
    else:
        width = rows * (2 if stage == "own" else 1)
        outs, share = [jax.ShapeDtypeStruct((tok, width), jnp.bfloat16)], 0.5
        scratch = [pltpu.VMEM((half, rows, HEAD_SIZE), jnp.float32)] * 2 + scratch
    vmem, smem = pl.BlockSpec(memory_space=pltpu.VMEM), pl.BlockSpec(memory_space=pltpu.SMEM)
    return pl.pallas_call(
        functools.partial(attention_kernel, stage, distances, n_head),
        out_shape=outs,
        in_specs=[smem, smem] + [vmem] * len(operands),
        out_specs=[vmem] * len(outs),
        scratch_shapes=scratch,
        compiler_params=pltpu.CompilerParams(vmem_limit_bytes=24 * 2**20),
        cost_estimate=pl.CostEstimate(
            flops=int(cost * 1e9),
            bytes_accessed=8 * 2**20,
            transcendentals=int(share * blocks * rows * 2 * tok),
        ),
    )(starts, recv_starts, *operands)


def per_device(queries, keys, values, block_start, out_weight):
    tok, group = queries.shape[0], queries.shape[1] // 2
    me, head = lax.axis_index("ctx"), lax.axis_index("head")
    cols = out_weight.shape[1] // 2
    core = me % 2
    lanes = (core * HEAD_SIZE, (1 - core) * HEAD_SIZE)
    corner = (core * group, ((1 - head) * 2 + me // 4 % 2) * (cols // 2))
    keys, lanes, corner, here_col = lax.optimization_barrier((keys, lanes, corner, head * cols))

    def cut(x, start, size):
        return lax.dynamic_slice(x, start, size, allow_negative_indices=False)

    def group_of(n):
        size = (tok, HEAD_SIZE)
        return jnp.concatenate([cut(keys, (0, lanes[n]), size), cut(values, (0, lanes[n]), size)], 1)

    mine, theirs = group_of(0), group_of(1)
    recv, recv_starts = lax.optimization_barrier((swap(theirs, 1), swap(block_start, 1)))
    one_behind = [rotate(mine, 4), rotate(recv, 4)]
    q_recv = swap(queries, 1)
    (own,) = small_call(join_kernel, [(2 * tok, 2 * HEAD_SIZE)], (mine, recv))
    starts = (block_start, recv_starts)
    q_recv, weight = lax.optimization_barrier((q_recv, out_weight))
    sent = cut(weight, corner, (group, cols // 2))
    q_recv, sent = lax.optimization_barrier((q_recv, sent))
    fetched = cross(sent, 0)
    q, *state = attention_call("first", ((0, 0),), 5, *starts, (queries, q_recv, own))
    q, one_behind = lax.optimization_barrier((q, one_behind))
    (one_behind,) = small_call(join_kernel, [own.shape], one_behind)
    two_behind = rotate(one_behind, 4)
    across = swap(one_behind, 2)
    third = swap(small_call(pick_kernel, [own.shape], (own, two_behind))[0], 2)
    state = attention_call("next", ((2, 2),), 2.1, *starts, (q, *state, one_behind))
    across, fetched = lax.optimization_barrier((across, fetched))
    state = attention_call("next", ((1, 3), (4, 4)), 4, *starts, (q, *state, across, two_behind))
    passed = swap(fetched, 4)
    (o_other,) = attention_call("other", ((3, 1),), 2, *starts, (q, *state, third))
    (heads,) = attention_call("own", ((3, 1),), 2, *starts, (q, *state, third, swap(o_other, 1)))
    heads_across = cross(heads, 0)
    rows_here = cut(out_weight, (0, here_col), (2 * group, cols))
    here = jnp.dot(heads, rows_here, preferred_element_type=jnp.float32)
    here = here.astype(jnp.bfloat16)
    _, late = lax.optimization_barrier((here, passed))
    weights = [fetched, passed, swap(fetched, 1)]
    weights += [swap(x, 1) for x in jnp.split(late, 2, 1)]
    return project(here, heads_across, weights)


def solution(mesh):
    in_specs = (P("ctx", "head"), P("ctx", "head"), P("ctx", "head"), P("ctx"), P("head", None))
    out_specs = P("ctx", "head")
    return jax.shard_map(
        per_device, mesh=mesh, in_specs=in_specs, out_specs=out_specs, check_vma=False
    )
```

```python
import functools

import jax
import jax.numpy as jnp
from jax import lax
from jax.experimental import pallas as pl
from jax.experimental.pallas import tpu as pltpu
from jax.sharding import PartitionSpec as P

HEAD_SIZE = 128
BLOCK = 128
LOG2E = 1.4426950408889634
MASKED = -1e30
TILE = 256


def rotate(x, distance):
    n = lax.axis_size("ctx")
    return lax.ppermute(x, "ctx", [(i, (i + distance) % n) for i in range(n)])


def swap(x, mask):
    return lax.ppermute(x, "ctx", [(i, i ^ mask) for i in range(lax.axis_size("ctx"))])


def cross(x, mask):
    n = lax.axis_size("ctx")
    route = [(2 * i + h, 2 * (i ^ mask) + 1 - h) for i in range(n) for h in range(2)]
    return lax.ppermute(x, ("ctx", "head"), route)


def small_call(kernel, shapes, operands):
    vmem = pl.BlockSpec(memory_space=pltpu.VMEM)
    return pl.pallas_call(
        kernel,
        out_shape=[jax.ShapeDtypeStruct(shape, operands[0].dtype) for shape in shapes],
        in_specs=[vmem] * len(operands),
        out_specs=[vmem] * len(shapes),
        compiler_params=pltpu.CompilerParams(vmem_limit_bytes=6 * 2**20),
        cost_estimate=pl.CostEstimate(flops=2**20, bytes_accessed=2**20, transcendentals=0),
    )(*operands)


def join_kernel(first_ref, second_ref, out_ref):
    tok = first_ref.shape[0]
    out_ref[:tok] = first_ref[...]
    out_ref[tok:] = second_ref[...]


def pick_kernel(even_ref, odd_ref, out_ref):
    odd = lax.axis_index("ctx") // 2 % 2 == 1

    @pl.when(odd)
    def _():
        out_ref[...] = odd_ref[...]

    @pl.when(jnp.logical_not(odd))
    def _():
        out_ref[...] = even_ref[...]


def project_kernel(given_ref, heads_ref, *refs):
    parts, out_ref, built, sems = refs[:5], refs[5], refs[6], refs[7]
    me = lax.axis_index("ctx")
    core, fetched = me % 2, me // 4 % 2
    group, width = parts[3].shape
    tiles = [x.at[:, n * width : (n + 1) * width] for x in parts[:3] for n in range(2)]
    tiles += parts[3:]
    copies = []
    for n in range(4):
        first = (fetched if n < 2 else 1 - fetched) * 2 + n % 2
        cols = pl.ds(pl.multiple_of(first * width, width), width)
        total = given_ref[:, cols].astype(jnp.float32)
        for index, tile in ((core, tiles[n]), (1 - core, tiles[4 + n])):
            heads = heads_ref[:, pl.ds(pl.multiple_of(index * group, group), group)]
            total += jnp.dot(heads, tile[...], preferred_element_type=jnp.float32)
        built[n] = total.astype(out_ref.dtype)
        copies.append(pltpu.make_async_copy(built.at[n], out_ref.at[:, cols], sems.at[n]))
        copies[-1].start()
    for copy in copies:
        copy.wait()


def project(given, heads, tiles):
    tok, cols = given.shape
    vmem = pl.BlockSpec(memory_space=pltpu.VMEM)
    return pl.pallas_call(
        project_kernel,
        out_shape=jax.ShapeDtypeStruct(given.shape, jnp.bfloat16),
        in_specs=[vmem] * 7,
        out_specs=pl.BlockSpec(memory_space=pltpu.HBM),
        scratch_shapes=[pltpu.VMEM((4, tok, cols // 4), jnp.bfloat16), pltpu.SemaphoreType.DMA((4,))],
        compiler_params=pltpu.CompilerParams(vmem_limit_bytes=16 * 2**20),
        cost_estimate=pl.CostEstimate(
            flops=2 * tok * heads.shape[1] * cols, bytes_accessed=4 * 2**20, transcendentals=0
        ),
    )(given, heads, *tiles)


def attention_kernel(stage, distances, n_head, starts_ref, recv_starts_ref, *refs):
    refs = list(refs)
    me = lax.axis_index("ctx")
    pair, core, col = me // 2, me % 2, (me // 2) % 2
    if stage == "first":
        queries_ref, q_recv_ref = refs[:2]
        refs = refs[2:]
    else:
        q_ref, stats_in, acc_in = refs[:3]
        refs = refs[3:]
    n_pieces = len(distances)
    pieces = refs[:n_pieces]
    refs = refs[n_pieces:]
    if stage == "first":
        q_ref, stats_ref, acc_ref, held_ref = refs
    elif stage == "next":
        stats_ref, acc_ref, held_ref = refs
    else:
        if stage == "own":
            swapped_ref, *refs = refs
        out_ref, stats_ref, acc_ref, held_ref = refs
    tok = starts_ref.shape[0] * BLOCK
    half = tok // BLOCK
    blocks = 2 * half
    rows = n_head * BLOCK
    factor = HEAD_SIZE**-0.5 * LOG2E
    tiles = [(b, slice(r, r + TILE)) for b in range(blocks) for r in range(0, rows, TILE)]

    for n, ref in enumerate(pieces):
        held_ref[n, pl.ds(pl.multiple_of(core * tok, tok), tok)] = ref[:tok]
        held_ref[n, pl.ds(pl.multiple_of((1 - core) * tok, tok), tok)] = ref[tok:]

    def start_of(b):
        mine = b // half == core
        return jnp.where(mine, starts_ref[b % half], recv_starts_ref[b % half])

    def rows_of(ref, j, lane0):
        t = slice(j * BLOCK, (j + 1) * BLOCK)
        return jnp.concatenate(
            [ref[t, pl.ds(lane0 + h * HEAD_SIZE, HEAD_SIZE)] for h in range(n_head)], axis=0
        )

    def scores(b, r, i, width):
        k = held_ref[i, :width, :HEAD_SIZE]
        return lax.dot_general(
            q_ref[b, r], k, (((1,), (1,)), ((), ())), preferred_element_type=jnp.float32
        )

    def weigh(p, i, width):
        v = held_ref[i, :width, HEAD_SIZE:]
        v = jnp.concatenate([v, jnp.ones_like(v)], axis=1)
        return jnp.dot(p.astype(jnp.bfloat16), v, preferred_element_type=jnp.float32)

    def keep(s, since):
        k_id = lax.broadcasted_iota(jnp.int32, (1, s.shape[1]), 1)
        return jnp.where(k_id >= since, s, MASKED)

    def both(top, total):
        lane = lax.broadcasted_iota(jnp.int32, total.shape, 1)
        return jnp.where(lane < HEAD_SIZE // 2, top, total)

    def update(i, base, b, r, stats_from, acc_from, to):
        s = keep(scores(b, r, i, 2 * tok), start_of(b) - base)
        stats = stats_from[b, r]
        old = stats[:, :1]
        top = jnp.maximum(old, jnp.max(s, axis=1, keepdims=True))
        p = jnp.exp2(s * factor - top * factor)
        decay = jnp.exp2((old - top) * factor)
        added = weigh(p, i, 2 * tok)
        stats_ref[to, r] = both(top, stats * decay + added[:, HEAD_SIZE:])
        acc_ref[to, r] = acc_from[b, r] * decay + added[:, :HEAD_SIZE]

    def attend_own():
        for j in range(half):
            lanes = pl.multiple_of(core * rows, rows)
            q_ref[core * half + j] = rows_of(queries_ref, j, lanes)
            q_ref[(1 - core) * half + j] = rows_of(q_recv_ref, j, lanes)
        t_id = lax.broadcasted_iota(jnp.int32, (TILE, BLOCK), 0) % BLOCK
        causal = lax.broadcasted_iota(jnp.int32, (TILE, BLOCK), 1) <= t_id
        for b, r in tiles:
            width = (b + 1) * BLOCK
            s = scores(b, r, 0, width)
            since = start_of(b) - pair * 2 * tok
            diag = jnp.where(causal, s[:, b * BLOCK :], MASKED)
            s = jnp.concatenate([keep(s[:, : b * BLOCK], since), diag], 1) if b else diag
            top = jnp.max(s, axis=1, keepdims=True)
            p = jnp.exp2(s * factor - top * factor)
            added = weigh(p, 0, width)
            stats_ref[b, r] = both(top, added[:, HEAD_SIZE:])
            acc_ref[b, r] = added[:, :HEAD_SIZE]

    def attend_next():
        stats_ref[...] = stats_in[...]
        acc_ref[...] = acc_in[...]

        @pl.loop(0, 2 * n_pieces)
        def _(step):
            i, first_block = step // 2, step % 2 * half
            behind = sum(
                jnp.where(i == n, jnp.where(col == 0, *d), 0) for n, d in enumerate(distances)
            )
            base = (pair - behind) * 2 * tok

            @pl.when(start_of(first_block) < base + 2 * tok)
            def _():
                for b, r in tiles[: len(tiles) // 2]:
                    b = first_block + b
                    update(i, base, b, r, stats_ref, acc_ref, b)

    def attend_last(shard):
        first_block = shard * half
        base = (pair - jnp.where(col == 0, *distances[0])) * 2 * tok
        needed = start_of(first_block) < base + 2 * tok

        @pl.when(needed)
        def _():
            for b, r in tiles[: len(tiles) // 2]:
                update(0, base, first_block + b, r, stats_in, acc_in, b)

        @pl.when(jnp.logical_not(needed))
        def _():
            stats_ref[...] = stats_in[pl.ds(first_block, half)]
            acc_ref[...] = acc_in[pl.ds(first_block, half)]

        for j in range(half):
            total = stats_ref[j, :, HEAD_SIZE // 2 : HEAD_SIZE // 2 + 1]
            o = (acc_ref[j] / total).astype(jnp.bfloat16)
            for h in range(n_head):
                first = core * rows + h * HEAD_SIZE if stage == "own" else h * HEAD_SIZE
                lanes = pl.ds(pl.multiple_of(first, HEAD_SIZE), HEAD_SIZE)
                out_ref[j * BLOCK : (j + 1) * BLOCK, lanes] = o[h * BLOCK : (h + 1) * BLOCK]
        if stage == "own":
            out_ref[:, pl.ds(pl.multiple_of((1 - core) * rows, rows), rows)] = swapped_ref[...]

    if stage == "first":
        attend_own()
    elif stage == "next":
        attend_next()
    else:
        attend_last(core if stage == "own" else 1 - core)


def attention_call(stage, distances, cost, starts, recv_starts, operands):
    tok, half = starts.shape[0] * BLOCK, starts.shape[0]
    rows = operands[1].shape[1] // (2 if stage == "first" else 1)
    blocks, n_head, n_pieces = 2 * half, rows // BLOCK, len(distances)
    state = [jax.ShapeDtypeStruct((blocks, rows, HEAD_SIZE), jnp.float32)] * 2
    scratch = [pltpu.VMEM((n_pieces, 2 * tok, 2 * HEAD_SIZE), jnp.bfloat16)]
    share = n_pieces
    if stage == "first":
        outs, share = [jax.ShapeDtypeStruct((blocks, rows, HEAD_SIZE), jnp.bfloat16)] + state, 0.6
    elif stage == "next":
        outs = state
    else:
        width = rows * (2 if stage == "own" else 1)
        outs, share = [jax.ShapeDtypeStruct((tok, width), jnp.bfloat16)], 0.5
        scratch = [pltpu.VMEM((half, rows, HEAD_SIZE), jnp.float32)] * 2 + scratch
    vmem, smem = pl.BlockSpec(memory_space=pltpu.VMEM), pl.BlockSpec(memory_space=pltpu.SMEM)
    return pl.pallas_call(
        functools.partial(attention_kernel, stage, distances, n_head),
        out_shape=outs,
        in_specs=[smem, smem] + [vmem] * len(operands),
        out_specs=[vmem] * len(outs),
        scratch_shapes=scratch,
        compiler_params=pltpu.CompilerParams(vmem_limit_bytes=24 * 2**20),
        cost_estimate=pl.CostEstimate(
            flops=int(cost * 1e9),
            bytes_accessed=8 * 2**20,
            transcendentals=int(share * blocks * rows * 2 * tok),
        ),
    )(starts, recv_starts, *operands)


def per_device(queries, keys, values, block_start, out_weight):
    tok, group = queries.shape[0], queries.shape[1] // 2
    me, head = lax.axis_index("ctx"), lax.axis_index("head")
    cols = out_weight.shape[1] // 2
    core = me % 2
    lanes = (core * HEAD_SIZE, (1 - core) * HEAD_SIZE)
    corner = (core * group, ((1 - head) * 2 + me // 4 % 2) * (cols // 2))
    keys, lanes, corner, here_col = lax.optimization_barrier((keys, lanes, corner, head * cols))

    def cut(x, start, size):
        return lax.dynamic_slice(x, start, size, allow_negative_indices=False)

    def group_of(n):
        size = (tok, HEAD_SIZE)
        return jnp.concatenate([cut(keys, (0, lanes[n]), size), cut(values, (0, lanes[n]), size)], 1)

    mine, theirs = group_of(0), group_of(1)
    recv, recv_starts = lax.optimization_barrier((swap(theirs, 1), swap(block_start, 1)))
    one_behind = [rotate(mine, 4), rotate(recv, 4)]
    q_recv = swap(queries, 1)
    (own,) = small_call(join_kernel, [(2 * tok, 2 * HEAD_SIZE)], (mine, recv))
    starts = (block_start, recv_starts)
    q_recv, weight = lax.optimization_barrier((q_recv, out_weight))
    sent = cut(weight, corner, (group, cols // 2))
    q_recv, sent = lax.optimization_barrier((q_recv, sent))
    fetched = cross(sent, 0)
    q, *state = attention_call("first", ((0, 0),), 5, *starts, (queries, q_recv, own))
    q, one_behind = lax.optimization_barrier((q, one_behind))
    (one_behind,) = small_call(join_kernel, [own.shape], one_behind)
    two_behind = rotate(one_behind, 4)
    across = swap(one_behind, 2)
    state = attention_call("next", ((2, 2),), 2.1, *starts, (q, *state, one_behind))
    _, ready = lax.optimization_barrier((state[0], two_behind))
    third = swap(small_call(pick_kernel, [own.shape], (own, ready))[0], 2)
    state = attention_call("next", ((1, 3), (4, 4)), 4, *starts, (q, *state, across, two_behind))
    _, fetched = lax.optimization_barrier((state[0], fetched))
    passed = swap(fetched, 4)
    (o_other,) = attention_call("other", ((3, 1),), 2, *starts, (q, *state, third))
    (heads,) = attention_call("own", ((3, 1),), 2, *starts, (q, *state, third, swap(o_other, 1)))
    heads_across = cross(heads, 0)
    rows_here = cut(out_weight, (0, here_col), (2 * group, cols))
    here = jnp.dot(heads, rows_here, preferred_element_type=jnp.float32)
    here = here.astype(jnp.bfloat16)
    _, late = lax.optimization_barrier((here, passed))
    weights = [fetched, passed, swap(fetched, 1)]
    weights += [swap(x, 1) for x in jnp.split(late, 2, 1)]
    return project(here, heads_across, weights)


def solution(mesh):
    in_specs = (P("ctx", "head"), P("ctx", "head"), P("ctx", "head"), P("ctx"), P("head", None))
    out_specs = P("ctx", "head")
    return jax.shard_map(
        per_device, mesh=mesh, in_specs=in_specs, out_specs=out_specs, check_vma=False
    )
```

```python
import functools

import jax
import jax.numpy as jnp
from jax import lax
from jax.experimental import pallas as pl
from jax.experimental.pallas import tpu as pltpu
from jax.sharding import PartitionSpec as P

HEAD_SIZE = 128
BLOCK = 128
LOG2E = 1.4426950408889634
MASKED = -1e30
TILE = 256


def rotate(x, distance):
    n = lax.axis_size("ctx")
    return lax.ppermute(x, "ctx", [(i, (i + distance) % n) for i in range(n)])


def swap(x, mask):
    return lax.ppermute(x, "ctx", [(i, i ^ mask) for i in range(lax.axis_size("ctx"))])


def cross(x, mask):
    n = lax.axis_size("ctx")
    route = [(2 * i + h, 2 * (i ^ mask) + 1 - h) for i in range(n) for h in range(2)]
    return lax.ppermute(x, ("ctx", "head"), route)


def small_call(kernel, shapes, operands):
    vmem = pl.BlockSpec(memory_space=pltpu.VMEM)
    return pl.pallas_call(
        kernel,
        out_shape=[jax.ShapeDtypeStruct(shape, operands[0].dtype) for shape in shapes],
        in_specs=[vmem] * len(operands),
        out_specs=[vmem] * len(shapes),
        compiler_params=pltpu.CompilerParams(vmem_limit_bytes=6 * 2**20),
        cost_estimate=pl.CostEstimate(flops=2**20, bytes_accessed=2**20, transcendentals=0),
    )(*operands)


def join_kernel(first_ref, second_ref, out_ref):
    tok = first_ref.shape[0]
    out_ref[:tok] = first_ref[...]
    out_ref[tok:] = second_ref[...]


def pick_kernel(even_ref, odd_ref, out_ref):
    odd = lax.axis_index("ctx") // 2 % 2 == 1

    @pl.when(odd)
    def _():
        out_ref[...] = odd_ref[...]

    @pl.when(jnp.logical_not(odd))
    def _():
        out_ref[...] = even_ref[...]


def spare_kernel(window_ref, out_ref):
    fetched = lax.axis_index("ctx") // 4 % 2
    first = fetched * (window_ref.shape[1] - out_ref.shape[1])
    out_ref[...] = window_ref[:, pl.ds(pl.multiple_of(first, HEAD_SIZE), out_ref.shape[1])]


def project_kernel(final, given_ref, heads_ref, window_ref, rest_ref, *refs):
    fetched = lax.axis_index("ctx") // 4 % 2
    wide, narrow = window_ref.shape[1], rest_ref.shape[1]
    half = wide // 2
    tiles = (
        (window_ref.at[:, :half], fetched * narrow),
        (window_ref.at[:, half:], fetched * narrow + half),
        (rest_ref, (1 - fetched) * wide),
    )
    copies = []
    for n, (tile, col) in enumerate(tiles):
        cols = pl.ds(pl.multiple_of(col, HEAD_SIZE), tile.shape[1])
        total = given_ref[:, cols].astype(jnp.float32)
        total += jnp.dot(heads_ref[...], tile[...], preferred_element_type=jnp.float32)
        if final:
            out_ref, built, sems = refs[0], refs[1 + n], refs[4]
            built[...] = total.astype(out_ref.dtype)
            copies.append(pltpu.make_async_copy(built, out_ref.at[:, cols], sems.at[n]))
            copies[-1].start()
        else:
            refs[0][:, cols] = total
    for copy in copies:
        copy.wait()


def project(final, given, heads, parts):
    tok, cols = given.shape
    vmem = pl.BlockSpec(memory_space=pltpu.VMEM)
    half = parts[0].shape[1] // 2
    scratch = [pltpu.VMEM((tok, n), jnp.bfloat16) for n in (half, half, parts[1].shape[1])]
    scratch += [pltpu.SemaphoreType.DMA((3,))]
    return pl.pallas_call(
        functools.partial(project_kernel, final),
        out_shape=jax.ShapeDtypeStruct(given.shape, jnp.bfloat16 if final else jnp.float32),
        in_specs=[vmem] * 4,
        out_specs=pl.BlockSpec(memory_space=pltpu.HBM) if final else vmem,
        scratch_shapes=scratch if final else [],
        compiler_params=pltpu.CompilerParams(vmem_limit_bytes=16 * 2**20),
        cost_estimate=pl.CostEstimate(
            flops=2 * tok * heads.shape[1] * cols, bytes_accessed=4 * 2**20, transcendentals=0
        ),
    )(given, heads, *parts)


def attention_kernel(stage, distances, n_head, starts_ref, recv_starts_ref, *refs):
    refs = list(refs)
    me = lax.axis_index("ctx")
    pair, core, col = me // 2, me % 2, (me // 2) % 2
    if stage == "first":
        queries_ref, q_recv_ref = refs[:2]
        refs = refs[2:]
    else:
        q_ref, stats_in, acc_in = refs[:3]
        refs = refs[3:]
    n_pieces = len(distances)
    pieces = refs[:n_pieces]
    refs = refs[n_pieces:]
    if stage == "first":
        q_ref, stats_ref, acc_ref, held_ref = refs
    elif stage == "next":
        stats_ref, acc_ref, held_ref = refs
    else:
        out_ref, stats_ref, acc_ref, held_ref = refs
    tok = starts_ref.shape[0] * BLOCK
    half = tok // BLOCK
    blocks = 2 * half
    rows = n_head * BLOCK
    factor = HEAD_SIZE**-0.5 * LOG2E
    tiles = [(b, slice(r, r + TILE)) for b in range(blocks) for r in range(0, rows, TILE)]

    for n, ref in enumerate(pieces):
        held_ref[n, pl.ds(pl.multiple_of(core * tok, tok), tok)] = ref[:tok]
        held_ref[n, pl.ds(pl.multiple_of((1 - core) * tok, tok), tok)] = ref[tok:]

    def start_of(b):
        mine = b // half == core
        return jnp.where(mine, starts_ref[b % half], recv_starts_ref[b % half])

    def rows_of(ref, j, lane0):
        t = slice(j * BLOCK, (j + 1) * BLOCK)
        return jnp.concatenate(
            [ref[t, pl.ds(lane0 + h * HEAD_SIZE, HEAD_SIZE)] for h in range(n_head)], axis=0
        )

    def scores(b, r, i, width):
        k = held_ref[i, :width, :HEAD_SIZE]
        return lax.dot_general(
            q_ref[b, r], k, (((1,), (1,)), ((), ())), preferred_element_type=jnp.float32
        )

    def weigh(p, i, width):
        v = held_ref[i, :width, HEAD_SIZE:]
        v = jnp.concatenate([v, jnp.ones_like(v)], axis=1)
        return jnp.dot(p.astype(jnp.bfloat16), v, preferred_element_type=jnp.float32)

    def keep(s, since):
        k_id = lax.broadcasted_iota(jnp.int32, (1, s.shape[1]), 1)
        return jnp.where(k_id >= since, s, MASKED)

    def both(top, total):
        lane = lax.broadcasted_iota(jnp.int32, total.shape, 1)
        return jnp.where(lane < HEAD_SIZE // 2, top, total)

    def update(i, base, b, r, stats_from, acc_from, to):
        s = keep(scores(b, r, i, 2 * tok), start_of(b) - base)
        stats = stats_from[b, r]
        old = stats[:, :1]
        top = jnp.maximum(old, jnp.max(s, axis=1, keepdims=True))
        p = jnp.exp2(s * factor - top * factor)
        decay = jnp.exp2((old - top) * factor)
        added = weigh(p, i, 2 * tok)
        stats_ref[to, r] = both(top, stats * decay + added[:, HEAD_SIZE:])
        acc_ref[to, r] = acc_from[b, r] * decay + added[:, :HEAD_SIZE]

    def attend_own():
        for j in range(half):
            lanes = pl.multiple_of(core * rows, rows)
            q_ref[core * half + j] = rows_of(queries_ref, j, lanes)
            q_ref[(1 - core) * half + j] = rows_of(q_recv_ref, j, lanes)
        t_id = lax.broadcasted_iota(jnp.int32, (TILE, BLOCK), 0) % BLOCK
        causal = lax.broadcasted_iota(jnp.int32, (TILE, BLOCK), 1) <= t_id
        for b, r in tiles:
            width = (b + 1) * BLOCK
            s = scores(b, r, 0, width)
            since = start_of(b) - pair * 2 * tok
            diag = jnp.where(causal, s[:, b * BLOCK :], MASKED)
            s = jnp.concatenate([keep(s[:, : b * BLOCK], since), diag], 1) if b else diag
            top = jnp.max(s, axis=1, keepdims=True)
            p = jnp.exp2(s * factor - top * factor)
            added = weigh(p, 0, width)
            stats_ref[b, r] = both(top, added[:, HEAD_SIZE:])
            acc_ref[b, r] = added[:, :HEAD_SIZE]

    def attend_next():
        stats_ref[...] = stats_in[...]
        acc_ref[...] = acc_in[...]

        @pl.loop(0, 2 * n_pieces)
        def _(step):
            i, first_block = step // 2, step % 2 * half
            behind = sum(
                jnp.where(i == n, jnp.where(col == 0, *d), 0) for n, d in enumerate(distances)
            )
            base = (pair - behind) * 2 * tok

            @pl.when(start_of(first_block) < base + 2 * tok)
            def _():
                for b, r in tiles[: len(tiles) // 2]:
                    b = first_block + b
                    update(i, base, b, r, stats_ref, acc_ref, b)

    def attend_last(shard):
        first_block = shard * half
        base = (pair - jnp.where(col == 0, *distances[0])) * 2 * tok
        needed = start_of(first_block) < base + 2 * tok

        @pl.when(needed)
        def _():
            for b, r in tiles[: len(tiles) // 2]:
                update(0, base, first_block + b, r, stats_in, acc_in, b)

        @pl.when(jnp.logical_not(needed))
        def _():
            stats_ref[...] = stats_in[pl.ds(first_block, half)]
            acc_ref[...] = acc_in[pl.ds(first_block, half)]

        for j in range(half):
            total = stats_ref[j, :, HEAD_SIZE // 2 : HEAD_SIZE // 2 + 1]
            o = (acc_ref[j] / total).astype(jnp.bfloat16)
            for h in range(n_head):
                out_ref[j * BLOCK : (j + 1) * BLOCK, h * HEAD_SIZE : (h + 1) * HEAD_SIZE] = o[
                    h * BLOCK : (h + 1) * BLOCK
                ]

    if stage == "first":
        attend_own()
    elif stage == "next":
        attend_next()
    else:
        attend_last(core if stage == "own" else 1 - core)


def attention_call(stage, distances, cost, starts, recv_starts, operands):
    tok, half = starts.shape[0] * BLOCK, starts.shape[0]
    rows = operands[1].shape[1] // (2 if stage == "first" else 1)
    blocks, n_head, n_pieces = 2 * half, rows // BLOCK, len(distances)
    state = [jax.ShapeDtypeStruct((blocks, rows, HEAD_SIZE), jnp.float32)] * 2
    scratch = [pltpu.VMEM((n_pieces, 2 * tok, 2 * HEAD_SIZE), jnp.bfloat16)]
    share = n_pieces
    if stage == "first":
        outs, share = [jax.ShapeDtypeStruct((blocks, rows, HEAD_SIZE), jnp.bfloat16)] + state, 0.6
    elif stage == "next":
        outs = state
    else:
        outs, share = [jax.ShapeDtypeStruct((tok, rows), jnp.bfloat16)], 0.5
        scratch = [pltpu.VMEM((half, rows, HEAD_SIZE), jnp.float32)] * 2 + scratch
    vmem, smem = pl.BlockSpec(memory_space=pltpu.VMEM), pl.BlockSpec(memory_space=pltpu.SMEM)
    return pl.pallas_call(
        functools.partial(attention_kernel, stage, distances, n_head),
        out_shape=outs,
        in_specs=[smem, smem] + [vmem] * len(operands),
        out_specs=[vmem] * len(outs),
        scratch_shapes=scratch,
        compiler_params=pltpu.CompilerParams(vmem_limit_bytes=24 * 2**20),
        cost_estimate=pl.CostEstimate(
            flops=int(cost * 1e9),
            bytes_accessed=8 * 2**20,
            transcendentals=int(share * blocks * rows * 2 * tok),
        ),
    )(starts, recv_starts, *operands)


def per_device(queries, keys, values, block_start, out_weight):
    tok, group = queries.shape[0], queries.shape[1] // 2
    me, head = lax.axis_index("ctx"), lax.axis_index("head")
    cols = out_weight.shape[1] // 2
    core = me % 2
    lanes = (core * HEAD_SIZE, (1 - core) * HEAD_SIZE)
    narrow = cols * 3 // 8
    corner = (core * group, (1 - head) * cols + me // 4 % 2 * narrow)
    corners = ((core * group, head * cols), ((1 - core) * group, head * cols))
    keys, lanes, corner, corners = lax.optimization_barrier((keys, lanes, corner, corners))

    def cut(x, start, size):
        return lax.dynamic_slice(x, start, size, allow_negative_indices=False)

    def group_of(n):
        size = (tok, HEAD_SIZE)
        return jnp.concatenate([cut(keys, (0, lanes[n]), size), cut(values, (0, lanes[n]), size)], 1)

    mine, theirs = group_of(0), group_of(1)
    recv, recv_starts = lax.optimization_barrier((swap(theirs, 1), swap(block_start, 1)))
    one_behind = [rotate(mine, 4), rotate(recv, 4)]
    q_recv = swap(queries, 1)
    (own,) = small_call(join_kernel, [(2 * tok, 2 * HEAD_SIZE)], (mine, recv))
    starts = (block_start, recv_starts)
    q_recv, weight = lax.optimization_barrier((q_recv, out_weight))
    sent = cut(weight, corner, (group, cols - narrow))
    q_recv, sent = lax.optimization_barrier((q_recv, sent))
    fetched = cross(sent, 0)
    q, *state = attention_call("first", ((0, 0),), 5, *starts, (queries, q_recv, own))
    q, one_behind = lax.optimization_barrier((q, one_behind))
    (one_behind,) = small_call(join_kernel, [own.shape], one_behind)
    two_behind = rotate(one_behind, 4)
    across = swap(one_behind, 2)
    state = attention_call("next", ((2, 2),), 2.1, *starts, (q, *state, one_behind))
    _, ready = lax.optimization_barrier((state[0], two_behind))
    third = swap(small_call(pick_kernel, [own.shape], (own, ready))[0], 2)
    state = attention_call("next", ((1, 3), (4, 4)), 4, *starts, (q, *state, across, two_behind))
    (o_other,) = attention_call("other", ((3, 1),), 2, *starts, (q, *state, third))
    _, fetched = lax.optimization_barrier((o_other, fetched))
    passed = swap(small_call(spare_kernel, [(group, narrow)], (fetched,))[0], 4)
    across_other = cross(o_other, 1)
    swapped_other = swap(o_other, 1)
    (o_own,) = attention_call("own", ((3, 1),), 2, *starts, (q, *state, third))
    across_own = cross(o_own, 0)
    here = sum(
        jnp.dot(o, cut(out_weight, at, (group, cols)), preferred_element_type=jnp.float32)
        for o, at in zip((o_own, swapped_other), corners, strict=True)
    )
    here = here.astype(jnp.bfloat16)
    _, _, _, late = lax.optimization_barrier((here, across_own, across_other, passed))
    other_rows = (swap(fetched, 1), swap(late, 1))
    here = project(False, here, across_own, (fetched, passed))
    return project(True, here, across_other, other_rows)


def solution(mesh):
    in_specs = (P("ctx", "head"), P("ctx", "head"), P("ctx", "head"), P("ctx"), P("head", None))
    out_specs = P("ctx", "head")
    return jax.shard_map(
        per_device, mesh=mesh, in_specs=in_specs, out_specs=out_specs, check_vma=False
    )
```

```python
import functools

import jax
import jax.numpy as jnp
from jax import lax
from jax.experimental import pallas as pl
from jax.experimental.pallas import tpu as pltpu
from jax.sharding import PartitionSpec as P

HEAD_SIZE = 128
BLOCK = 128
LOG2E = 1.4426950408889634
MASKED = -1e30
TILE = 256


def rotate(x, distance):
    n = lax.axis_size("ctx")
    return lax.ppermute(x, "ctx", [(i, (i + distance) % n) for i in range(n)])


def shift(x, distance):
    n = lax.axis_size("ctx")
    return lax.ppermute(x, "ctx", [(i, i + distance) for i in range(n - distance)])


def swap(x, mask):
    return lax.ppermute(x, "ctx", [(i, i ^ mask) for i in range(lax.axis_size("ctx"))])


def cross(x, mask):
    n = lax.axis_size("ctx")
    route = [(2 * i + h, 2 * (i ^ mask) + 1 - h) for i in range(n) for h in range(2)]
    return lax.ppermute(x, ("ctx", "head"), route)


def small_call(kernel, shapes, operands):
    vmem = pl.BlockSpec(memory_space=pltpu.VMEM)
    return pl.pallas_call(
        kernel,
        out_shape=[jax.ShapeDtypeStruct(shape, operands[0].dtype) for shape in shapes],
        in_specs=[vmem] * len(operands),
        out_specs=[vmem] * len(shapes),
        compiler_params=pltpu.CompilerParams(vmem_limit_bytes=6 * 2**20),
        cost_estimate=pl.CostEstimate(flops=2**20, bytes_accessed=2**20, transcendentals=0),
    )(*operands)


def join_kernel(first_ref, second_ref, out_ref):
    tok = first_ref.shape[0]
    out_ref[:tok] = first_ref[...]
    out_ref[tok:] = second_ref[...]


def pick_kernel(even_ref, odd_ref, out_ref):
    odd = lax.axis_index("ctx") // 2 % 2 == 1

    @pl.when(odd)
    def _():
        out_ref[...] = odd_ref[...]

    @pl.when(jnp.logical_not(odd))
    def _():
        out_ref[...] = even_ref[...]


def spare_kernel(window_ref, out_ref):
    fetched = lax.axis_index("ctx") // 4 % 2
    first = fetched * (window_ref.shape[1] - out_ref.shape[1])
    out_ref[...] = window_ref[:, pl.ds(pl.multiple_of(first, HEAD_SIZE), out_ref.shape[1])]


def project_kernel(final, given_ref, heads_ref, window_ref, rest_ref, *refs):
    fetched = lax.axis_index("ctx") // 4 % 2
    wide, narrow = window_ref.shape[1], rest_ref.shape[1]
    half = wide // 2
    tiles = (
        (window_ref.at[:, :half], fetched * narrow),
        (window_ref.at[:, half:], fetched * narrow + half),
        (rest_ref, (1 - fetched) * wide),
    )
    copies = []
    for n, (tile, col) in enumerate(tiles):
        cols = pl.ds(pl.multiple_of(col, HEAD_SIZE), tile.shape[1])
        total = given_ref[:, cols].astype(jnp.float32)
        total += jnp.dot(heads_ref[...], tile[...], preferred_element_type=jnp.float32)
        if final:
            out_ref, built, sems = refs[0], refs[1 + n], refs[4]
            built[...] = total.astype(out_ref.dtype)
            copies.append(pltpu.make_async_copy(built, out_ref.at[:, cols], sems.at[n]))
            copies[-1].start()
        else:
            refs[0][:, cols] = total
    for copy in copies:
        copy.wait()


def project(final, given, heads, parts):
    tok, cols = given.shape
    vmem = pl.BlockSpec(memory_space=pltpu.VMEM)
    half = parts[0].shape[1] // 2
    scratch = [pltpu.VMEM((tok, n), jnp.bfloat16) for n in (half, half, parts[1].shape[1])]
    scratch += [pltpu.SemaphoreType.DMA((3,))]
    return pl.pallas_call(
        functools.partial(project_kernel, final),
        out_shape=jax.ShapeDtypeStruct(given.shape, jnp.bfloat16 if final else jnp.float32),
        in_specs=[vmem] * 4,
        out_specs=pl.BlockSpec(memory_space=pltpu.HBM) if final else vmem,
        scratch_shapes=scratch if final else [],
        compiler_params=pltpu.CompilerParams(vmem_limit_bytes=16 * 2**20),
        cost_estimate=pl.CostEstimate(
            flops=2 * tok * heads.shape[1] * cols, bytes_accessed=4 * 2**20, transcendentals=0
        ),
    )(given, heads, *parts)


def attention_kernel(stage, distances, n_head, starts_ref, recv_starts_ref, *refs):
    refs = list(refs)
    me = lax.axis_index("ctx")
    pair, core, col = me // 2, me % 2, (me // 2) % 2
    if stage == "first":
        queries_ref, q_recv_ref = refs[:2]
        refs = refs[2:]
    else:
        q_ref, stats_in, acc_in = refs[:3]
        refs = refs[3:]
    n_pieces = len(distances)
    pieces = refs[:n_pieces]
    refs = refs[n_pieces:]
    if stage == "first":
        q_ref, stats_ref, acc_ref, held_ref = refs
    elif stage == "next":
        stats_ref, acc_ref, held_ref = refs
    else:
        out_ref, stats_ref, acc_ref, held_ref = refs
    tok = starts_ref.shape[0] * BLOCK
    half = tok // BLOCK
    blocks = 2 * half
    rows = n_head * BLOCK
    factor = HEAD_SIZE**-0.5 * LOG2E
    tiles = [(b, slice(r, r + TILE)) for b in range(blocks) for r in range(0, rows, TILE)]

    for n, ref in enumerate(pieces):
        held_ref[n, pl.ds(pl.multiple_of(core * tok, tok), tok)] = ref[:tok]
        held_ref[n, pl.ds(pl.multiple_of((1 - core) * tok, tok), tok)] = ref[tok:]

    def start_of(b):
        mine = b // half == core
        return jnp.where(mine, starts_ref[b % half], recv_starts_ref[b % half])

    def rows_of(ref, j, lane0):
        t = slice(j * BLOCK, (j + 1) * BLOCK)
        return jnp.concatenate(
            [ref[t, pl.ds(lane0 + h * HEAD_SIZE, HEAD_SIZE)] for h in range(n_head)], axis=0
        )

    def scores(b, r, i, width):
        k = held_ref[i, :width, :HEAD_SIZE]
        return lax.dot_general(
            q_ref[b, r], k, (((1,), (1,)), ((), ())), preferred_element_type=jnp.float32
        )

    def weigh(p, i, width):
        v = held_ref[i, :width, HEAD_SIZE:]
        v = jnp.concatenate([v, jnp.ones_like(v)], axis=1)
        return jnp.dot(p.astype(jnp.bfloat16), v, preferred_element_type=jnp.float32)

    def keep(s, since):
        k_id = lax.broadcasted_iota(jnp.int32, (1, s.shape[1]), 1)
        return jnp.where(k_id >= since, s, MASKED)

    def both(top, total):
        lane = lax.broadcasted_iota(jnp.int32, total.shape, 1)
        return jnp.where(lane < HEAD_SIZE // 2, top, total)

    def update(i, base, b, r, stats_from, acc_from, to):
        s = keep(scores(b, r, i, 2 * tok), start_of(b) - base)
        stats = stats_from[b, r]
        old = stats[:, :1]
        top = jnp.maximum(old, jnp.max(s, axis=1, keepdims=True))
        p = jnp.exp2(s * factor - top * factor)
        decay = jnp.exp2((old - top) * factor)
        added = weigh(p, i, 2 * tok)
        stats_ref[to, r] = both(top, stats * decay + added[:, HEAD_SIZE:])
        acc_ref[to, r] = acc_from[b, r] * decay + added[:, :HEAD_SIZE]

    def attend_own():
        for j in range(half):
            lanes = pl.multiple_of(core * rows, rows)
            q_ref[core * half + j] = rows_of(queries_ref, j, lanes)
            q_ref[(1 - core) * half + j] = rows_of(q_recv_ref, j, lanes)
        t_id = lax.broadcasted_iota(jnp.int32, (TILE, BLOCK), 0) % BLOCK
        causal = lax.broadcasted_iota(jnp.int32, (TILE, BLOCK), 1) <= t_id
        for b, r in tiles:
            width = (b + 1) * BLOCK
            s = scores(b, r, 0, width)
            since = start_of(b) - pair * 2 * tok
            diag = jnp.where(causal, s[:, b * BLOCK :], MASKED)
            s = jnp.concatenate([keep(s[:, : b * BLOCK], since), diag], 1) if b else diag
            top = jnp.max(s, axis=1, keepdims=True)
            p = jnp.exp2(s * factor - top * factor)
            added = weigh(p, 0, width)
            stats_ref[b, r] = both(top, added[:, HEAD_SIZE:])
            acc_ref[b, r] = added[:, :HEAD_SIZE]

    def attend_next():
        stats_ref[...] = stats_in[...]
        acc_ref[...] = acc_in[...]

        @pl.loop(0, 2 * n_pieces)
        def _(step):
            i, first_block = step // 2, step % 2 * half
            behind = sum(
                jnp.where(i == n, jnp.where(col == 0, *d), 0) for n, d in enumerate(distances)
            )
            base = (pair - behind) * 2 * tok

            @pl.when(start_of(first_block) < base + 2 * tok)
            def _():
                for b, r in tiles[: len(tiles) // 2]:
                    b = first_block + b
                    update(i, base, b, r, stats_ref, acc_ref, b)

    def attend_last(shard):
        first_block = shard * half
        base = (pair - jnp.where(col == 0, *distances[0])) * 2 * tok
        needed = start_of(first_block) < base + 2 * tok

        @pl.when(needed)
        def _():
            for b, r in tiles[: len(tiles) // 2]:
                update(0, base, first_block + b, r, stats_in, acc_in, b)

        @pl.when(jnp.logical_not(needed))
        def _():
            stats_ref[...] = stats_in[pl.ds(first_block, half)]
            acc_ref[...] = acc_in[pl.ds(first_block, half)]

        for j in range(half):
            total = stats_ref[j, :, HEAD_SIZE // 2 : HEAD_SIZE // 2 + 1]
            o = (acc_ref[j] / total).astype(jnp.bfloat16)
            for h in range(n_head):
                out_ref[j * BLOCK : (j + 1) * BLOCK, h * HEAD_SIZE : (h + 1) * HEAD_SIZE] = o[
                    h * BLOCK : (h + 1) * BLOCK
                ]

    if stage == "first":
        attend_own()
    elif stage == "next":
        attend_next()
    else:
        attend_last(core if stage == "own" else 1 - core)


def attention_call(stage, distances, cost, starts, recv_starts, operands):
    tok, half = starts.shape[0] * BLOCK, starts.shape[0]
    rows = operands[1].shape[1] // (2 if stage == "first" else 1)
    blocks, n_head, n_pieces = 2 * half, rows // BLOCK, len(distances)
    state = [jax.ShapeDtypeStruct((blocks, rows, HEAD_SIZE), jnp.float32)] * 2
    scratch = [pltpu.VMEM((n_pieces, 2 * tok, 2 * HEAD_SIZE), jnp.bfloat16)]
    share = n_pieces
    if stage == "first":
        outs, share = [jax.ShapeDtypeStruct((blocks, rows, HEAD_SIZE), jnp.bfloat16)] + state, 0.6
    elif stage == "next":
        outs = state
    else:
        outs, share = [jax.ShapeDtypeStruct((tok, rows), jnp.bfloat16)], 0.5
        scratch = [pltpu.VMEM((half, rows, HEAD_SIZE), jnp.float32)] * 2 + scratch
    vmem, smem = pl.BlockSpec(memory_space=pltpu.VMEM), pl.BlockSpec(memory_space=pltpu.SMEM)
    return pl.pallas_call(
        functools.partial(attention_kernel, stage, distances, n_head),
        out_shape=outs,
        in_specs=[smem, smem] + [vmem] * len(operands),
        out_specs=[vmem] * len(outs),
        scratch_shapes=scratch,
        compiler_params=pltpu.CompilerParams(vmem_limit_bytes=24 * 2**20),
        cost_estimate=pl.CostEstimate(
            flops=int(cost * 1e9),
            bytes_accessed=8 * 2**20,
            transcendentals=int(share * blocks * rows * 2 * tok),
        ),
    )(starts, recv_starts, *operands)


def per_device(queries, keys, values, block_start, out_weight):
    tok, group = queries.shape[0], queries.shape[1] // 2
    me, head = lax.axis_index("ctx"), lax.axis_index("head")
    cols = out_weight.shape[1] // 2
    core = me % 2
    lanes = (core * HEAD_SIZE, (1 - core) * HEAD_SIZE)
    narrow = cols * 3 // 8
    corner = (core * group, (1 - head) * cols + me // 4 % 2 * narrow)
    corners = ((core * group, head * cols), ((1 - core) * group, head * cols))
    keys, lanes, corner, corners = lax.optimization_barrier((keys, lanes, corner, corners))

    def cut(x, start, size):
        return lax.dynamic_slice(x, start, size, allow_negative_indices=False)

    def group_of(n):
        size = (tok, HEAD_SIZE)
        return jnp.concatenate([cut(keys, (0, lanes[n]), size), cut(values, (0, lanes[n]), size)], 1)

    mine, theirs = group_of(0), group_of(1)
    recv, recv_starts = lax.optimization_barrier((swap(theirs, 1), swap(block_start, 1)))
    one_behind = [rotate(mine, 4), rotate(recv, 4)]
    q_recv = swap(queries, 1)
    (own,) = small_call(join_kernel, [(2 * tok, 2 * HEAD_SIZE)], (mine, recv))
    starts = (block_start, recv_starts)
    q_recv, weight = lax.optimization_barrier((q_recv, out_weight))
    sent = cut(weight, corner, (group, cols - narrow))
    q_recv, sent = lax.optimization_barrier((q_recv, sent))
    fetched = cross(sent, 0)
    q, *state = attention_call("first", ((0, 0),), 5, *starts, (queries, q_recv, own))
    q, one_behind = lax.optimization_barrier((q, one_behind))
    (one_behind,) = small_call(join_kernel, [own.shape], one_behind)
    two_behind = shift(one_behind, 4)
    across = swap(one_behind, 2)
    state = attention_call("next", ((2, 2),), 2.1, *starts, (q, *state, one_behind))
    _, ready = lax.optimization_barrier((state[0], two_behind))
    third = swap(small_call(pick_kernel, [own.shape], (own, ready))[0], 2)
    state = attention_call("next", ((1, 3), (4, 4)), 4, *starts, (q, *state, across, two_behind))
    (o_other,) = attention_call("other", ((3, 1),), 2, *starts, (q, *state, third))
    _, fetched = lax.optimization_barrier((o_other, fetched))
    passed = swap(small_call(spare_kernel, [(group, narrow)], (fetched,))[0], 4)
    across_other = cross(o_other, 1)
    swapped_other = swap(o_other, 1)
    (o_own,) = attention_call("own", ((3, 1),), 2, *starts, (q, *state, third))
    across_own = cross(o_own, 0)
    here = sum(
        jnp.dot(o, cut(out_weight, at, (group, cols)), preferred_element_type=jnp.float32)
        for o, at in zip((o_own, swapped_other), corners, strict=True)
    )
    here = here.astype(jnp.bfloat16)
    _, _, _, late = lax.optimization_barrier((here, across_own, across_other, passed))
    other_rows = (swap(fetched, 1), swap(late, 1))
    here = project(False, here, across_own, (fetched, passed))
    return project(True, here, across_other, other_rows)


def solution(mesh):
    in_specs = (P("ctx", "head"), P("ctx", "head"), P("ctx", "head"), P("ctx"), P("head", None))
    out_specs = P("ctx", "head")
    return jax.shard_map(
        per_device, mesh=mesh, in_specs=in_specs, out_specs=out_specs, check_vma=False
    )
```

```python
import functools

import jax
import jax.numpy as jnp
from jax import lax
from jax.experimental import pallas as pl
from jax.experimental.pallas import tpu as pltpu
from jax.sharding import PartitionSpec as P

HEAD_SIZE = 128
BLOCK = 128
LOG2E = 1.4426950408889634
MASKED = -1e30
TILE = 256


def rotate(x, distance):
    n = lax.axis_size("ctx")
    return lax.ppermute(x, "ctx", [(i, (i + distance) % n) for i in range(n)])


def shift(x, distance):
    n = lax.axis_size("ctx")
    return lax.ppermute(x, "ctx", [(i, i + distance) for i in range(n - distance)])


def swap(x, mask):
    return lax.ppermute(x, "ctx", [(i, i ^ mask) for i in range(lax.axis_size("ctx"))])


def cross(x, mask):
    n = lax.axis_size("ctx")
    route = [(2 * i + h, 2 * (i ^ mask) + 1 - h) for i in range(n) for h in range(2)]
    return lax.ppermute(x, ("ctx", "head"), route)


def small_call(kernel, shapes, operands):
    vmem = pl.BlockSpec(memory_space=pltpu.VMEM)
    return pl.pallas_call(
        kernel,
        out_shape=[jax.ShapeDtypeStruct(shape, operands[0].dtype) for shape in shapes],
        in_specs=[vmem] * len(operands),
        out_specs=[vmem] * len(shapes),
        compiler_params=pltpu.CompilerParams(vmem_limit_bytes=6 * 2**20),
        cost_estimate=pl.CostEstimate(flops=2**20, bytes_accessed=2**20, transcendentals=0),
    )(*operands)


def join_kernel(first_ref, second_ref, out_ref):
    tok = first_ref.shape[0]
    out_ref[:tok] = first_ref[...]
    out_ref[tok:] = second_ref[...]


def pick_kernel(even_ref, odd_ref, out_ref):
    odd = lax.axis_index("ctx") // 2 % 2 == 1

    @pl.when(odd)
    def _():
        out_ref[...] = odd_ref[...]

    @pl.when(jnp.logical_not(odd))
    def _():
        out_ref[...] = even_ref[...]


def spare_kernel(window_ref, out_ref):
    fetched = lax.axis_index("ctx") // 4 % 2
    first = fetched * (window_ref.shape[1] - out_ref.shape[1])
    out_ref[...] = window_ref[:, pl.ds(pl.multiple_of(first, HEAD_SIZE), out_ref.shape[1])]


def project_kernel(final, wide, has_window, given_ref, heads_ref, *refs):
    cols_all = given_ref.shape[1]
    narrow = cols_all - wide
    fetched = lax.axis_index("ctx") // 4 % 2
    window_ref, refs = (refs[0], refs[1:]) if has_window else (None, refs)
    n_out = 5 if final else 1
    rest_ref, refs = (refs[0], refs[1:]) if len(refs) > n_out else (None, refs)
    half = -(-wide // 256) * 128
    tiles = (
        (window_ref, 0, half, fetched * narrow),
        (window_ref, half, wide - half, fetched * narrow + half),
        (rest_ref, 0, narrow, (1 - fetched) * wide),
    )
    copies = []
    for n, (ref, start, width, col) in enumerate(tiles):
        cols = pl.ds(pl.multiple_of(col, HEAD_SIZE), width)
        total = given_ref[:, cols].astype(jnp.float32)
        if ref is not None:
            rows = ref[:, start : start + width]
            total += jnp.dot(heads_ref[...], rows, preferred_element_type=jnp.float32)
        if final:
            out_ref, built, sems = refs[0], refs[1 + n], refs[4]
            built[...] = total.astype(out_ref.dtype)
            copies.append(pltpu.make_async_copy(built, out_ref.at[:, cols], sems.at[n]))
            copies[-1].start()
        else:
            refs[0][:, cols] = total
    for copy in copies:
        copy.wait()


def project(final, wide, given, heads, window, rest):
    tok, cols = given.shape
    parts = [x for x in (window, rest) if x is not None]
    vmem = pl.BlockSpec(memory_space=pltpu.VMEM)
    half = -(-wide // 256) * 128
    scratch = [pltpu.VMEM((tok, n), jnp.bfloat16) for n in (half, wide - half, cols - wide)]
    scratch += [pltpu.SemaphoreType.DMA((3,))]
    return pl.pallas_call(
        functools.partial(project_kernel, final, wide, window is not None),
        out_shape=jax.ShapeDtypeStruct(given.shape, jnp.bfloat16 if final else jnp.float32),
        in_specs=[vmem] * (2 + len(parts)),
        out_specs=pl.BlockSpec(memory_space=pltpu.HBM) if final else vmem,
        scratch_shapes=scratch if final else [],
        compiler_params=pltpu.CompilerParams(vmem_limit_bytes=16 * 2**20),
        cost_estimate=pl.CostEstimate(
            flops=2 * tok * heads.shape[1] * cols, bytes_accessed=4 * 2**20, transcendentals=0
        ),
    )(given, heads, *parts)


def attention_kernel(stage, distances, n_head, starts_ref, recv_starts_ref, *refs):
    refs = list(refs)
    me = lax.axis_index("ctx")
    pair, core, col = me // 2, me % 2, (me // 2) % 2
    if stage == "first":
        queries_ref, q_recv_ref = refs[:2]
        refs = refs[2:]
    else:
        q_ref, stats_in, acc_in = refs[:3]
        refs = refs[3:]
    n_pieces = len(distances)
    pieces = refs[:n_pieces]
    refs = refs[n_pieces:]
    if stage == "first":
        q_ref, stats_ref, acc_ref, held_ref = refs
    elif stage == "next":
        stats_ref, acc_ref, held_ref = refs
    else:
        out_ref, stats_ref, acc_ref, held_ref = refs
    tok = starts_ref.shape[0] * BLOCK
    half = tok // BLOCK
    blocks = 2 * half
    rows = n_head * BLOCK
    factor = HEAD_SIZE**-0.5 * LOG2E
    tiles = [(b, slice(r, r + TILE)) for b in range(blocks) for r in range(0, rows, TILE)]

    for n, ref in enumerate(pieces):
        held_ref[n, pl.ds(pl.multiple_of(core * tok, tok), tok)] = ref[:tok]
        held_ref[n, pl.ds(pl.multiple_of((1 - core) * tok, tok), tok)] = ref[tok:]

    def start_of(b):
        mine = b // half == core
        return jnp.where(mine, starts_ref[b % half], recv_starts_ref[b % half])

    def rows_of(ref, j, lane0):
        t = slice(j * BLOCK, (j + 1) * BLOCK)
        return jnp.concatenate(
            [ref[t, pl.ds(lane0 + h * HEAD_SIZE, HEAD_SIZE)] for h in range(n_head)], axis=0
        )

    def scores(b, r, i, width):
        k = held_ref[i, :width, :HEAD_SIZE]
        return lax.dot_general(
            q_ref[b, r], k, (((1,), (1,)), ((), ())), preferred_element_type=jnp.float32
        )

    def weigh(p, i, width):
        v = held_ref[i, :width, HEAD_SIZE:]
        v = jnp.concatenate([v, jnp.ones_like(v)], axis=1)
        return jnp.dot(p.astype(jnp.bfloat16), v, preferred_element_type=jnp.float32)

    def keep(s, since):
        k_id = lax.broadcasted_iota(jnp.int32, (1, s.shape[1]), 1)
        return jnp.where(k_id >= since, s, MASKED)

    def both(top, total):
        lane = lax.broadcasted_iota(jnp.int32, total.shape, 1)
        return jnp.where(lane < HEAD_SIZE // 2, top, total)

    def update(i, base, b, r, stats_from, acc_from, to):
        s = keep(scores(b, r, i, 2 * tok), start_of(b) - base)
        stats = stats_from[b, r]
        old = stats[:, :1]
        top = jnp.maximum(old, jnp.max(s, axis=1, keepdims=True))
        p = jnp.exp2(s * factor - top * factor)
        decay = jnp.exp2((old - top) * factor)
        added = weigh(p, i, 2 * tok)
        stats_ref[to, r] = both(top, stats * decay + added[:, HEAD_SIZE:])
        acc_ref[to, r] = acc_from[b, r] * decay + added[:, :HEAD_SIZE]

    def attend_own():
        for j in range(half):
            lanes = pl.multiple_of(core * rows, rows)
            q_ref[core * half + j] = rows_of(queries_ref, j, lanes)
            q_ref[(1 - core) * half + j] = rows_of(q_recv_ref, j, lanes)
        t_id = lax.broadcasted_iota(jnp.int32, (TILE, BLOCK), 0) % BLOCK
        causal = lax.broadcasted_iota(jnp.int32, (TILE, BLOCK), 1) <= t_id
        for b, r in tiles:
            width = (b + 1) * BLOCK
            s = scores(b, r, 0, width)
            since = start_of(b) - pair * 2 * tok
            diag = jnp.where(causal, s[:, b * BLOCK :], MASKED)
            s = jnp.concatenate([keep(s[:, : b * BLOCK], since), diag], 1) if b else diag
            top = jnp.max(s, axis=1, keepdims=True)
            p = jnp.exp2(s * factor - top * factor)
            added = weigh(p, 0, width)
            stats_ref[b, r] = both(top, added[:, HEAD_SIZE:])
            acc_ref[b, r] = added[:, :HEAD_SIZE]

    def attend_next():
        stats_ref[...] = stats_in[...]
        acc_ref[...] = acc_in[...]

        @pl.loop(0, 2 * n_pieces)
        def _(step):
            i, first_block = step // 2, step % 2 * half
            behind = sum(
                jnp.where(i == n, jnp.where(col == 0, *d), 0) for n, d in enumerate(distances)
            )
            base = (pair - behind) * 2 * tok

            @pl.when(start_of(first_block) < base + 2 * tok)
            def _():
                for b, r in tiles[: len(tiles) // 2]:
                    b = first_block + b
                    update(i, base, b, r, stats_ref, acc_ref, b)

    def attend_last(shard):
        first_block = shard * half
        base = (pair - jnp.where(col == 0, *distances[0])) * 2 * tok
        needed = start_of(first_block) < base + 2 * tok

        @pl.when(needed)
        def _():
            for b, r in tiles[: len(tiles) // 2]:
                update(0, base, first_block + b, r, stats_in, acc_in, b)

        @pl.when(jnp.logical_not(needed))
        def _():
            stats_ref[...] = stats_in[pl.ds(first_block, half)]
            acc_ref[...] = acc_in[pl.ds(first_block, half)]

        for j in range(half):
            total = stats_ref[j, :, HEAD_SIZE // 2 : HEAD_SIZE // 2 + 1]
            o = (acc_ref[j] * (1.0 / total)).astype(jnp.bfloat16)
            for h in range(n_head):
                out_ref[j * BLOCK : (j + 1) * BLOCK, h * HEAD_SIZE : (h + 1) * HEAD_SIZE] = o[
                    h * BLOCK : (h + 1) * BLOCK
                ]

    if stage == "first":
        attend_own()
    elif stage == "next":
        attend_next()
    else:
        attend_last(core if stage == "own" else 1 - core)


def attention_call(stage, distances, cost, starts, recv_starts, operands):
    tok, half = starts.shape[0] * BLOCK, starts.shape[0]
    rows = operands[1].shape[1] // (2 if stage == "first" else 1)
    blocks, n_head, n_pieces = 2 * half, rows // BLOCK, len(distances)
    state = [jax.ShapeDtypeStruct((blocks, rows, HEAD_SIZE), jnp.float32)] * 2
    scratch = [pltpu.VMEM((n_pieces, 2 * tok, 2 * HEAD_SIZE), jnp.bfloat16)]
    share = n_pieces
    if stage == "first":
        outs, share = [jax.ShapeDtypeStruct((blocks, rows, HEAD_SIZE), jnp.bfloat16)] + state, 0.6
    elif stage == "next":
        outs = state
    else:
        outs, share = [jax.ShapeDtypeStruct((tok, rows), jnp.bfloat16)], 0.5
        scratch = [pltpu.VMEM((half, rows, HEAD_SIZE), jnp.float32)] * 2 + scratch
    vmem, smem = pl.BlockSpec(memory_space=pltpu.VMEM), pl.BlockSpec(memory_space=pltpu.SMEM)
    return pl.pallas_call(
        functools.partial(attention_kernel, stage, distances, n_head),
        out_shape=outs,
        in_specs=[smem, smem] + [vmem] * len(operands),
        out_specs=[vmem] * len(outs),
        scratch_shapes=scratch,
        compiler_params=pltpu.CompilerParams(vmem_limit_bytes=24 * 2**20),
        cost_estimate=pl.CostEstimate(
            flops=int(cost * 1e9),
            bytes_accessed=8 * 2**20,
            transcendentals=int(share * blocks * rows * 2 * tok),
        ),
    )(starts, recv_starts, *operands)


def per_device(queries, keys, values, block_start, out_weight):
    tok, group = queries.shape[0], queries.shape[1] // 2
    me, head = lax.axis_index("ctx"), lax.axis_index("head")
    cols = out_weight.shape[1] // 2
    core = me % 2
    lanes = (core * HEAD_SIZE, (1 - core) * HEAD_SIZE)
    narrow = cols * 3 // 8
    corner = (core * group, (1 - head) * cols + me // 4 % 2 * narrow)
    corners = ((core * group, head * cols), ((1 - core) * group, head * cols))
    keys, lanes, corner, corners = lax.optimization_barrier((keys, lanes, corner, corners))

    def cut(x, start, size):
        return lax.dynamic_slice(x, start, size, allow_negative_indices=False)

    def group_of(n):
        size = (tok, HEAD_SIZE)
        return jnp.concatenate([cut(keys, (0, lanes[n]), size), cut(values, (0, lanes[n]), size)], 1)

    mine, theirs = group_of(0), group_of(1)
    recv, recv_starts = lax.optimization_barrier((swap(theirs, 1), swap(block_start, 1)))
    one_behind = [rotate(mine, 4), rotate(recv, 4)]
    q_recv = swap(queries, 1)
    (own,) = small_call(join_kernel, [(2 * tok, 2 * HEAD_SIZE)], (mine, recv))
    starts = (block_start, recv_starts)
    q_recv, weight = lax.optimization_barrier((q_recv, out_weight))
    sent = cut(weight, corner, (group, cols - narrow))
    q_recv, sent = lax.optimization_barrier((q_recv, sent))
    fetched = cross(sent, 0)
    q, *state = attention_call("first", ((0, 0),), 5, *starts, (queries, q_recv, own))
    q, one_behind = lax.optimization_barrier((q, one_behind))
    (one_behind,) = small_call(join_kernel, [own.shape], one_behind)
    two_behind = shift(one_behind, 4)
    across = swap(one_behind, 2)
    state = attention_call("next", ((2, 2),), 2.1, *starts, (q, *state, one_behind))
    _, ready = lax.optimization_barrier((state[0], two_behind))
    third = swap(small_call(pick_kernel, [own.shape], (own, ready))[0], 2)
    state = attention_call("next", ((1, 3), (4, 4)), 4, *starts, (q, *state, across, two_behind))
    (o_other,) = attention_call("other", ((3, 1),), 2, *starts, (q, *state, third))
    _, fetched = lax.optimization_barrier((o_other, fetched))
    passed = swap(small_call(spare_kernel, [(group, narrow)], (fetched,))[0], 4)
    across_other = cross(o_other, 1)
    swapped_other = swap(o_other, 1)
    (o_own,) = attention_call("own", ((3, 1),), 2, *starts, (q, *state, third))
    across_own = cross(o_own, 0)
    here = sum(
        jnp.dot(o, cut(out_weight, at, (group, cols)), preferred_element_type=jnp.float32)
        for o, at in zip((o_own, swapped_other), corners, strict=True)
    )
    here = here.astype(jnp.bfloat16)
    _, _, _, late = lax.optimization_barrier((here, across_own, across_other, passed))
    here = project(False, cols - narrow, here, across_other, swap(fetched, 1), None)
    here = project(False, cols - narrow, here, across_own, fetched, passed)
    return project(True, cols - narrow, here, across_other, None, swap(late, 1))


def solution(mesh):
    in_specs = (P("ctx", "head"), P("ctx", "head"), P("ctx", "head"), P("ctx"), P("head", None))
    out_specs = P("ctx", "head")
    return jax.shard_map(
        per_device, mesh=mesh, in_specs=in_specs, out_specs=out_specs, check_vma=False
    )
```

```python
import functools

import jax
import jax.numpy as jnp
from jax import lax
from jax.experimental import pallas as pl
from jax.experimental.pallas import tpu as pltpu
from jax.sharding import PartitionSpec as P

HEAD_SIZE = 128
BLOCK = 128
LOG2E = 1.4426950408889634
MASKED = -1e30
TILE = 256


def shift(x, distance):
    n = lax.axis_size("ctx")
    return lax.ppermute(x, "ctx", [(i, i + distance) for i in range(n - distance)])


def swap(x, mask):
    return lax.ppermute(x, "ctx", [(i, i ^ mask) for i in range(lax.axis_size("ctx"))])


def cross(x, mask):
    n = lax.axis_size("ctx")
    route = [(2 * i + h, 2 * (i ^ mask) + 1 - h) for i in range(n) for h in range(2)]
    return lax.ppermute(x, ("ctx", "head"), route)


def small_call(kernel, shapes, operands):
    vmem = pl.BlockSpec(memory_space=pltpu.VMEM)
    return pl.pallas_call(
        kernel,
        out_shape=[jax.ShapeDtypeStruct(shape, operands[0].dtype) for shape in shapes],
        in_specs=[vmem] * len(operands),
        out_specs=[vmem] * len(shapes),
        compiler_params=pltpu.CompilerParams(vmem_limit_bytes=6 * 2**20),
        cost_estimate=pl.CostEstimate(flops=2**20, bytes_accessed=2**20, transcendentals=0),
    )(*operands)


def join_kernel(first_ref, second_ref, out_ref):
    tok = first_ref.shape[0]
    out_ref[:tok] = first_ref[...]
    out_ref[tok:] = second_ref[...]


def pick_kernel(even_ref, odd_ref, out_ref):
    odd = lax.axis_index("ctx") // 2 % 2 == 1

    @pl.when(odd)
    def _():
        out_ref[...] = odd_ref[...]

    @pl.when(jnp.logical_not(odd))
    def _():
        out_ref[...] = even_ref[...]


def spare_kernel(window_ref, out_ref):
    fetched = lax.axis_index("ctx") // 4 % 2
    first = fetched * (window_ref.shape[1] - out_ref.shape[1])
    out_ref[...] = window_ref[:, pl.ds(pl.multiple_of(first, HEAD_SIZE), out_ref.shape[1])]


def project_kernel(final, wide, has_window, given_ref, heads_ref, *refs):
    cols_all = given_ref.shape[1]
    narrow = cols_all - wide
    fetched = lax.axis_index("ctx") // 4 % 2
    window_ref, refs = (refs[0], refs[1:]) if has_window else (None, refs)
    n_out = 5 if final else 1
    rest_ref, refs = (refs[0], refs[1:]) if len(refs) > n_out else (None, refs)
    half = -(-wide // 256) * 128
    tiles = (
        (window_ref, 0, half, fetched * narrow),
        (window_ref, half, wide - half, fetched * narrow + half),
        (rest_ref, 0, narrow, (1 - fetched) * wide),
    )
    copies = []
    for n, (ref, start, width, col) in enumerate(tiles):
        cols = pl.ds(pl.multiple_of(col, HEAD_SIZE), width)
        total = given_ref[:, cols].astype(jnp.float32)
        if ref is not None:
            rows = ref[:, start : start + width]
            total += jnp.dot(heads_ref[...], rows, preferred_element_type=jnp.float32)
        if final:
            out_ref, built, sems = refs[0], refs[1 + n], refs[4]
            built[...] = total.astype(out_ref.dtype)
            copies.append(pltpu.make_async_copy(built, out_ref.at[:, cols], sems.at[n]))
            copies[-1].start()
        else:
            refs[0][:, cols] = total
    for copy in copies:
        copy.wait()


def project(final, wide, given, heads, window, rest):
    tok, cols = given.shape
    parts = [x for x in (window, rest) if x is not None]
    vmem = pl.BlockSpec(memory_space=pltpu.VMEM)
    half = -(-wide // 256) * 128
    scratch = [pltpu.VMEM((tok, n), jnp.bfloat16) for n in (half, wide - half, cols - wide)]
    scratch += [pltpu.SemaphoreType.DMA((3,))]
    return pl.pallas_call(
        functools.partial(project_kernel, final, wide, window is not None),
        out_shape=jax.ShapeDtypeStruct(given.shape, jnp.bfloat16 if final else jnp.float32),
        in_specs=[vmem] * (2 + len(parts)),
        out_specs=pl.BlockSpec(memory_space=pltpu.HBM) if final else vmem,
        scratch_shapes=scratch if final else [],
        compiler_params=pltpu.CompilerParams(vmem_limit_bytes=16 * 2**20),
        cost_estimate=pl.CostEstimate(
            flops=2 * tok * heads.shape[1] * cols, bytes_accessed=4 * 2**20, transcendentals=0
        ),
    )(given, heads, *parts)


def attention_kernel(stage, distances, n_head, starts_ref, recv_starts_ref, *refs):
    refs = list(refs)
    me = lax.axis_index("ctx")
    pair, core, col = me // 2, me % 2, (me // 2) % 2
    if stage == "first":
        queries_ref, q_recv_ref = refs[:2]
        refs = refs[2:]
    else:
        q_ref, stats_in, acc_in = refs[:3]
        refs = refs[3:]
    n_pieces = len(distances)
    pieces = refs[:n_pieces]
    refs = refs[n_pieces:]
    if stage == "first":
        q_ref, stats_ref, acc_ref, held_ref = refs
    elif stage == "next":
        stats_ref, acc_ref, held_ref = refs
    else:
        out_ref, stats_ref, acc_ref, held_ref = refs
    tok = starts_ref.shape[0] * BLOCK
    half = tok // BLOCK
    blocks = 2 * half
    rows = n_head * BLOCK
    factor = HEAD_SIZE**-0.5 * LOG2E
    tiles = [(b, slice(r, r + TILE)) for b in range(blocks) for r in range(0, rows, TILE)]

    for n, ref in enumerate(pieces):
        held_ref[n, pl.ds(pl.multiple_of(core * tok, tok), tok)] = ref[:tok]
        held_ref[n, pl.ds(pl.multiple_of((1 - core) * tok, tok), tok)] = ref[tok:]

    def start_of(b):
        mine = b // half == core
        return jnp.where(mine, starts_ref[b % half], recv_starts_ref[b % half])

    def rows_of(ref, j, lane0):
        t = slice(j * BLOCK, (j + 1) * BLOCK)
        return jnp.concatenate(
            [ref[t, pl.ds(lane0 + h * HEAD_SIZE, HEAD_SIZE)] for h in range(n_head)], axis=0
        )

    def scores(b, r, i, width):
        k = held_ref[i, :width, :HEAD_SIZE]
        return lax.dot_general(
            q_ref[b, r], k, (((1,), (1,)), ((), ())), preferred_element_type=jnp.float32
        )

    def weigh(p, i, width):
        v = held_ref[i, :width, HEAD_SIZE:]
        v = jnp.concatenate([v, jnp.ones_like(v)], axis=1)
        return jnp.dot(p.astype(jnp.bfloat16), v, preferred_element_type=jnp.float32)

    def keep(s, since):
        k_id = lax.broadcasted_iota(jnp.int32, (1, s.shape[1]), 1)
        return jnp.where(k_id >= since, s, MASKED)

    def both(top, total):
        lane = lax.broadcasted_iota(jnp.int32, total.shape, 1)
        return jnp.where(lane < HEAD_SIZE // 2, top, total)

    def update(i, base, b, r, stats_from, acc_from, to):
        s = keep(scores(b, r, i, 2 * tok), start_of(b) - base)
        stats = stats_from[b, r]
        old = stats[:, :1]
        top = jnp.maximum(old, jnp.max(s, axis=1, keepdims=True))
        p = jnp.exp2(s * factor - top * factor)
        decay = jnp.exp2((old - top) * factor)
        added = weigh(p, i, 2 * tok)
        stats_ref[to, r] = both(top, stats * decay + added[:, HEAD_SIZE:])
        acc_ref[to, r] = acc_from[b, r] * decay + added[:, :HEAD_SIZE]

    def attend_own():
        for j in range(half):
            lanes = pl.multiple_of(core * rows, rows)
            q_ref[core * half + j] = rows_of(queries_ref, j, lanes)
            q_ref[(1 - core) * half + j] = rows_of(q_recv_ref, j, lanes)
        t_id = lax.broadcasted_iota(jnp.int32, (TILE, BLOCK), 0) % BLOCK
        causal = lax.broadcasted_iota(jnp.int32, (TILE, BLOCK), 1) <= t_id
        for b, r in tiles:
            width = (b + 1) * BLOCK
            s = scores(b, r, 0, width)
            since = start_of(b) - pair * 2 * tok
            diag = jnp.where(causal, s[:, b * BLOCK :], MASKED)
            s = jnp.concatenate([keep(s[:, : b * BLOCK], since), diag], 1) if b else diag
            top = jnp.max(s, axis=1, keepdims=True)
            p = jnp.exp2(s * factor - top * factor)
            added = weigh(p, 0, width)
            stats_ref[b, r] = both(top, added[:, HEAD_SIZE:])
            acc_ref[b, r] = added[:, :HEAD_SIZE]

    def attend_next():
        stats_ref[...] = stats_in[...]
        acc_ref[...] = acc_in[...]

        @pl.loop(0, 2 * n_pieces)
        def _(step):
            i, first_block = step // 2, step % 2 * half
            behind = sum(
                jnp.where(i == n, jnp.where(col == 0, *d), 0) for n, d in enumerate(distances)
            )
            base = (pair - behind) * 2 * tok

            @pl.when(start_of(first_block) < base + 2 * tok)
            def _():
                for b, r in tiles[: len(tiles) // 2]:
                    b = first_block + b
                    update(i, base, b, r, stats_ref, acc_ref, b)

    def attend_last(shard):
        first_block = shard * half
        base = (pair - jnp.where(col == 0, *distances[0])) * 2 * tok
        needed = start_of(first_block) < base + 2 * tok

        @pl.when(needed)
        def _():
            for b, r in tiles[: len(tiles) // 2]:
                update(0, base, first_block + b, r, stats_in, acc_in, b)

        @pl.when(jnp.logical_not(needed))
        def _():
            stats_ref[...] = stats_in[pl.ds(first_block, half)]
            acc_ref[...] = acc_in[pl.ds(first_block, half)]

        for j in range(half):
            total = stats_ref[j, :, HEAD_SIZE // 2 : HEAD_SIZE // 2 + 1]
            o = (acc_ref[j] * (1.0 / total)).astype(jnp.bfloat16)
            for h in range(n_head):
                out_ref[j * BLOCK : (j + 1) * BLOCK, h * HEAD_SIZE : (h + 1) * HEAD_SIZE] = o[
                    h * BLOCK : (h + 1) * BLOCK
                ]

    if stage == "first":
        attend_own()
    elif stage == "next":
        attend_next()
    else:
        attend_last(core if stage == "own" else 1 - core)


def attention_call(stage, distances, cost, starts, recv_starts, operands):
    tok, half = starts.shape[0] * BLOCK, starts.shape[0]
    rows = operands[1].shape[1] // (2 if stage == "first" else 1)
    blocks, n_head, n_pieces = 2 * half, rows // BLOCK, len(distances)
    state = [jax.ShapeDtypeStruct((blocks, rows, HEAD_SIZE), jnp.float32)] * 2
    scratch = [pltpu.VMEM((n_pieces, 2 * tok, 2 * HEAD_SIZE), jnp.bfloat16)]
    share = n_pieces
    if stage == "first":
        outs, share = [jax.ShapeDtypeStruct((blocks, rows, HEAD_SIZE), jnp.bfloat16)] + state, 0.6
    elif stage == "next":
        outs = state
    else:
        outs, share = [jax.ShapeDtypeStruct((tok, rows), jnp.bfloat16)], 0.5
        scratch = [pltpu.VMEM((half, rows, HEAD_SIZE), jnp.float32)] * 2 + scratch
    vmem, smem = pl.BlockSpec(memory_space=pltpu.VMEM), pl.BlockSpec(memory_space=pltpu.SMEM)
    return pl.pallas_call(
        functools.partial(attention_kernel, stage, distances, n_head),
        out_shape=outs,
        in_specs=[smem, smem] + [vmem] * len(operands),
        out_specs=[vmem] * len(outs),
        scratch_shapes=scratch,
        compiler_params=pltpu.CompilerParams(vmem_limit_bytes=24 * 2**20),
        cost_estimate=pl.CostEstimate(
            flops=int(cost * 1e9),
            bytes_accessed=8 * 2**20,
            transcendentals=int(share * blocks * rows * 2 * tok),
        ),
    )(starts, recv_starts, *operands)


def per_device(queries, keys, values, block_start, out_weight):
    tok, group = queries.shape[0], queries.shape[1] // 2
    me, head = lax.axis_index("ctx"), lax.axis_index("head")
    cols = out_weight.shape[1] // 2
    core = me % 2
    lanes = (core * HEAD_SIZE, (1 - core) * HEAD_SIZE)
    narrow = cols * 3 // 8
    corner = (core * group, (1 - head) * cols + me // 4 % 2 * narrow)
    corners = ((core * group, head * cols), ((1 - core) * group, head * cols))
    keys, lanes, corner, corners = lax.optimization_barrier((keys, lanes, corner, corners))

    def cut(x, start, size):
        return lax.dynamic_slice(x, start, size, allow_negative_indices=False)

    def group_of(n):
        size = (tok, HEAD_SIZE)
        return jnp.concatenate([cut(keys, (0, lanes[n]), size), cut(values, (0, lanes[n]), size)], 1)

    mine, theirs = group_of(0), group_of(1)
    recv, recv_starts = lax.optimization_barrier((swap(theirs, 1), swap(block_start, 1)))
    one_behind = [shift(mine, 4), shift(recv, 4)]
    q_recv = swap(queries, 1)
    (own,) = small_call(join_kernel, [(2 * tok, 2 * HEAD_SIZE)], (mine, recv))
    starts = (block_start, recv_starts)
    q_recv, weight = lax.optimization_barrier((q_recv, out_weight))
    sent = cut(weight, corner, (group, cols - narrow))
    q_recv, sent = lax.optimization_barrier((q_recv, sent))
    fetched = cross(sent, 0)
    q, *state = attention_call("first", ((0, 0),), 5, *starts, (queries, q_recv, own))
    q, one_behind = lax.optimization_barrier((q, one_behind))
    (one_behind,) = small_call(join_kernel, [own.shape], one_behind)
    two_behind = shift(one_behind, 4)
    across = swap(one_behind, 2)
    state = attention_call("next", ((2, 2),), 2.1, *starts, (q, *state, one_behind))
    _, ready = lax.optimization_barrier((state[0], two_behind))
    third = swap(small_call(pick_kernel, [own.shape], (own, ready))[0], 2)
    state = attention_call("next", ((1, 3), (4, 4)), 4, *starts, (q, *state, across, two_behind))
    (o_other,) = attention_call("other", ((3, 1),), 2, *starts, (q, *state, third))
    _, fetched = lax.optimization_barrier((o_other, fetched))
    passed = swap(small_call(spare_kernel, [(group, narrow)], (fetched,))[0], 4)
    across_other = cross(o_other, 1)
    swapped_other = swap(o_other, 1)
    (o_own,) = attention_call("own", ((3, 1),), 2, *starts, (q, *state, third))
    across_own = cross(o_own, 0)
    here = sum(
        jnp.dot(o, cut(out_weight, at, (group, cols)), preferred_element_type=jnp.float32)
        for o, at in zip((o_own, swapped_other), corners, strict=True)
    )
    here = here.astype(jnp.bfloat16)
    _, _, _, late = lax.optimization_barrier((here, across_own, across_other, passed))
    here = project(False, cols - narrow, here, across_other, swap(fetched, 1), None)
    here = project(False, cols - narrow, here, across_own, fetched, passed)
    return project(True, cols - narrow, here, across_other, None, swap(late, 1))


def solution(mesh):
    in_specs = (P("ctx", "head"), P("ctx", "head"), P("ctx", "head"), P("ctx"), P("head", None))
    out_specs = P("ctx", "head")
    return jax.shard_map(
        per_device, mesh=mesh, in_specs=in_specs, out_specs=out_specs, check_vma=False
    )
```

```python
import functools
import math

import jax
import jax.numpy as jnp
from jax import lax
from jax.experimental import pallas as pl
from jax.experimental.pallas import tpu as pltpu
from jax.sharding import PartitionSpec as P

HEAD_SIZE = 128
BLOCK = 128
LOG2E = 1.4426950408889634
MASKED = -math.inf
TILE = 256


def rotate(x, distance):
    n = lax.axis_size("ctx")
    return lax.ppermute(x, "ctx", [(i, (i + distance) % n) for i in range(n)])


def shift(x, distance):
    n = lax.axis_size("ctx")
    return lax.ppermute(x, "ctx", [(i, i + distance) for i in range(n - distance)])


def swap(x, mask):
    return lax.ppermute(x, "ctx", [(i, i ^ mask) for i in range(lax.axis_size("ctx"))])


def cross(x, mask):
    n = lax.axis_size("ctx")
    route = [(2 * i + h, 2 * (i ^ mask) + 1 - h) for i in range(n) for h in range(2)]
    return lax.ppermute(x, ("ctx", "head"), route)


def small_call(kernel, shapes, operands):
    vmem = pl.BlockSpec(memory_space=pltpu.VMEM)
    return pl.pallas_call(
        kernel,
        out_shape=[jax.ShapeDtypeStruct(shape, operands[0].dtype) for shape in shapes],
        in_specs=[vmem] * len(operands),
        out_specs=[vmem] * len(shapes),
        compiler_params=pltpu.CompilerParams(vmem_limit_bytes=6 * 2**20),
        cost_estimate=pl.CostEstimate(flops=2**20, bytes_accessed=2**20, transcendentals=0),
    )(*operands)


def join_kernel(first_ref, second_ref, out_ref):
    tok = first_ref.shape[0]
    out_ref[:tok] = first_ref[...]
    out_ref[tok:] = second_ref[...]


def pick_kernel(even_ref, odd_ref, out_ref):
    odd = lax.axis_index("ctx") // 2 % 2 == 1

    @pl.when(odd)
    def _():
        out_ref[...] = odd_ref[...]

    @pl.when(jnp.logical_not(odd))
    def _():
        out_ref[...] = even_ref[...]


def spare_kernel(window_ref, out_ref):
    fetched = lax.axis_index("ctx") // 4 % 2
    first = fetched * (window_ref.shape[1] - out_ref.shape[1])
    out_ref[...] = window_ref[:, pl.ds(pl.multiple_of(first, HEAD_SIZE), out_ref.shape[1])]


def project_kernel(final, wide, has_window, given_ref, heads_ref, *refs):
    cols_all = given_ref.shape[1]
    narrow = cols_all - wide
    fetched = lax.axis_index("ctx") // 4 % 2
    window_ref, refs = (refs[0], refs[1:]) if has_window else (None, refs)
    n_out = 5 if final else 1
    rest_ref, refs = (refs[0], refs[1:]) if len(refs) > n_out else (None, refs)
    half = -(-wide // 256) * 128
    tiles = (
        (window_ref, 0, half, fetched * narrow),
        (window_ref, half, wide - half, fetched * narrow + half),
        (rest_ref, 0, narrow, (1 - fetched) * wide),
    )
    copies = []
    for n, (ref, start, width, col) in enumerate(tiles):
        cols = pl.ds(pl.multiple_of(col, HEAD_SIZE), width)
        total = given_ref[:, cols].astype(jnp.float32)
        if ref is not None:
            rows = ref[:, start : start + width]
            total += jnp.dot(heads_ref[...], rows, preferred_element_type=jnp.float32)
        if final:
            out_ref, built, sems = refs[0], refs[1 + n], refs[4]
            built[...] = total.astype(out_ref.dtype)
            copies.append(pltpu.make_async_copy(built, out_ref.at[:, cols], sems.at[n]))
            copies[-1].start()
        else:
            refs[0][:, cols] = total
    for copy in copies:
        copy.wait()


def project(final, wide, given, heads, window, rest):
    tok, cols = given.shape
    parts = [x for x in (window, rest) if x is not None]
    vmem = pl.BlockSpec(memory_space=pltpu.VMEM)
    half = -(-wide // 256) * 128
    scratch = [pltpu.VMEM((tok, n), jnp.bfloat16) for n in (half, wide - half, cols - wide)]
    scratch += [pltpu.SemaphoreType.DMA((3,))]
    return pl.pallas_call(
        functools.partial(project_kernel, final, wide, window is not None),
        out_shape=jax.ShapeDtypeStruct(given.shape, jnp.bfloat16 if final else jnp.float32),
        in_specs=[vmem] * (2 + len(parts)),
        out_specs=pl.BlockSpec(memory_space=pltpu.HBM) if final else vmem,
        scratch_shapes=scratch if final else [],
        compiler_params=pltpu.CompilerParams(vmem_limit_bytes=16 * 2**20),
        cost_estimate=pl.CostEstimate(
            flops=2 * tok * heads.shape[1] * cols, bytes_accessed=4 * 2**20, transcendentals=0
        ),
    )(given, heads, *parts)


def attention_kernel(stage, distances, n_head, starts_ref, recv_starts_ref, *refs):
    refs = list(refs)
    me = lax.axis_index("ctx")
    pair, core, col = me // 2, me % 2, (me // 2) % 2
    if stage == "first":
        queries_ref, q_recv_ref = refs[:2]
        refs = refs[2:]
    else:
        q_ref, stats_in, acc_in = refs[:3]
        refs = refs[3:]
    n_pieces = len(distances)
    pieces = refs[:n_pieces]
    refs = refs[n_pieces:]
    if stage == "first":
        q_ref, stats_ref, acc_ref, held_ref = refs
    elif stage == "next":
        stats_ref, acc_ref, held_ref = refs
    else:
        out_ref, stats_ref, acc_ref, held_ref = refs
    tok = starts_ref.shape[0] * BLOCK
    half = tok // BLOCK
    blocks = 2 * half
    rows = n_head * BLOCK
    factor = HEAD_SIZE**-0.5 * LOG2E
    tiles = [(b, slice(r, r + TILE)) for b in range(blocks) for r in range(0, rows, TILE)]

    for n, ref in enumerate(pieces):
        held_ref[n, pl.ds(pl.multiple_of(core * tok, tok), tok)] = ref[:tok]
        held_ref[n, pl.ds(pl.multiple_of((1 - core) * tok, tok), tok)] = ref[tok:]

    def start_of(b):
        mine = b // half == core
        return jnp.where(mine, starts_ref[b % half], recv_starts_ref[b % half])

    def rows_of(ref, j, lane0):
        t = slice(j * BLOCK, (j + 1) * BLOCK)
        return jnp.concatenate(
            [ref[t, pl.ds(lane0 + h * HEAD_SIZE, HEAD_SIZE)] for h in range(n_head)], axis=0
        )

    def scores(b, r, i, width):
        k = held_ref[i, :width, :HEAD_SIZE]
        return lax.dot_general(
            q_ref[b, r], k, (((1,), (1,)), ((), ())), preferred_element_type=jnp.float32
        )

    def weigh(p, i, width):
        v = held_ref[i, :width, HEAD_SIZE:]
        v = jnp.concatenate([v, jnp.ones_like(v)], axis=1)
        return jnp.dot(p.astype(jnp.bfloat16), v, preferred_element_type=jnp.float32)

    def keep(s, since):
        k_id = lax.broadcasted_iota(jnp.int32, (1, s.shape[1]), 1)
        return jnp.where(k_id >= since, s, MASKED)

    def both(top, total):
        lane = lax.broadcasted_iota(jnp.int32, total.shape, 1)
        return jnp.where(lane < HEAD_SIZE // 2, top, total)

    def update(i, base, b, r, stats_from, acc_from, to):
        s = keep(scores(b, r, i, 2 * tok), start_of(b) - base)
        stats = stats_from[b, r]
        old = stats[:, :1]
        top = jnp.maximum(old, jnp.max(s, axis=1, keepdims=True))
        p = jnp.exp2(s * factor - top * factor)
        decay = jnp.exp2((old - top) * factor)
        added = weigh(p, i, 2 * tok)
        stats_ref[to, r] = both(top, stats * decay + added[:, HEAD_SIZE:])
        acc_ref[to, r] = acc_from[b, r] * decay + added[:, :HEAD_SIZE]

    def attend_own():
        for j in range(half):
            lanes = pl.multiple_of(core * rows, rows)
            q_ref[core * half + j] = rows_of(queries_ref, j, lanes)
            q_ref[(1 - core) * half + j] = rows_of(q_recv_ref, j, lanes)
        t_id = lax.broadcasted_iota(jnp.int32, (TILE, BLOCK), 0) % BLOCK
        causal = lax.broadcasted_iota(jnp.int32, (TILE, BLOCK), 1) <= t_id
        for b, r in tiles:
            width = (b + 1) * BLOCK
            s = scores(b, r, 0, width)
            since = start_of(b) - pair * 2 * tok
            diag = jnp.where(causal, s[:, b * BLOCK :], MASKED)
            s = jnp.concatenate([keep(s[:, : b * BLOCK], since), diag], 1) if b else diag
            top = jnp.max(s, axis=1, keepdims=True)
            p = jnp.exp2(s * factor - top * factor)
            added = weigh(p, 0, width)
            stats_ref[b, r] = both(top, added[:, HEAD_SIZE:])
            acc_ref[b, r] = added[:, :HEAD_SIZE]

    def attend_next():
        stats_ref[...] = stats_in[...]
        acc_ref[...] = acc_in[...]

        @pl.loop(0, 2 * n_pieces)
        def _(step):
            i, first_block = step // 2, step % 2 * half
            behind = sum(
                jnp.where(i == n, jnp.where(col == 0, *d), 0) for n, d in enumerate(distances)
            )
            base = (pair - behind) * 2 * tok

            @pl.when(start_of(first_block) < base + 2 * tok)
            def _():
                for b, r in tiles[: len(tiles) // 2]:
                    b = first_block + b
                    update(i, base, b, r, stats_ref, acc_ref, b)

    def attend_last(shard):
        first_block = shard * half
        base = (pair - jnp.where(col == 0, *distances[0])) * 2 * tok
        needed = start_of(first_block) < base + 2 * tok

        @pl.when(needed)
        def _():
            for b, r in tiles[: len(tiles) // 2]:
                update(0, base, first_block + b, r, stats_in, acc_in, b)

        @pl.when(jnp.logical_not(needed))
        def _():
            stats_ref[...] = stats_in[pl.ds(first_block, half)]
            acc_ref[...] = acc_in[pl.ds(first_block, half)]

        for j in range(half):
            total = stats_ref[j, :, HEAD_SIZE // 2 : HEAD_SIZE // 2 + 1]
            o = (acc_ref[j] * (1.0 / total)).astype(jnp.bfloat16)
            for h in range(n_head):
                out_ref[j * BLOCK : (j + 1) * BLOCK, h * HEAD_SIZE : (h + 1) * HEAD_SIZE] = o[
                    h * BLOCK : (h + 1) * BLOCK
                ]

    if stage == "first":
        attend_own()
    elif stage == "next":
        attend_next()
    else:
        attend_last(core if stage == "own" else 1 - core)


def attention_call(stage, distances, cost, starts, recv_starts, operands):
    tok, half = starts.shape[0] * BLOCK, starts.shape[0]
    rows = operands[1].shape[1] // (2 if stage == "first" else 1)
    blocks, n_head, n_pieces = 2 * half, rows // BLOCK, len(distances)
    state = [jax.ShapeDtypeStruct((blocks, rows, HEAD_SIZE), jnp.float32)] * 2
    scratch = [pltpu.VMEM((n_pieces, 2 * tok, 2 * HEAD_SIZE), jnp.bfloat16)]
    share = n_pieces
    if stage == "first":
        outs, share = [jax.ShapeDtypeStruct((blocks, rows, HEAD_SIZE), jnp.bfloat16)] + state, 0.6
    elif stage == "next":
        outs = state
    else:
        outs, share = [jax.ShapeDtypeStruct((tok, rows), jnp.bfloat16)], 0.5
        scratch = [pltpu.VMEM((half, rows, HEAD_SIZE), jnp.float32)] * 2 + scratch
    vmem, smem = pl.BlockSpec(memory_space=pltpu.VMEM), pl.BlockSpec(memory_space=pltpu.SMEM)
    return pl.pallas_call(
        functools.partial(attention_kernel, stage, distances, n_head),
        out_shape=outs,
        in_specs=[smem, smem] + [vmem] * len(operands),
        out_specs=[vmem] * len(outs),
        scratch_shapes=scratch,
        compiler_params=pltpu.CompilerParams(vmem_limit_bytes=24 * 2**20),
        cost_estimate=pl.CostEstimate(
            flops=int(cost * 1e9),
            bytes_accessed=8 * 2**20,
            transcendentals=int(share * blocks * rows * 2 * tok),
        ),
    )(starts, recv_starts, *operands)


def per_device(queries, keys, values, block_start, out_weight):
    tok, group = queries.shape[0], queries.shape[1] // 2
    me, head = lax.axis_index("ctx"), lax.axis_index("head")
    cols = out_weight.shape[1] // 2
    core = me % 2
    lanes = (core * HEAD_SIZE, (1 - core) * HEAD_SIZE)
    narrow = cols * 3 // 8
    corner = (core * group, (1 - head) * cols + me // 4 % 2 * narrow)
    corners = ((core * group, head * cols), ((1 - core) * group, head * cols))
    keys, lanes, corner, corners = lax.optimization_barrier((keys, lanes, corner, corners))

    def cut(x, start, size):
        return lax.dynamic_slice(x, start, size, allow_negative_indices=False)

    def group_of(n):
        size = (tok, HEAD_SIZE)
        return jnp.concatenate([cut(keys, (0, lanes[n]), size), cut(values, (0, lanes[n]), size)], 1)

    mine, theirs = group_of(0), group_of(1)
    recv, recv_starts = lax.optimization_barrier((swap(theirs, 1), swap(block_start, 1)))
    one_behind = [rotate(mine, 4), rotate(recv, 4)]
    q_recv = swap(queries, 1)
    (own,) = small_call(join_kernel, [(2 * tok, 2 * HEAD_SIZE)], (mine, recv))
    starts = (block_start, recv_starts)
    q_recv, weight = lax.optimization_barrier((q_recv, out_weight))
    sent = cut(weight, corner, (group, cols - narrow))
    q_recv, sent = lax.optimization_barrier((q_recv, sent))
    fetched = cross(sent, 0)
    q, *state = attention_call("first", ((0, 0),), 5, *starts, (queries, q_recv, own))
    q, one_behind = lax.optimization_barrier((q, one_behind))
    (one_behind,) = small_call(join_kernel, [own.shape], one_behind)
    two_behind = shift(one_behind, 4)
    across = swap(one_behind, 2)
    state = attention_call("next", ((2, 2),), 2.1, *starts, (q, *state, one_behind))
    _, ready = lax.optimization_barrier((state[0], two_behind))
    third = swap(small_call(pick_kernel, [own.shape], (own, ready))[0], 2)
    state = attention_call("next", ((1, 3), (4, 4)), 4, *starts, (q, *state, across, two_behind))
    (o_other,) = attention_call("other", ((3, 1),), 2, *starts, (q, *state, third))
    _, fetched = lax.optimization_barrier((o_other, fetched))
    passed = swap(small_call(spare_kernel, [(group, narrow)], (fetched,))[0], 4)
    across_other = cross(o_other, 1)
    swapped_other = swap(o_other, 1)
    (o_own,) = attention_call("own", ((3, 1),), 2, *starts, (q, *state, third))
    across_own = cross(o_own, 0)
    here = sum(
        jnp.dot(o, cut(out_weight, at, (group, cols)), preferred_element_type=jnp.float32)
        for o, at in zip((o_own, swapped_other), corners, strict=True)
    )
    here = here.astype(jnp.bfloat16)
    _, _, _, late = lax.optimization_barrier((here, across_own, across_other, passed))
    here = project(False, cols - narrow, here, across_other, swap(fetched, 1), None)
    here = project(False, cols - narrow, here, across_own, fetched, passed)
    return project(True, cols - narrow, here, across_other, None, swap(late, 1))


def solution(mesh):
    in_specs = (P("ctx", "head"), P("ctx", "head"), P("ctx", "head"), P("ctx"), P("head", None))
    out_specs = P("ctx", "head")
    return jax.shard_map(
        per_device, mesh=mesh, in_specs=in_specs, out_specs=out_specs, check_vma=False
    )
```

```python
import functools
import math

import jax
import jax.numpy as jnp
from jax import lax
from jax.experimental import pallas as pl
from jax.experimental.pallas import tpu as pltpu
from jax.sharding import PartitionSpec as P

HEAD_SIZE = 128
BLOCK = 128
LOG2E = 1.4426950408889634
MASKED = -math.inf
TILE = 256


def rotate(x, distance):
    n = lax.axis_size("ctx")
    return lax.ppermute(x, "ctx", [(i, (i + distance) % n) for i in range(n)])


def shift(x, distance):
    n = lax.axis_size("ctx")
    return lax.ppermute(x, "ctx", [(i, i + distance) for i in range(n - distance)])


def swap(x, mask):
    return lax.ppermute(x, "ctx", [(i, i ^ mask) for i in range(lax.axis_size("ctx"))])


def cross(x, mask):
    n = lax.axis_size("ctx")
    route = [(2 * i + h, 2 * (i ^ mask) + 1 - h) for i in range(n) for h in range(2)]
    return lax.ppermute(x, ("ctx", "head"), route)


def small_call(kernel, shapes, operands):
    vmem = pl.BlockSpec(memory_space=pltpu.VMEM)
    return pl.pallas_call(
        kernel,
        out_shape=[jax.ShapeDtypeStruct(shape, operands[0].dtype) for shape in shapes],
        in_specs=[vmem] * len(operands),
        out_specs=[vmem] * len(shapes),
        compiler_params=pltpu.CompilerParams(vmem_limit_bytes=6 * 2**20),
        cost_estimate=pl.CostEstimate(flops=2**20, bytes_accessed=2**20, transcendentals=0),
    )(*operands)


def join_kernel(first_ref, second_ref, out_ref):
    tok = first_ref.shape[0]
    out_ref[:tok] = first_ref[...]
    out_ref[tok:] = second_ref[...]


def pick_kernel(even_ref, odd_ref, out_ref):
    odd = lax.axis_index("ctx") // 2 % 2 == 1

    @pl.when(odd)
    def _():
        out_ref[...] = odd_ref[...]

    @pl.when(jnp.logical_not(odd))
    def _():
        out_ref[...] = even_ref[...]


def spare_kernel(window_ref, out_ref):
    fetched = lax.axis_index("ctx") // 4 % 2
    first = fetched * (window_ref.shape[1] - out_ref.shape[1])
    out_ref[...] = window_ref[:, pl.ds(pl.multiple_of(first, HEAD_SIZE), out_ref.shape[1])]


def project_kernel(final, wide, has_window, given_ref, heads_ref, *refs):
    cols_all = given_ref.shape[1]
    narrow = cols_all - wide
    fetched = lax.axis_index("ctx") // 4 % 2
    window_ref, refs = (refs[0], refs[1:]) if has_window else (None, refs)
    n_out = 5 if final else 1
    rest_ref, refs = (refs[0], refs[1:]) if len(refs) > n_out else (None, refs)
    half = -(-wide // 256) * 128
    tiles = (
        (window_ref, 0, half, fetched * narrow),
        (window_ref, half, wide - half, fetched * narrow + half),
        (rest_ref, 0, narrow, (1 - fetched) * wide),
    )
    copies = []
    for n, (ref, start, width, col) in enumerate(tiles):
        cols = pl.ds(pl.multiple_of(col, HEAD_SIZE), width)
        total = given_ref[:, cols].astype(jnp.float32)
        if ref is not None:
            rows = ref[:, start : start + width]
            total += jnp.dot(heads_ref[...], rows, preferred_element_type=jnp.float32)
        if final:
            out_ref, built, sems = refs[0], refs[1 + n], refs[4]
            built[...] = total.astype(out_ref.dtype)
            copies.append(pltpu.make_async_copy(built, out_ref.at[:, cols], sems.at[n]))
            copies[-1].start()
        else:
            refs[0][:, cols] = total
    for copy in copies:
        copy.wait()


def project(final, wide, given, heads, window, rest):
    tok, cols = given.shape
    parts = [x for x in (window, rest) if x is not None]
    vmem = pl.BlockSpec(memory_space=pltpu.VMEM)
    half = -(-wide // 256) * 128
    scratch = [pltpu.VMEM((tok, n), jnp.bfloat16) for n in (half, wide - half, cols - wide)]
    scratch += [pltpu.SemaphoreType.DMA((3,))]
    return pl.pallas_call(
        functools.partial(project_kernel, final, wide, window is not None),
        out_shape=jax.ShapeDtypeStruct(given.shape, jnp.bfloat16 if final else jnp.float32),
        in_specs=[vmem] * (2 + len(parts)),
        out_specs=pl.BlockSpec(memory_space=pltpu.HBM) if final else vmem,
        scratch_shapes=scratch if final else [],
        compiler_params=pltpu.CompilerParams(vmem_limit_bytes=16 * 2**20),
        cost_estimate=pl.CostEstimate(
            flops=2 * tok * heads.shape[1] * cols, bytes_accessed=4 * 2**20, transcendentals=0
        ),
    )(given, heads, *parts)


def attention_kernel(stage, distances, n_head, starts_ref, recv_starts_ref, *refs):
    refs = list(refs)
    me = lax.axis_index("ctx")
    pair, core, col = me // 2, me % 2, (me // 2) % 2
    if stage == "first":
        queries_ref, q_recv_ref = refs[:2]
        refs = refs[2:]
    else:
        q_ref, stats_in, acc_in = refs[:3]
        refs = refs[3:]
    n_pieces = len(distances)
    pieces = refs[:n_pieces]
    refs = refs[n_pieces:]
    if stage == "first":
        q_ref, stats_ref, acc_ref, held_ref = refs
    elif stage == "next":
        stats_ref, acc_ref, held_ref = refs
    else:
        out_ref, stats_ref, acc_ref, held_ref = refs
    tok = starts_ref.shape[0] * BLOCK
    half = tok // BLOCK
    blocks = 2 * half
    rows = n_head * BLOCK
    factor = HEAD_SIZE**-0.5 * LOG2E
    tiles = [(b, slice(r, r + TILE)) for b in range(blocks) for r in range(0, rows, TILE)]

    for n, ref in enumerate(pieces):
        held_ref[n, pl.ds(pl.multiple_of(core * tok, tok), tok)] = ref[:tok]
        held_ref[n, pl.ds(pl.multiple_of((1 - core) * tok, tok), tok)] = ref[tok:]

    def start_of(b):
        mine = b // half == core
        return jnp.where(mine, starts_ref[b % half], recv_starts_ref[b % half])

    def rows_of(ref, j, lane0):
        t = slice(j * BLOCK, (j + 1) * BLOCK)
        return jnp.concatenate(
            [ref[t, pl.ds(lane0 + h * HEAD_SIZE, HEAD_SIZE)] for h in range(n_head)], axis=0
        )

    def scores(b, r, i, width):
        k = held_ref[i, :width, :HEAD_SIZE]
        return lax.dot_general(
            q_ref[b, r], k, (((1,), (1,)), ((), ())), preferred_element_type=jnp.float32
        )

    def weigh(p, i, width):
        v = held_ref[i, :width, HEAD_SIZE:]
        v = jnp.concatenate([v, jnp.ones_like(v)], axis=1)
        return jnp.dot(p.astype(jnp.bfloat16), v, preferred_element_type=jnp.float32)

    def keep(s, since):
        k_id = lax.broadcasted_iota(jnp.int32, (1, s.shape[1]), 1)
        return jnp.where(k_id >= since, s, MASKED)

    def both(top, total):
        lane = lax.broadcasted_iota(jnp.int32, total.shape, 1)
        return jnp.where(lane < HEAD_SIZE // 2, top, total)

    def update(i, base, b, r, stats_from, acc_from, to):
        s = keep(scores(b, r, i, 2 * tok), start_of(b) - base)
        stats = stats_from[b, r]
        old = stats[:, :1]
        top = jnp.maximum(old, jnp.max(s, axis=1, keepdims=True))
        p = jnp.exp2(s * factor - top * factor)
        decay = jnp.exp2((old - top) * factor)
        added = weigh(p, i, 2 * tok)
        stats_ref[to, r] = both(top, stats * decay + added[:, HEAD_SIZE:])
        acc_ref[to, r] = acc_from[b, r] * decay + added[:, :HEAD_SIZE]

    def attend_own():
        for j in range(half):
            lanes = pl.multiple_of(core * rows, rows)
            q_ref[core * half + j] = rows_of(queries_ref, j, lanes)
            q_ref[(1 - core) * half + j] = rows_of(q_recv_ref, j, lanes)
        t_id = lax.broadcasted_iota(jnp.int32, (TILE, BLOCK), 0) % BLOCK
        causal = lax.broadcasted_iota(jnp.int32, (TILE, BLOCK), 1) <= t_id
        for b, r in tiles:
            width = (b + 1) * BLOCK
            s = scores(b, r, 0, width)
            since = start_of(b) - pair * 2 * tok
            diag = jnp.where(causal, s[:, b * BLOCK :], MASKED)
            s = jnp.concatenate([keep(s[:, : b * BLOCK], since), diag], 1) if b else diag
            top = jnp.max(s, axis=1, keepdims=True)
            p = jnp.exp2(s * factor - top * factor)
            added = weigh(p, 0, width)
            stats_ref[b, r] = both(top, added[:, HEAD_SIZE:])
            acc_ref[b, r] = added[:, :HEAD_SIZE]

    def attend_next():
        stats_ref[...] = stats_in[...]
        acc_ref[...] = acc_in[...]

        @pl.loop(0, 2 * n_pieces)
        def _(step):
            i, first_block = step // 2, step % 2 * half
            behind = sum(
                jnp.where(i == n, jnp.where(col == 0, *d), 0) for n, d in enumerate(distances)
            )
            base = (pair - behind) * 2 * tok

            @pl.when(start_of(first_block) < base + 2 * tok)
            def _():
                for b, r in tiles[: len(tiles) // 2]:
                    b = first_block + b
                    update(i, base, b, r, stats_ref, acc_ref, b)

    def attend_last(shard):
        first_block = shard * half
        base = (pair - jnp.where(col == 0, *distances[0])) * 2 * tok
        needed = start_of(first_block) < base + 2 * tok

        @pl.when(needed)
        def _():
            for b, r in tiles[: len(tiles) // 2]:
                update(0, base, first_block + b, r, stats_in, acc_in, b)

        @pl.when(jnp.logical_not(needed))
        def _():
            stats_ref[...] = stats_in[pl.ds(first_block, half)]
            acc_ref[...] = acc_in[pl.ds(first_block, half)]

        for j in range(half):
            total = stats_ref[j, :, HEAD_SIZE // 2 : HEAD_SIZE // 2 + 1]
            o = (acc_ref[j] * (1.0 / total)).astype(jnp.bfloat16)
            for h in range(n_head):
                out_ref[j * BLOCK : (j + 1) * BLOCK, h * HEAD_SIZE : (h + 1) * HEAD_SIZE] = o[
                    h * BLOCK : (h + 1) * BLOCK
                ]

    if stage == "first":
        attend_own()
    elif stage == "next":
        attend_next()
    else:
        attend_last(core if stage == "own" else 1 - core)


def attention_call(stage, distances, cost, starts, recv_starts, operands):
    tok, half = starts.shape[0] * BLOCK, starts.shape[0]
    rows = operands[1].shape[1] // (2 if stage == "first" else 1)
    blocks, n_head, n_pieces = 2 * half, rows // BLOCK, len(distances)
    state = [jax.ShapeDtypeStruct((blocks, rows, HEAD_SIZE), jnp.float32)] * 2
    scratch = [pltpu.VMEM((n_pieces, 2 * tok, 2 * HEAD_SIZE), jnp.bfloat16)]
    share = n_pieces
    if stage == "first":
        outs, share = [jax.ShapeDtypeStruct((blocks, rows, HEAD_SIZE), jnp.bfloat16)] + state, 0.6
    elif stage == "next":
        outs = state
    else:
        outs, share = [jax.ShapeDtypeStruct((tok, rows), jnp.bfloat16)], 0.5
        scratch = [pltpu.VMEM((half, rows, HEAD_SIZE), jnp.float32)] * 2 + scratch
    vmem, smem = pl.BlockSpec(memory_space=pltpu.VMEM), pl.BlockSpec(memory_space=pltpu.SMEM)
    return pl.pallas_call(
        functools.partial(attention_kernel, stage, distances, n_head),
        out_shape=outs,
        in_specs=[smem, smem] + [vmem] * len(operands),
        out_specs=[vmem] * len(outs),
        scratch_shapes=scratch,
        compiler_params=pltpu.CompilerParams(vmem_limit_bytes=24 * 2**20),
        cost_estimate=pl.CostEstimate(
            flops=int(cost * 1e9),
            bytes_accessed=8 * 2**20,
            transcendentals=int(share * blocks * rows * 2 * tok),
        ),
    )(starts, recv_starts, *operands)


def per_device(queries, keys, values, block_start, out_weight):
    tok, group = queries.shape[0], queries.shape[1] // 2
    me, head = lax.axis_index("ctx"), lax.axis_index("head")
    cols = out_weight.shape[1] // 2
    core = me % 2
    lanes = (core * HEAD_SIZE, (1 - core) * HEAD_SIZE)
    narrow = cols * 3 // 8
    corner = (core * group, (1 - head) * cols + me // 4 % 2 * narrow)
    corners = ((core * group, head * cols), ((1 - core) * group, head * cols))
    keys, lanes, corner, corners = lax.optimization_barrier((keys, lanes, corner, corners))

    def cut(x, start, size):
        return lax.dynamic_slice(x, start, size, allow_negative_indices=False)

    def group_of(n, *both):
        size = (tok, HEAD_SIZE)
        return jnp.concatenate([cut(x, (0, lanes[n]), size) for x in both], 1)

    mine = group_of(0, keys, values)
    _, *later = lax.optimization_barrier((mine, keys, values))
    theirs = group_of(1, *later)
    recv, recv_starts = lax.optimization_barrier((swap(theirs, 1), swap(block_start, 1)))
    one_behind = [rotate(mine, 4), rotate(recv, 4)]
    q_recv = swap(queries, 1)
    (own,) = small_call(join_kernel, [(2 * tok, 2 * HEAD_SIZE)], (mine, recv))
    starts = (block_start, recv_starts)
    q_recv, weight = lax.optimization_barrier((q_recv, out_weight))
    sent = cut(weight, corner, (group, cols - narrow))
    q_recv, sent = lax.optimization_barrier((q_recv, sent))
    fetched = cross(sent, 0)
    q, *state = attention_call("first", ((0, 0),), 5, *starts, (queries, q_recv, own))
    q, one_behind = lax.optimization_barrier((q, one_behind))
    (one_behind,) = small_call(join_kernel, [own.shape], one_behind)
    two_behind = shift(one_behind, 4)
    across = swap(one_behind, 2)
    state = attention_call("next", ((2, 2),), 2.1, *starts, (q, *state, one_behind))
    _, ready = lax.optimization_barrier((state[0], two_behind))
    third = swap(small_call(pick_kernel, [own.shape], (own, ready))[0], 2)
    state = attention_call("next", ((1, 3), (4, 4)), 4, *starts, (q, *state, across, two_behind))
    (o_other,) = attention_call("other", ((3, 1),), 2, *starts, (q, *state, third))
    _, fetched = lax.optimization_barrier((o_other, fetched))
    passed = swap(small_call(spare_kernel, [(group, narrow)], (fetched,))[0], 4)
    across_other = cross(o_other, 1)
    swapped_other = swap(o_other, 1)
    (o_own,) = attention_call("own", ((3, 1),), 2, *starts, (q, *state, third))
    across_own = cross(o_own, 0)
    here = sum(
        jnp.dot(o, cut(out_weight, at, (group, cols)), preferred_element_type=jnp.float32)
        for o, at in zip((o_own, swapped_other), corners, strict=True)
    )
    here = here.astype(jnp.bfloat16)
    _, _, _, late = lax.optimization_barrier((here, across_own, across_other, passed))
    here = project(False, cols - narrow, here, across_other, swap(fetched, 1), None)
    here = project(False, cols - narrow, here, across_own, fetched, passed)
    return project(True, cols - narrow, here, across_other, None, swap(late, 1))


def solution(mesh):
    in_specs = (P("ctx", "head"), P("ctx", "head"), P("ctx", "head"), P("ctx"), P("head", None))
    out_specs = P("ctx", "head")
    return jax.shard_map(
        per_device, mesh=mesh, in_specs=in_specs, out_specs=out_specs, check_vma=False
    )
```
